32 devices in a mesh: dp: 8 (over z, core), mp: 4 (over y, x).
Axes of the slice: x: 2, y: 2, z: 4, core: 2. Of those that a mesh axis runs over, the one named last changes fastest.
Arguments:
- images_small: bfloat16 [8, 10, 10, 1024], P('dp', None, None, 'mp'), may hold values from -48 to 48
- images_medium: bfloat16 [48, 12, 12, 1024], P('dp', None, None, 'mp'), may hold values from -48 to 48
- images_large: bfloat16 [32, 14, 14, 1024], P('dp', None, None, 'mp'), may hold values from -48 to 48
- width_choice: int32 [3], replicated, may hold values from 0 to 2, each once
- gates_small: int32 [8], P('dp'), may hold values from 0 to 1, as said below
- gates_medium: int32 [48], P('dp'), may hold values from 0 to 1, as said below
- gates_large: int32 [32], P('dp'), may hold values from 0 to 1, as said below
- cotangent_small: bfloat16 [8, 5, 5, 2048], P('dp', None, None, 'mp'), may hold values from -6 to 6
- cotangent_medium: bfloat16 [48, 6, 6, 2048], P('dp', None, None, 'mp'), may hold values from -6 to 6
- cotangent_large: bfloat16 [32, 7, 7, 2048], P('dp', None, None, 'mp'), may hold values from -6 to 6
- squeeze_one: bfloat16 [512, 1024], P('mp'), may hold values from -0.1875 to 0.1875
- squeeze_gain_one: float32 [512], P('mp'), may hold values from 0.25 to 1.75
- squeeze_offset_one: float32 [512], P('mp'), may hold values from -1.2 to 1.2
- spatial_one: bfloat16 [512, 3, 3, 512], P('mp'), may hold values from -0.09375 to 0.09375
- spatial_gain_one: float32 [512], P('mp'), may hold values from 0.25 to 1.75
- spatial_offset_one: float32 [512], P('mp'), may hold values from -1.2 to 1.2
- expand_one: bfloat16 [512, 2048], P('mp'), may hold values from -0.25 to 0.25
- expand_gain_one: float32 [2048], P('mp'), may hold values from 0.25 to 1.75
- expand_offset_one: float32 [2048], P('mp'), may hold values from -1.2 to 1.2
- shortcut_one: bfloat16 [1024, 2048], P('mp'), may hold values from -0.1875 to 0.1875
- shortcut_gain: float32 [2048], P('mp'), may hold values from 0.25 to 1.75
- shortcut_offset: float32 [2048], P('mp'), may hold values from -1.2 to 1.2
- squeeze_two: bfloat16 [512, 2048], P('mp'), may hold values from -0.125 to 0.125
- squeeze_gain_two: float32 [512], P('mp'), may hold values from 0.25 to 1.75
- squeeze_offset_two: float32 [512], P('mp'), may hold values from -1.2 to 1.2
- spatial_two: bfloat16 [512, 3, 3, 512], P('mp'), may hold values from -0.09375 to 0.09375
- spatial_gain_two: float32 [512], P('mp'), may hold values from 0.25 to 1.75
- spatial_offset_two: float32 [512], P('mp'), may hold values from -1.2 to 1.2
- expand_two: bfloat16 [512, 2048], P('mp'), may hold values from -0.25 to 0.25
- expand_gain_two: float32 [2048], P('mp'), may hold values from 0.25 to 1.75
- expand_offset_two: float32 [2048], P('mp'), may hold values from -1.2 to 1.2
Outputs:
- output_small: float32 [8, 5, 5, 2048], P('dp', None, None, 'mp')
- output_medium: float32 [48, 6, 6, 2048], P('dp', None, None, 'mp')
- output_large: float32 [32, 7, 7, 2048], P('dp', None, None, 'mp')
- input_grad_small: float32 [8, 10, 10, 1024], P('dp', None, None, 'mp')
- input_grad_medium: float32 [48, 12, 12, 1024], P('dp', None, None, 'mp')
- input_grad_large: float32 [32, 14, 14, 1024], P('dp', None, None, 'mp')
- grad_squeeze_one: float32 [512, 1024], P('mp')
- grad_squeeze_gain_one: float32 [512], P('mp')
- grad_squeeze_offset_one: float32 [512], P('mp')
- grad_spatial_one: float32 [512, 3, 3, 512], P('mp')
- grad_spatial_gain_one: float32 [512], P('mp')
- grad_spatial_offset_one: float32 [512], P('mp')
- grad_expand_one: float32 [512, 2048], P('mp')
- grad_expand_gain_one: float32 [2048], P('mp')
- grad_expand_offset_one: float32 [2048], P('mp')
- grad_shortcut_one: float32 [1024, 2048], P('mp')
- grad_shortcut_gain: float32 [2048], P('mp')
- grad_shortcut_offset: float32 [2048], P('mp')
- grad_squeeze_two: float32 [512, 2048], P('mp')
- grad_squeeze_gain_two: float32 [512], P('mp')
- grad_squeeze_offset_two: float32 [512], P('mp')
- grad_spatial_two: float32 [512, 3, 3, 512], P('mp')
- grad_spatial_gain_two: float32 [512], P('mp')
- grad_spatial_offset_two: float32 [512], P('mp')
- grad_expand_two: float32 [512, 2048], P('mp')
- grad_expand_gain_two: float32 [2048], P('mp')
- grad_expand_offset_two: float32 [2048], P('mp')
The draws below stay inside these ranges and needn't reach their ends.
Inputs may be any that keep to these rules, and one draw needn't show every extreme that they name: The three groups take three different widths; group g uses the first 512 * (2 + width_choice[g]) // 4 bottleneck channels. `gates_small`: 1 applies the second block's residual branch to that image; exactly 6 of the images have 1. `gates_medium`: 1 applies the second block's residual branch to that image; exactly 36 of the images have 1. `gates_large`: 1 applies the second block's residual branch to that image; exactly 24 of the images have 1.
All inputs are finite; a program needn't handle non-finite values.
Results may differ from the reference program's by a relative error of at most 0.034.
Values may be sent and summed in bfloat16 or wider, within the bound.
A program may use at most 192 MiB of HBM per device.

```python
import math
import jax
import jax.numpy as jnp
from jax import lax

MID = 512
IN_CH = 1024
OUT_CH = 2048
SIDE_S = 10
SIDE_M = 12
SIDE_L = 14
IMAGES_S = 8
IMAGES_M = 48
IMAGES_L = 32


def field(key, images, edge_size, channels):
    base_key, image_key, channel_key = jax.random.split(key, 3)
    normal_part = jnp.clip(jax.random.normal(base_key, (images, edge_size, edge_size, channels), jnp.float32), -4.0, 4.0)
    position = jnp.arange(images, dtype=jnp.float32) / max(images - 1, 1)
    image_scale = jnp.exp(position * math.log(3.0)) * jax.random.uniform(image_key, (images,), jnp.float32, 0.8, 1.25)
    channel_scale = jnp.exp(jax.random.uniform(channel_key, (channels,), jnp.float32, -1.15, 1.15))
    values = normal_part
    return values * image_scale[:, None, None, None] * channel_scale


def gate_flags(key, images):
    order = jax.random.permutation(key, images)
    return (order < images - images // 4).astype(jnp.int32)


def draw_images_small(key, part):
    key = jax.random.fold_in(key, 11)
    return field(key, IMAGES_S, SIDE_S, IN_CH).astype(jnp.bfloat16)


def draw_images_medium(key, part):
    key = jax.random.fold_in(key, 12)
    return field(key, IMAGES_M, SIDE_M, IN_CH).astype(jnp.bfloat16)


def draw_images_large(key, part):
    key = jax.random.fold_in(key, 13)
    return field(key, IMAGES_L, SIDE_L, IN_CH).astype(jnp.bfloat16)


def draw_gates_small(key, part):
    key = jax.random.fold_in(key, 21)
    return gate_flags(key, IMAGES_S)


def draw_gates_medium(key, part):
    key = jax.random.fold_in(key, 22)
    return gate_flags(key, IMAGES_M)


def draw_gates_large(key, part):
    key = jax.random.fold_in(key, 23)
    return gate_flags(key, IMAGES_L)


def levels(rng, dims, shards, low, largest):
    def one(axis_at, blocks):
        steps = jax.random.uniform(jax.random.fold_in(jax.random.fold_in(rng, 6), axis_at), (blocks,), jnp.float32, low / len(shards), largest / len(shards))
        return jnp.repeat(jnp.exp(steps), dims[axis_at] // blocks).reshape((-1,) + (1,) * (len(dims) - axis_at - 1))

    gain = one(*shards[0])
    for cut in shards[1:]:
        gain = gain * one(*cut)
    return gain


def centred(own_key, extent, width, limit, cuts=(), held_as=jnp.bfloat16):
    result = jax.random.normal(own_key, extent, jnp.float32) * width
    if len(cuts) > 0:
        result = levels(own_key, extent, cuts, -0.22, 0.18) * result
    return jnp.clip(result, min=-limit, max=limit).astype(held_as)


def setup_inputs(seed: int = 0) -> dict:
    arg_keys = jax.random.split(jax.random.key(seed), 32)
    return {
        "images_small": draw_images_small(jax.random.fold_in(arg_keys[31], 71), 0),
        "images_medium": draw_images_medium(jax.random.fold_in(arg_keys[31], 71), 0),
        "images_large": draw_images_large(jax.random.fold_in(arg_keys[31], 71), 0),
        "width_choice": jax.random.permutation(arg_keys[3], 3).astype(jnp.int32),
        "gates_small": draw_gates_small(jax.random.fold_in(arg_keys[31], 71), 0),
        "gates_medium": draw_gates_medium(jax.random.fold_in(arg_keys[31], 71), 0),
        "gates_large": draw_gates_large(jax.random.fold_in(arg_keys[31], 71), 0),
        "cotangent_small": centred(arg_keys[7], (IMAGES_S, SIDE_S // 2, SIDE_S // 2, OUT_CH), 1.0, 6.0, ((0, 8), (3, 4))),
        "cotangent_medium": centred(arg_keys[8], (IMAGES_M, SIDE_M // 2, SIDE_M // 2, OUT_CH), 1.0, 6.0, ((0, 8), (3, 4))),
        "cotangent_large": centred(arg_keys[9], (IMAGES_L, SIDE_L // 2, SIDE_L // 2, OUT_CH), 1.0, 6.0, ((0, 8), (3, 4))),
        "squeeze_one": centred(arg_keys[10], (MID, IN_CH), IN_CH ** -0.5, 0.1875, ((0, 4),)),
        "squeeze_gain_one": jnp.clip(1.0 + 0.15 * jax.random.normal(arg_keys[11], (MID,), jnp.float32), 0.25, 1.75),
        "squeeze_offset_one": centred(arg_keys[12], (MID,), 0.3, 1.2, ((0, 4),), jnp.float32),
        "spatial_one": centred(arg_keys[13], (MID, 3, 3, MID), (9 * MID) ** -0.5, 0.09375, ((0, 4),)),
        "spatial_gain_one": jnp.clip(1.0 + 0.15 * jax.random.normal(arg_keys[14], (MID,), jnp.float32), 0.25, 1.75),
        "spatial_offset_one": centred(arg_keys[15], (MID,), 0.3, 1.2, ((0, 4),), jnp.float32),
        "expand_one": centred(arg_keys[16], (MID, OUT_CH), MID ** -0.5, 0.25, ((0, 4),)),
        "expand_gain_one": jnp.clip(1.0 + 0.15 * jax.random.normal(arg_keys[17], (OUT_CH,), jnp.float32), 0.25, 1.75),
        "expand_offset_one": centred(arg_keys[18], (OUT_CH,), 0.3, 1.2, ((0, 4),), jnp.float32),
        "shortcut_one": centred(arg_keys[19], (IN_CH, OUT_CH), IN_CH ** -0.5, 0.1875, ((0, 4),)),
        "shortcut_gain": jnp.clip(1.0 + 0.15 * jax.random.normal(arg_keys[20], (OUT_CH,), jnp.float32), 0.25, 1.75),
        "shortcut_offset": centred(arg_keys[21], (OUT_CH,), 0.3, 1.2, ((0, 4),), jnp.float32),
        "squeeze_two": centred(arg_keys[22], (MID, OUT_CH), OUT_CH ** -0.5, 0.125, ((0, 4),)),
        "squeeze_gain_two": jnp.clip(1.0 + 0.15 * jax.random.normal(arg_keys[23], (MID,), jnp.float32), 0.25, 1.75),
        "squeeze_offset_two": centred(arg_keys[24], (MID,), 0.3, 1.2, ((0, 4),), jnp.float32),
        "spatial_two": centred(arg_keys[25], (MID, 3, 3, MID), (9 * MID) ** -0.5, 0.09375, ((0, 4),)),
        "spatial_gain_two": jnp.clip(1.0 + 0.15 * jax.random.normal(arg_keys[26], (MID,), jnp.float32), 0.25, 1.75),
        "spatial_offset_two": centred(arg_keys[27], (MID,), 0.3, 1.2, ((0, 4),), jnp.float32),
        "expand_two": centred(arg_keys[28], (MID, OUT_CH), MID ** -0.5, 0.25, ((0, 4),)),
        "expand_gain_two": jnp.clip(1.0 + 0.15 * jax.random.normal(arg_keys[29], (OUT_CH,), jnp.float32), 0.25, 1.75),
        "expand_offset_two": centred(arg_keys[30], (OUT_CH,), 0.3, 1.2, ((0, 4),), jnp.float32),
    }


EPSILON = 1e-05

@jax.custom_vjp
def low(v):
    return lax.optimization_barrier(v.astype(jnp.bfloat16)).astype(jnp.float32)

@jax.custom_vjp
def low_back(v):
    return v

def low_keep(v):
    return (low(v), None)

def low_pass(kept, grad):
    return (grad,)

def back_keep(v):
    return (v, None)

def back_low(kept, grad):
    return (low(grad),)
low.defvjp(low_keep, low_pass)
low_back.defvjp(back_keep, back_low)

def sigmoid_linear(values):
    return values * jax.nn.sigmoid(values)

def pointwise(hidden, weight):
    return jnp.einsum('nhwc,cd->nhwd', hidden, weight, precision=lax.Precision.HIGHEST)

def reduce_pointwise(hidden, weight):
    return jnp.einsum('nhwc,dc->nhwd', hidden, weight, precision=lax.Precision.HIGHEST)

def spatial(hidden, weight, stride):
    kernel = jnp.transpose(weight, (1, 2, 3, 0))
    return lax.conv_general_dilated(hidden, kernel, (stride, stride), ((1, 1), (1, 1)), dimension_numbers=('NHWC', 'HWIO', 'NHWC'), precision=lax.Precision.HIGHEST)

def batch_norm(values, norm_gain, offset):
    centre = lax.optimization_barrier(jnp.mean(values, axis=(0, 1, 2)))
    spread = lax.optimization_barrier(jnp.mean(values * values, axis=(0, 1, 2))) - centre * centre
    return (values - centre) * lax.rsqrt(spread + EPSILON) * norm_gain + offset

def block_one(images, width_mask, params):
    squeeze, squeeze_gain, squeeze_offset, spatial_conv, spatial_gain, spatial_offset, expand, expand_gain, expand_offset, shortcut, shortcut_gain, shortcut_offset = params
    entry = low_back(reduce_pointwise(images, squeeze))
    hidden = low(width_mask * sigmoid_linear(batch_norm(entry, squeeze_gain, squeeze_offset)))
    middle = low_back(spatial(hidden, spatial_conv, 2))
    narrow = low(width_mask * sigmoid_linear(batch_norm(middle, spatial_gain, spatial_offset)))
    widened = low_back(pointwise(narrow, expand))
    bypass = low_back(pointwise(images[:, ::2, ::2, :], shortcut))
    return sigmoid_linear(batch_norm(widened, expand_gain, expand_offset) + batch_norm(bypass, shortcut_gain, shortcut_offset))

def block_two(images, width_mask, depth_gate, params):
    squeeze, squeeze_gain, squeeze_offset, spatial_conv, spatial_gain, spatial_offset, expand, expand_gain, expand_offset = params
    entry = low_back(reduce_pointwise(low(images), squeeze))
    hidden = low(width_mask * sigmoid_linear(batch_norm(entry, squeeze_gain, squeeze_offset)))
    middle = low_back(spatial(hidden, spatial_conv, 1))
    narrow = low(width_mask * sigmoid_linear(batch_norm(middle, spatial_gain, spatial_offset)))
    widened = low_back(pointwise(narrow, expand))
    return sigmoid_linear(images + depth_gate[:, None, None, None] * batch_norm(widened, expand_gain, expand_offset))

def reference(images_small, images_medium, images_large, width_choice, gates_small, gates_medium, gates_large, cotangent_small, cotangent_medium, cotangent_large, squeeze_one, squeeze_gain_one, squeeze_offset_one, spatial_one, spatial_gain_one, spatial_offset_one, expand_one, expand_gain_one, expand_offset_one, shortcut_one, shortcut_gain, shortcut_offset, squeeze_two, squeeze_gain_two, squeeze_offset_two, spatial_two, spatial_gain_two, spatial_offset_two, expand_two, expand_gain_two, expand_offset_two):
    params = tuple((weight.astype(jnp.float32) for weight in (squeeze_one, squeeze_gain_one, squeeze_offset_one, spatial_one, spatial_gain_one, spatial_offset_one, expand_one, expand_gain_one, expand_offset_one, shortcut_one, shortcut_gain, shortcut_offset, squeeze_two, squeeze_gain_two, squeeze_offset_two, spatial_two, spatial_gain_two, spatial_offset_two, expand_two, expand_gain_two, expand_offset_two)))
    inputs = tuple((images.astype(jnp.float32) for images in (images_small, images_medium, images_large)))
    cotangents = tuple((values.astype(jnp.float32) for values in (cotangent_small, cotangent_medium, cotangent_large)))
    channel_index = jnp.arange(MID, dtype=jnp.int32)
    width_masks = [(channel_index < MID * (2 + width_choice[member]) // 4).astype(jnp.float32) for member in range(3)]
    depth_gates = [flags.astype(jnp.float32) for flags in (gates_small, gates_medium, gates_large)]

    def forward(weights, batches):
        results = []
        for member in range(3):
            middle = block_one(batches[member], width_masks[member], weights[:12])
            results.append(block_two(middle, width_masks[member], depth_gates[member], weights[12:]))
        return tuple(results)
    outputs, pullback = jax.vjp(forward, params, inputs)
    weight_grads, input_grads = pullback(cotangents)
    return (outputs[0], outputs[1], outputs[2], input_grads[0], input_grads[1], input_grads[2], weight_grads[0], weight_grads[1], weight_grads[2], weight_grads[3], weight_grads[4], weight_grads[5], weight_grads[6], weight_grads[7], weight_grads[8], weight_grads[9], weight_grads[10], weight_grads[11], weight_grads[12], weight_grads[13], weight_grads[14], weight_grads[15], weight_grads[16], weight_grads[17], weight_grads[18], weight_grads[19], weight_grads[20])
```

```python
import functools
import types

import jax
import jax.numpy as jnp
import numpy as np
from jax import lax
from jax.experimental import pallas as pl
from jax.experimental.pallas import tpu as pltpu
from jax.sharding import PartitionSpec as P

EPSILON = 1e-05


def sigmoid_linear(values):
    return values * jax.nn.sigmoid(values)


def sigmoid_slope(values):
    logistic = jax.nn.sigmoid(values)
    return logistic * (1.0 + values * (1.0 - logistic))


def pointwise(hidden, weight):
    return jnp.einsum("nhwc,cd->nhwd", hidden, weight, preferred_element_type=jnp.float32)


def back_pointwise(gradients, weight):
    return jnp.einsum("nhwd,cd->nhwc", gradients, weight, preferred_element_type=jnp.float32)


def weight_term(activations, gradients):
    return jnp.einsum("nhwc,nhwd->cd", activations, gradients, preferred_element_type=jnp.float32)


def reduce_pointwise(hidden, weight):
    return jnp.einsum("nhwc,dc->nhwd", hidden, weight, preferred_element_type=jnp.float32)


def reduce_back(gradients, weight):
    return jnp.einsum("nhwd,dc->nhwc", gradients, weight, preferred_element_type=jnp.float32)


def reduce_term(gradients, activations):
    return jnp.einsum("nhwd,nhwc->dc", gradients, activations, preferred_element_type=jnp.float32)


def gather_taps(hidden, stride):
    extent = hidden.shape[1] // stride
    span_end = stride * (extent - 1) + 1
    padded = jnp.pad(hidden, ((0, 0), (1, 1), (1, 1), (0, 0)))
    pieces = [
        padded[:, vertical : vertical + span_end : stride, lateral : lateral + span_end : stride, :]
        for vertical in range(3)
        for lateral in range(3)
    ]
    return jnp.concatenate(pieces, axis=3)


def spread_taps(columns, stride, edge_size, channels):
    extent = columns.shape[1]
    span_end = stride * (extent - 1) + 1
    padded = jnp.zeros((columns.shape[0], edge_size + 2, edge_size + 2, channels), jnp.float32)
    for position in range(9):
        vertical = position // 3
        lateral = position % 3
        padded = padded.at[
            :, vertical : vertical + span_end : stride, lateral : lateral + span_end : stride, :
        ].add(columns[..., position * channels : (position + 1) * channels])
    return padded[:, 1:-1, 1:-1, :]


def stat_terms(values):
    return jnp.stack([jnp.sum(values, axis=(0, 1, 2)), jnp.sum(values * values, axis=(0, 1, 2))])


def grad_terms(gradients, normed):
    return jnp.stack(
        [jnp.sum(gradients, axis=(0, 1, 2)), jnp.sum(gradients * normed, axis=(0, 1, 2))]
    )


def samples_of(values):
    return values.shape[0] * values.shape[1] * values.shape[2] * lax.axis_size("dp")


def norm_apply(values, totals, samples, norm_gain, offset):
    centre = totals[0] / samples
    spread = totals[1] / samples - centre * centre
    factor = lax.rsqrt(spread + EPSILON)
    normed = (values - centre) * factor
    return (normed, factor, normed * norm_gain + offset)


def norm_back(gradients, normed, factor, totals, samples, norm_gain):
    return norm_gain * factor * (gradients - totals[0] / samples - normed * (totals[1] / samples))


def forward_totals(partials):
    return lax.psum(jnp.stack(partials), "dp")


def backward_totals(partials):
    return lax.psum(jnp.stack(partials), "dp")


def gather_channels(pieces):
    return (
        lax.all_gather(pieces[0], "mp", axis=3, tiled=True),
        lax.all_gather(pieces[1], "mp", axis=3, tiled=True),
        lax.all_gather(pieces[2], "mp", axis=3, tiled=True),
    )


def gather_hidden(pieces):
    return (
        lax.all_gather(pieces[0], "mp", axis=3, tiled=True),
        lax.all_gather(pieces[1], "mp", axis=3, tiled=True),
        lax.all_gather(pieces[2], "mp", axis=3, tiled=True),
    )


def gather_spatial_grads(pieces):
    return (
        lax.all_gather(pieces[0], "mp", axis=3, tiled=True),
        lax.all_gather(pieces[1], "mp", axis=3, tiled=True),
        lax.all_gather(pieces[2], "mp", axis=3, tiled=True),
    )


def gather_entry_grads(pieces):
    return (
        lax.all_gather(pieces[0], "mp", axis=3, tiled=True),
        lax.all_gather(pieces[1], "mp", axis=3, tiled=True),
        lax.all_gather(pieces[2], "mp", axis=3, tiled=True),
    )


def front_forward(gathered, stride, params, width_masks):
    squeeze, squeeze_gain, squeeze_offset, spatial_conv, spatial_gain, spatial_offset = params
    entry = [reduce_pointwise(values, squeeze) for values in gathered]
    entry_totals = forward_totals([stat_terms(values) for values in entry])
    entry_norm = [
        norm_apply(
            entry[member],
            entry_totals[member],
            samples_of(entry[member]),
            squeeze_gain,
            squeeze_offset,
        )
        for member in range(3)
    ]
    hidden = [
        (width_masks[member] * sigmoid_linear(entry_norm[member][2])).astype(jnp.bfloat16)
        for member in range(3)
    ]
    hidden_full = gather_hidden(hidden)
    taps = [gather_taps(values, stride) for values in hidden_full]
    spatial_rows = spatial_conv.reshape(spatial_conv.shape[0], -1)
    middle = [reduce_pointwise(values, spatial_rows) for values in taps]
    middle_totals = forward_totals([stat_terms(values) for values in middle])
    middle_norm = [
        norm_apply(
            middle[member],
            middle_totals[member],
            samples_of(middle[member]),
            spatial_gain,
            spatial_offset,
        )
        for member in range(3)
    ]
    narrow = [
        (width_masks[member] * sigmoid_linear(middle_norm[member][2])).astype(jnp.bfloat16)
        for member in range(3)
    ]
    return (entry_norm, taps, middle_norm, narrow)


def front_backward(narrow_grads, saved, gathered, stride, params, width_masks, column_weights):
    squeeze, squeeze_gain, squeeze_offset, spatial_conv, spatial_gain, spatial_offset = params
    entry_norm, taps, middle_norm, narrow = saved
    middle_out = [
        narrow_grads[member] * width_masks[member] * sigmoid_slope(middle_norm[member][2])
        for member in range(3)
    ]
    middle_totals = backward_totals(
        [grad_terms(middle_out[member], middle_norm[member][0]) for member in range(3)]
    )
    middle_grads = [
        norm_back(
            middle_out[member],
            middle_norm[member][0],
            middle_norm[member][1],
            middle_totals[member],
            samples_of(middle_out[member]),
            spatial_gain,
        ).astype(jnp.bfloat16)
        for member in range(3)
    ]
    spatial_grad = sum(
        (reduce_term(middle_grads[member], taps[member]) for member in range(3))
    ).reshape(spatial_conv.shape)
    squeeze_cols, spatial_cols = column_weights
    channels = spatial_cols.shape[3]
    spatial_flat = spatial_cols.reshape(spatial_cols.shape[0], -1)
    middle_full = gather_spatial_grads(middle_grads)
    hidden_grads = [
        spread_taps(
            reduce_back(middle_full[member], spatial_flat),
            stride,
            gathered[member].shape[1],
            channels,
        )
        for member in range(3)
    ]
    entry_out = [
        hidden_grads[member] * width_masks[member] * sigmoid_slope(entry_norm[member][2])
        for member in range(3)
    ]
    entry_totals = backward_totals(
        [grad_terms(entry_out[member], entry_norm[member][0]) for member in range(3)]
    )
    entry_grads = [
        norm_back(
            entry_out[member],
            entry_norm[member][0],
            entry_norm[member][1],
            entry_totals[member],
            samples_of(entry_out[member]),
            squeeze_gain,
        ).astype(jnp.bfloat16)
        for member in range(3)
    ]
    squeeze_grad = sum((reduce_term(entry_grads[member], gathered[member]) for member in range(3)))
    entry_full = gather_entry_grads(entry_grads)
    squeeze_flat = squeeze_cols.reshape(squeeze_cols.shape[0], -1)
    input_part = [reduce_back(entry_full[member], squeeze_flat) for member in range(3)]
    gain_grads = (
        jnp.sum(entry_totals[:, 1], axis=0),
        jnp.sum(entry_totals[:, 0], axis=0),
        jnp.sum(middle_totals[:, 1], axis=0),
        jnp.sum(middle_totals[:, 0], axis=0),
    )
    return (input_part, squeeze_grad, spatial_grad, gain_grads)


def tail_forward(narrow, bypass_inputs, expand, shortcut):
    partials = []
    for member in range(3):
        pieces = [pointwise(narrow[member], expand)]
        if shortcut is not None:
            pieces.append(pointwise(bypass_inputs[member], shortcut))
        partials.append(jnp.stack(pieces))
    partials = (
        lax.psum_scatter(
            partials[0].astype(jnp.bfloat16), "mp", scatter_dimension=4, tiled=True
        ).astype(jnp.float32),
        lax.psum_scatter(
            partials[1].astype(jnp.bfloat16), "mp", scatter_dimension=4, tiled=True
        ).astype(jnp.float32),
        lax.psum_scatter(
            partials[2].astype(jnp.bfloat16), "mp", scatter_dimension=4, tiled=True
        ).astype(jnp.float32),
    )
    return (partials, narrow)


def tail_backward(gradients, sources, bypass_inputs, expand, shortcut):
    arriving = (
        lax.all_gather(gradients[0], "mp", axis=4, tiled=True),
        lax.all_gather(gradients[1], "mp", axis=4, tiled=True),
        lax.all_gather(gradients[2], "mp", axis=4, tiled=True),
    )
    expand_grad = sum((weight_term(sources[member], arriving[member][0]) for member in range(3)))
    narrow_terms = [back_pointwise(arriving[member][0], expand) for member in range(3)]
    if shortcut is None:
        return (narrow_terms, expand_grad, None, None)
    shortcut_grad = sum(
        (weight_term(bypass_inputs[member], arriving[member][1]) for member in range(3))
    )
    bypass_terms = [back_pointwise(arriving[member][1], shortcut) for member in range(3)]
    return (narrow_terms, expand_grad, shortcut_grad, bypass_terms)


def on_device(
    images_small,
    images_medium,
    images_large,
    width_choice,
    gates_small,
    gates_medium,
    gates_large,
    cotangent_small,
    cotangent_medium,
    cotangent_large,
    squeeze_one,
    squeeze_gain_one,
    squeeze_offset_one,
    spatial_one,
    spatial_gain_one,
    spatial_offset_one,
    expand_one,
    expand_gain_one,
    expand_offset_one,
    shortcut_one,
    shortcut_gain,
    shortcut_offset,
    squeeze_two,
    squeeze_gain_two,
    squeeze_offset_two,
    spatial_two,
    spatial_gain_two,
    spatial_offset_two,
    expand_two,
    expand_gain_two,
    expand_offset_two,
):
    images = [images_small, images_medium, images_large]
    depth_gates = [
        flags.astype(jnp.float32)[:, None, None, None]
        for flags in (gates_small, gates_medium, gates_large)
    ]
    cotangents = [
        values.astype(jnp.float32)
        for values in (cotangent_small, cotangent_medium, cotangent_large)
    ]
    mid_local = squeeze_one.shape[0]
    channel_index = lax.axis_index("mp") * mid_local + jnp.arange(mid_local, dtype=jnp.int32)
    limits = mid_local * lax.axis_size("mp") * (2 + width_choice) // 4
    width_masks = [(channel_index < limits[member]).astype(jnp.float32) for member in range(3)]
    out_local = expand_gain_one.shape[0]
    params_one = (
        squeeze_one,
        squeeze_gain_one,
        squeeze_offset_one,
        spatial_one,
        spatial_gain_one,
        spatial_offset_one,
    )
    params_two = (
        squeeze_two,
        squeeze_gain_two,
        squeeze_offset_two,
        spatial_two,
        spatial_gain_two,
        spatial_offset_two,
    )
    expand_first, bypass_weight, expand_second = (expand_one, shortcut_one, expand_two)
    squeeze_cols_one, spatial_cols_one, squeeze_cols_two, spatial_cols_two = (
        lax.all_to_all(
            squeeze_one.reshape(mid_local, 1, 1, -1), "mp", split_axis=3, concat_axis=0, tiled=True
        ),
        lax.all_to_all(spatial_one, "mp", split_axis=3, concat_axis=0, tiled=True),
        lax.all_to_all(
            squeeze_two.reshape(mid_local, 1, 1, -1), "mp", split_axis=3, concat_axis=0, tiled=True
        ),
        lax.all_to_all(spatial_two, "mp", split_axis=3, concat_axis=0, tiled=True),
    )
    columns_one = (squeeze_cols_one, spatial_cols_one)
    columns_two = (squeeze_cols_two, spatial_cols_two)
    first_full = gather_channels(images)
    first_saved = front_forward(first_full, 2, params_one, width_masks)
    bypass_inputs = [values[:, ::2, ::2, :] for values in images]
    first_tail, first_sources = tail_forward(
        first_saved[3], bypass_inputs, expand_first, bypass_weight
    )
    first_totals = forward_totals(
        [
            jnp.concatenate(
                [stat_terms(first_tail[member][0]), stat_terms(first_tail[member][1])], axis=1
            )
            for member in range(3)
        ]
    )
    widened_norm = [
        norm_apply(
            first_tail[member][0],
            first_totals[member][:, :out_local],
            samples_of(first_tail[member][0]),
            expand_gain_one,
            expand_offset_one,
        )
        for member in range(3)
    ]
    bypass_norm = [
        norm_apply(
            first_tail[member][1],
            first_totals[member][:, out_local:],
            samples_of(first_tail[member][1]),
            shortcut_gain,
            shortcut_offset,
        )
        for member in range(3)
    ]
    first_sum = [widened_norm[member][2] + bypass_norm[member][2] for member in range(3)]
    block_out = [sigmoid_linear(values) for values in first_sum]
    second_full = gather_channels([values.astype(jnp.bfloat16) for values in block_out])
    second_saved = front_forward(second_full, 1, params_two, width_masks)
    second_tail, second_sources = tail_forward(second_saved[3], None, expand_second, None)
    second_totals = forward_totals([stat_terms(second_tail[member][0]) for member in range(3)])
    final_norm = [
        norm_apply(
            second_tail[member][0],
            second_totals[member],
            samples_of(second_tail[member][0]),
            expand_gain_two,
            expand_offset_two,
        )
        for member in range(3)
    ]
    second_sum = [
        block_out[member] + depth_gates[member] * final_norm[member][2] for member in range(3)
    ]
    results = [sigmoid_linear(values) for values in second_sum]
    second_slope = [sigmoid_slope(second_sum[member]) * cotangents[member] for member in range(3)]
    final_out = [depth_gates[member] * second_slope[member] for member in range(3)]
    final_totals = backward_totals(
        [grad_terms(final_out[member], final_norm[member][0]) for member in range(3)]
    )
    final_grads = [
        norm_back(
            final_out[member],
            final_norm[member][0],
            final_norm[member][1],
            final_totals[member],
            samples_of(final_out[member]),
            expand_gain_two,
        ).astype(jnp.bfloat16)[None]
        for member in range(3)
    ]
    second_result = tail_backward(final_grads, second_sources, None, expand_second, None)
    second_input_part, squeeze_two_grad, spatial_two_grad, second_gain_grads = front_backward(
        second_result[0], second_saved, second_full, 1, params_two, width_masks, columns_two
    )
    expand_two_grad = second_result[1]
    block_grads = [second_slope[member] + second_input_part[member] for member in range(3)]
    first_slope = [sigmoid_slope(first_sum[member]) * block_grads[member] for member in range(3)]
    first_grad_totals = backward_totals(
        [
            jnp.concatenate(
                [
                    grad_terms(first_slope[member], widened_norm[member][0]),
                    grad_terms(first_slope[member], bypass_norm[member][0]),
                ],
                axis=1,
            )
            for member in range(3)
        ]
    )
    tail_grads = [
        jnp.stack(
            [
                norm_back(
                    first_slope[member],
                    widened_norm[member][0],
                    widened_norm[member][1],
                    first_grad_totals[member][:, :out_local],
                    samples_of(first_slope[member]),
                    expand_gain_one,
                ),
                norm_back(
                    first_slope[member],
                    bypass_norm[member][0],
                    bypass_norm[member][1],
                    first_grad_totals[member][:, out_local:],
                    samples_of(first_slope[member]),
                    shortcut_gain,
                ),
            ]
        ).astype(jnp.bfloat16)
        for member in range(3)
    ]
    first_result = tail_backward(
        tail_grads, first_sources, bypass_inputs, expand_first, bypass_weight
    )
    expand_one_grad = first_result[1]
    shortcut_grad = first_result[2]
    bypass_terms = first_result[3]
    first_input_part, squeeze_one_grad, spatial_one_grad, first_gain_grads = front_backward(
        first_result[0], first_saved, first_full, 2, params_one, width_masks, columns_one
    )
    input_grads = [
        first_input_part[member].at[:, ::2, ::2, :].add(bypass_terms[member]) for member in range(3)
    ]
    summed = (
        lax.psum(squeeze_one_grad.astype(jnp.bfloat16), "dp").astype(jnp.float32),
        lax.psum(spatial_one_grad.astype(jnp.bfloat16), "dp").astype(jnp.float32),
        lax.psum(expand_one_grad.astype(jnp.bfloat16), "dp").astype(jnp.float32),
        lax.psum(shortcut_grad.astype(jnp.bfloat16), "dp").astype(jnp.float32),
        lax.psum(squeeze_two_grad.astype(jnp.bfloat16), "dp").astype(jnp.float32),
        lax.psum(spatial_two_grad.astype(jnp.bfloat16), "dp").astype(jnp.float32),
        lax.psum(expand_two_grad.astype(jnp.bfloat16), "dp").astype(jnp.float32),
    )
    expand_gain_one_grad = jnp.sum(first_grad_totals[:, 1, :out_local], axis=0)
    expand_offset_one_grad = jnp.sum(first_grad_totals[:, 0, :out_local], axis=0)
    shortcut_gain_grad = jnp.sum(first_grad_totals[:, 1, out_local:], axis=0)
    shortcut_offset_grad = jnp.sum(first_grad_totals[:, 0, out_local:], axis=0)
    expand_gain_two_grad = jnp.sum(final_totals[:, 1], axis=0)
    expand_offset_two_grad = jnp.sum(final_totals[:, 0], axis=0)
    return (
        results[0],
        results[1],
        results[2],
        input_grads[0],
        input_grads[1],
        input_grads[2],
        summed[0],
        first_gain_grads[0],
        first_gain_grads[1],
        summed[1],
        first_gain_grads[2],
        first_gain_grads[3],
        summed[2],
        expand_gain_one_grad,
        expand_offset_one_grad,
        summed[3],
        shortcut_gain_grad,
        shortcut_offset_grad,
        summed[4],
        second_gain_grads[0],
        second_gain_grads[1],
        summed[5],
        second_gain_grads[2],
        second_gain_grads[3],
        summed[6],
        expand_gain_two_grad,
        expand_offset_two_grad,
    )


LANE = 128
GUARD = 32
MESH_ID = pl.DeviceIdType.MESH
DMA = pltpu.SemaphoreType.DMA
VMEM = pltpu.VMEM
F32 = jnp.float32
BF16 = jnp.bfloat16
WEIGHTS = 7
TENSOR_Q1, TENSOR_S1, TENSOR_E1, TENSOR_SC, TENSOR_Q2, TENSOR_S2, TENSOR_E2 = range(WEIGHTS)
NORM_Q1, NORM_S1, NORM_Q2, NORM_S2 = range(4)
NORM_E1, NORM_SC, NORM_E2 = range(3)


def nn(left, right):
    return lax.dot_general(left, right, (((1,), (0,)), ((), ())), preferred_element_type=F32)


def nt(left, right):
    return lax.dot_general(left, right, (((1,), (1,)), ((), ())), preferred_element_type=F32)


def tn(left, right):
    return lax.dot_general(left, right, (((0,), (0,)), ((), ())), preferred_element_type=F32)


def bag(tree):
    if isinstance(tree, dict):
        return types.SimpleNamespace(**{name: bag(value) for name, value in tree.items()})
    return tree


class Segment:
    def __init__(self, group, start, images, side, replicas):
        self.group = group
        self.side = side
        self.images = images
        self.inside = images <= 4
        self.right = images if self.inside else 1
        self.down = self.right * side
        self.start = start
        self.real = images * side * side
        self.size = -(-self.real // 16) * 16
        self.stop = start + self.size
        self.count = float(self.real * replicas)

    def pixel_first(self, values):
        return values.transpose(1, 2, 0, 3) if self.inside else values

    def image_first(self, values):
        return values.transpose(2, 0, 1, 3) if self.inside else values


class Chain:
    def __init__(self, groups, shapes, replicas):
        self.segments = []
        start = 0
        for group in groups:
            images, side = shapes[group]
            segment = Segment(group, start, images, side // 2, replicas)
            self.segments.append(segment)
            start = segment.stop
        self.rows = start
        self.padded = start + 2 * GUARD


class Weight:
    def __init__(self, block, width, taps, direct):
        self.block = block
        self.width = width
        self.taps = taps
        self.direct = direct
        self.ways = 4 if direct else 2
        self.piece = block // (2 * self.ways)


def weight_table(mid, wide, inner):
    return [
        Weight(mid, inner, 1, True),
        Weight(mid, mid, 9, True),
        Weight(mid, wide, 1, False),
        Weight(inner, wide, 1, True),
        Weight(mid, wide, 1, False),
        Weight(mid, mid, 9, True),
        Weight(mid, wide, 1, False),
    ]


def chain_scratch(chain, mid, wide, inner, dpn, mpn):
    rows = chain.rows
    padded = chain.padded
    near = mpn - 1

    def summed(lead, width):
        return dict(
            send=VMEM((mpn, lead, width), BF16),
            recv=VMEM((near, lead, width), BF16),
            sent=DMA((near,)),
            came=DMA((near,)),
        )

    def gathered(lead, width):
        return dict(full=VMEM((mpn, lead, width), BF16), sent=DMA((near,)), came=DMA((near,)))

    def reduced(terms, width):
        depth = -(-(len(chain.segments) * terms * width // LANE) // 8) * 8
        return dict(
            stat=VMEM((dpn, depth, LANE), F32), sent=DMA((dpn - 1,)), came=DMA((dpn,))
        )

    return dict(
        z1=summed(4 * rows, mid),
        z2=summed(rows, mid),
        u1=summed(rows, mid),
        u2=summed(rows, mid),
        b2=summed(rows, mid),
        b1=summed(rows, mid),
        bx=summed(rows, inner),
        xs=gathered(rows, inner),
        h2=gathered(rows, mid),
        v2=gathered(rows, mid),
        g2=gathered(rows, mid),
        g1=gathered(rows, mid),
        k2=gathered(rows, mid),
        k1=gathered(4 * rows, mid),
        f1=reduced(2, mid),
        f2=reduced(2, mid),
        f3=reduced(2, wide),
        fp=reduced(2, wide),
        f4=reduced(2, mid),
        f5=reduced(2, mid),
        f6=reduced(2, wide),
        r6=reduced(2, wide),
        r5=reduced(2, mid),
        r4=reduced(2, mid),
        r3=reduced(3, wide),
        r2=reduced(2, mid),
        r1=reduced(2, mid),
        n1=VMEM((4, rows, mid), F32),
        sl1=VMEM((4, rows, mid), F32),
        h1=VMEM((4, padded, mid), F32),
        t1=VMEM((rows, 9 * mid), BF16),
        n2=VMEM((rows, mid), F32),
        sl2=VMEM((rows, mid), F32),
        n3=VMEM((rows, wide), F32),
        bypass=VMEM((rows, wide), F32),
        y=VMEM((rows, wide), F32),
        slq=VMEM((rows, wide), F32),
        r=VMEM((rows, wide), BF16),
        n4=VMEM((rows, mid), F32),
        sl4=VMEM((rows, mid), F32),
        v1=VMEM((padded, mid), F32),
        t2=VMEM((rows, 9 * mid), BF16),
        n5=VMEM((rows, mid), F32),
        sl5=VMEM((rows, mid), F32),
        n6=VMEM((rows, wide), F32),
        d2=VMEM((rows, wide), F32),
        du3=VMEM((rows, wide), BF16),
        dz3=VMEM((rows, wide), BF16),
        dzp=VMEM((rows, wide), BF16),
        dt=VMEM((padded, 9 * mid), F32),
        d=VMEM((4, rows, mid), F32),
        back=VMEM((rows, inner), F32),
        gate=VMEM((rows, LANE), F32),
        facm=VMEM((4, 8, mid), F32),
        facw=VMEM((3, 8, wide), F32),
        gm=VMEM((8, mid), F32),
        gw=VMEM((8, wide), F32),
    )


def weight_scratch(weight, dpn, mpn):
    near = mpn - 1
    spread = (mpn, weight.taps, weight.block // 2, weight.width)
    pieces = (weight.ways, mpn, weight.taps, weight.piece, weight.width)
    return dict(
        full=VMEM((weight.taps, mpn * weight.block, weight.width), BF16),
        sent=DMA((near,)),
        came=DMA((near,)),
        passed=DMA((near,)),
        given=DMA((near,)),
        own=DMA((1,)),
        part=VMEM((mpn, weight.taps, weight.block, weight.width), BF16),
        twin=VMEM(spread, BF16),
        sums=VMEM(pieces, BF16),
        hop=VMEM(pieces, BF16),
        fin=VMEM(pieces, BF16),
        swap=VMEM(pieces, BF16),
        twins=DMA((2,)),
        swaps=DMA((2,)),
        outs=DMA((2,)),
        hop_sent=DMA((4,)),
        hop_came=DMA((4,)),
        mix_sent=DMA((near,)),
        mix_came=DMA((near,)),
        cast_sent=DMA((4,)),
        cast_came=DMA((4,)),
    )


class Body:
    def __init__(self, given, made, scratch, chains, weights, sizes):
        self.given = given
        self.made = made
        self.links = scratch.chains
        self.weights = weights
        self.held = scratch.weights
        self.chains = chains
        self.mid, self.wide, self.inner, self.dpn, self.mpn = sizes
        self.dp = lax.axis_index("dp")
        self.mp = lax.axis_index("mp")
        self.z = lax.div(self.dp, 2)
        self.core = lax.rem(self.dp, 2)
        self.levels = self.dpn // 2
        across = lax.div(self.mp, 2)
        along = lax.rem(self.mp, 2)
        self.peers = (
            across * 2 + (1 - along),
            (1 - across) * 2 + along,
            (1 - across) * 2 + (1 - along),
        )
        self.twin = self.z * 2 + (1 - self.core)
        self.others = [lax.rem(self.dp + step, self.dpn) for step in range(1, self.dpn)]
        self.stack = [lax.rem(self.z + step, self.levels) for step in range(1, self.levels)]
        self.flying = {}
        self.passing = {}
        self.present = set()

    def barrier(self):
        semaphore = pltpu.get_barrier_semaphore()
        for peer in self.peers:
            pl.semaphore_signal(
                semaphore, inc=1, device_id=(self.dp, peer), device_id_type=MESH_ID
            )
        for other in self.others:
            pl.semaphore_signal(
                semaphore, inc=1, device_id=(other, self.mp), device_id_type=MESH_ID
            )
        pl.semaphore_wait(semaphore, len(self.peers) + len(self.others))

    def remote(self, source, target, sent, came, device):
        return pltpu.make_async_remote_copy(
            src_ref=source,
            dst_ref=target,
            send_sem=sent,
            recv_sem=came,
            device_id=device,
            device_id_type=MESH_ID,
        )


    def scatter(self, link, values):
        width = link.send.shape[2]
        for block in range(self.mpn):
            link.send[block] = values[:, block * width : (block + 1) * width].astype(BF16)
        copies = []
        for step, peer in enumerate(self.peers):
            copy = self.remote(
                link.send.at[peer],
                link.recv.at[step],
                link.sent.at[step],
                link.came.at[step],
                (self.dp, peer),
            )
            copy.start()
            copies.append(copy)
        yield
        for copy in copies:
            copy.wait()
        total = link.send[self.mp].astype(F32)
        for step in range(self.mpn - 1):
            total = total + link.recv[step].astype(F32)
        return total

    def gather(self, link):
        full = link.full
        copies = []
        for step, peer in enumerate(self.peers):
            copy = self.remote(
                full.at[self.mp],
                full.at[self.mp],
                link.sent.at[step],
                link.came.at[step],
                (self.dp, peer),
            )
            copy.start()
            copies.append(copy)
        yield
        for step, peer in enumerate(self.peers):
            copies[step].wait_send()
            self.remote(
                full.at[peer],
                full.at[peer],
                link.sent.at[step],
                link.came.at[step],
                (self.dp, peer),
            ).wait_recv()

    def joined(self, link):
        return jnp.concatenate([link.full[block] for block in range(self.mpn)], axis=1)

    def reduce(self, link, terms):
        stat = link.stat
        depth = stat.shape[1]
        lanes = terms[0].shape[1] // LANE
        lines = [
            term[:, lane * LANE : (lane + 1) * LANE] for term in terms for lane in range(lanes)
        ]
        if depth > len(lines):
            lines.append(jnp.zeros((depth - len(lines), LANE), F32))
        stat[self.dp] = jnp.concatenate(lines, axis=0)
        copies = []
        for step, other in enumerate(self.others):
            copy = self.remote(
                stat.at[self.dp],
                stat.at[self.dp],
                link.sent.at[step],
                link.came.at[self.dp],
                (other, self.mp),
            )
            copy.start()
            copies.append(copy)
        yield
        for step, other in enumerate(self.others):
            copies[step].wait_send()
            self.remote(
                stat.at[other],
                stat.at[other],
                link.sent.at[step],
                link.came.at[other],
                (other, self.mp),
            ).wait_recv()
        total = stat[0]
        for source in range(1, self.dpn):
            total = total + stat[source]
        rows = []
        for index in range(len(terms)):
            first = index * lanes
            pieces = [total[first + lane : first + lane + 1] for lane in range(lanes)]
            rows.append(pieces[0] if lanes == 1 else jnp.concatenate(pieces, axis=1))
        return rows


    def half(self, block, first, core):
        return pl.ds(pl.multiple_of(first + core * (block // 2), 16), block // 2)

    def weight_start(self, tensor):
        weight = self.weights[tensor]
        held = self.held[tensor]
        source = self.given.weights[tensor]
        block, width = weight.block, weight.width

        def columns(device):
            return pl.ds(pl.multiple_of(device * width, LANE), width)

        copies = []
        for step, peer in enumerate(self.peers):
            copy = self.remote(
                source.at[:, self.half(block, 0, self.core), columns(peer)],
                held.full.at[:, self.half(block, self.mp * block, self.core), :],
                held.sent.at[step],
                held.came.at[step],
                (self.dp, peer),
            )
            copy.start()
            copies.append(copy)
        own = pltpu.make_async_copy(
            source.at[:, :, columns(self.mp)],
            held.full.at[:, pl.ds(pl.multiple_of(self.mp * block, 16), block), :],
            held.own.at[0],
        )
        own.start()
        self.flying[tensor] = (copies, own)

    def weight_pass(self, tensor):
        if tensor in self.passing:
            return
        copies, own = self.flying[tensor]
        block = self.weights[tensor].block
        held = self.held[tensor]
        passed = []
        for step, peer in enumerate(self.peers):
            came = held.full.at[:, self.half(block, peer * block, self.core), :]
            copies[step].wait_send()
            self.remote(
                came, came, held.sent.at[step], held.came.at[step], (self.dp, peer)
            ).wait_recv()
            copy = self.remote(
                came, came, held.passed.at[step], held.given.at[step], (self.twin, self.mp)
            )
            copy.start()
            passed.append(copy)
        own.wait()
        self.passing[tensor] = passed

    def weight(self, tensor):
        held = self.held[tensor]
        weight = self.weights[tensor]
        block = weight.block
        if tensor not in self.present:
            self.weight_pass(tensor)
            for step, peer in enumerate(self.peers):
                rest = held.full.at[:, self.half(block, peer * block, 1 - self.core), :]
                self.passing[tensor][step].wait_send()
                self.remote(
                    rest, rest, held.passed.at[step], held.given.at[step], (self.twin, self.mp)
                ).wait_recv()
            self.present.add(tensor)
        if weight.taps == 1:
            return held.full[0]
        return jnp.concatenate([held.full[tap] for tap in range(weight.taps)], axis=1)


    def keep(self, segment, values):
        if segment.real == segment.size:
            return values
        rows = lax.broadcasted_iota(jnp.int32, values.shape, values.ndim - 2)
        return jnp.where(rows < segment.real, values, 0.0)

    def factors(self, sums, squares, count):
        centre = sums / count
        spread = squares / count - centre * centre
        return centre, lax.rsqrt(spread + EPSILON)

    def sum_rows(self, values):
        return jnp.sum(values.reshape(-1, values.shape[-1]), axis=0, keepdims=True)

    def moments(self, chain, values):
        terms = []
        for segment in chain.segments:
            part = values[..., segment.start : segment.stop, :]
            terms.append(self.sum_rows(part))
            terms.append(self.sum_rows(part * part))
        return terms

    def mid_row(self, norm, what):
        return self.given.mids[norm * 2 + what][...].reshape(1, self.mid)

    def wide_row(self, norm, what):
        return self.given.wides[norm * 2 + what][...].reshape(1, self.wide)

    def width_mask(self, group):
        limit = lax.div(self.mid * self.mpn * (2 + self.given.widths[group]), 4)
        index = lax.broadcasted_iota(jnp.int32, (1, self.mid), 1) + self.mp * self.mid
        return (index < limit).astype(F32)

    def narrow_norm(self, chain, link, norm, values, totals, normed_ref, slope_ref, store):
        gain = self.mid_row(norm, 0)
        offset = self.mid_row(norm, 1)
        for index, segment in enumerate(chain.segments):
            rows = slice(segment.start, segment.stop)
            count = segment.count * (4 if norm == NORM_Q1 else 1)
            centre, factor = self.factors(totals[2 * index], totals[2 * index + 1], count)
            link.facm[norm, index : index + 1, :] = factor
            mask = self.width_mask(segment.group)
            normed = (values[..., rows, :] - centre) * factor
            normed_ref[..., rows, :] = normed
            affine = normed * gain + offset
            logistic = jax.nn.sigmoid(affine)
            slope_ref[..., rows, :] = mask * (logistic * (1.0 + affine * (1.0 - logistic)))
            store(segment, self.keep(segment, mask * (affine * logistic)).astype(BF16))

    def narrow_terms(self, chain, gradients, normed_ref):
        terms = []
        for segment in chain.segments:
            rows = slice(segment.start, segment.stop)
            part = gradients[..., rows, :]
            terms.append(self.sum_rows(part))
            terms.append(self.sum_rows(part * normed_ref[..., rows, :]))
        return terms

    def narrow_back(self, chain, link, norm, gradients_ref, totals, normed_ref, store):
        gain = self.mid_row(norm, 0)
        gain_total = None
        offset_total = None
        for index, segment in enumerate(chain.segments):
            rows = slice(segment.start, segment.stop)
            count = segment.count * (4 if norm == NORM_Q1 else 1)
            factor = link.facm[norm, index : index + 1, :]
            first, second = totals[2 * index], totals[2 * index + 1]
            gain_total = second if gain_total is None else gain_total + second
            offset_total = first if offset_total is None else offset_total + first
            change = (gain * factor) * (
                gradients_ref[..., rows, :]
                - first / count
                - normed_ref[..., rows, :] * (second / count)
            )
            store(segment, self.keep(segment, change).astype(BF16))
        link.gm[2 * norm : 2 * norm + 1, :] = gain_total
        link.gm[2 * norm + 1 : 2 * norm + 2, :] = offset_total


    def edge(self, edges, start, size, down, right):
        mask = None
        for shift, first in ((down, 0), (right, 2)):
            if shift == 0:
                continue
            values = edges[first + (0 if shift < 0 else 1), start : start + size, :]
            mask = values if mask is None else mask * values
        return mask

    def tap_list(self, stride):
        taps = []
        for vertical in range(3):
            for lateral in range(3):
                if stride == 2:
                    plane = 2 * (vertical != 1) + (lateral != 1)
                    taps.append((plane, -(vertical == 0), -(lateral == 0)))
                else:
                    taps.append((0, vertical - 1, lateral - 1))
        return taps

    def collect(self, chain, stride, padded, edges, taps_ref):
        mid = self.mid
        for position, (plane, down, right) in enumerate(self.tap_list(stride)):
            for index, segment in enumerate(chain.segments):
                shift = down * segment.down + right * segment.right
                base = GUARD + segment.start
                rows = slice(base + shift, base + shift + segment.size)
                values = padded[plane, rows, :] if stride == 2 else padded[rows, :]
                mask = self.edge(edges.at[index], base, segment.size, down, right)
                if mask is not None:
                    values = values * mask
                taps_ref[
                    segment.start : segment.stop, position * mid : (position + 1) * mid
                ] = values.astype(BF16)

    def spread(self, chain, stride, columns, edges):
        mid = self.mid
        taps = self.tap_list(stride)
        results = []
        for index, segment in enumerate(chain.segments):
            base = GUARD + segment.start
            for plane in range(4 if stride == 2 else 1):
                total = None
                for position, (where, down, right) in enumerate(taps):
                    if where != plane:
                        continue
                    start = base - (down * segment.down + right * segment.right)
                    values = columns[
                        start : start + segment.size, position * mid : (position + 1) * mid
                    ]
                    mask = self.edge(edges.at[index], start, segment.size, down, right)
                    if mask is not None:
                        values = values * mask
                    total = values if total is None else total + values
                results.append((segment, plane, self.keep(segment, total)))
        return results


    def clear(self, chain, link):
        rows = chain.rows
        for array in (link.h1, link.v1, link.dt):
            blank = jnp.zeros(array.shape[:-2] + (GUARD, array.shape[-1]), array.dtype)
            array[..., 0:GUARD, :] = blank
            array[..., GUARD + rows : 2 * GUARD + rows, :] = blank
        link.gm[...] = jnp.zeros_like(link.gm)
        link.gw[...] = jnp.zeros_like(link.gw)
        for segment in chain.segments:
            flags = [
                self.given.gates[segment.group][image].astype(F32)
                for image in range(segment.images)
            ]
            area = segment.side * segment.side
            link.gate[segment.start : segment.stop, :] = jnp.zeros((segment.size, LANE), F32)
            if segment.inside:
                rows = lax.broadcasted_iota(jnp.int32, (segment.size, LANE), 0)
                place = lax.rem(rows, segment.images)
                total = jnp.zeros((segment.size, LANE), F32)
                for image, flag in enumerate(flags):
                    total = jnp.where(place == image, flag, total)
                link.gate[segment.start : segment.stop, :] = total
            else:
                for image, flag in enumerate(flags):
                    start = segment.start + image * area
                    link.gate[start : start + area, :] = jnp.full((area, LANE), flag, F32)

    def gates(self, link, rows):
        return jnp.concatenate([link.gate[rows, :]] * (self.wide // LANE), axis=1)

    def bypass(self, chain, link, pixels):
        link.xs.full[self.mp] = pixels[0]
        yield from self.gather(link.xs)
        product = nn(self.joined(link.xs), self.weight(TENSOR_SC))
        link.bypass[...] = product
        totals = yield from self.reduce(link.fp, self.moments(chain, product))
        for index, segment in enumerate(chain.segments):
            rows = slice(segment.start, segment.stop)
            centre, factor = self.factors(
                totals[2 * index], totals[2 * index + 1], segment.count
            )
            link.facw[NORM_SC, index : index + 1, :] = factor
            link.bypass[rows, :] = (link.bypass[rows, :] - centre) * factor

    def chain(self, chain, link, given, made):
        rows = chain.rows
        mid = self.mid

        def into(full):
            def store(segment, values):
                full[self.mp, segment.start : segment.stop, :] = values

            return store

        pixels = given.pixels[...].reshape(4 * rows, self.inner)
        total = yield from self.scatter(link.z1, nt(pixels, self.weight(TENSOR_Q1)))
        total = total.reshape(4, rows, mid)
        link.n1[...] = total
        totals = yield from self.reduce(link.f1, self.moments(chain, total))

        def store_one(segment, values):
            start = GUARD + segment.start
            link.h1[:, start : start + segment.size, :] = values.astype(F32)

        self.narrow_norm(chain, link, NORM_Q1, link.n1, totals, link.n1, link.sl1, store_one)
        self.collect(chain, 2, link.h1, given.edges, link.t1)
        total = yield from self.scatter(link.z2, nt(link.t1[...], self.weight(TENSOR_S1)))
        link.n2[...] = total
        totals = yield from self.reduce(link.f2, self.moments(chain, total))
        self.narrow_norm(
            chain, link, NORM_S1, link.n2, totals, link.n2, link.sl2, into(link.h2.full)
        )
        yield from self.gather(link.h2)
        product = nn(self.joined(link.h2), self.weight(TENSOR_E1))
        link.n3[...] = product
        totals = yield from self.reduce(link.f3, self.moments(chain, product))
        for index, segment in enumerate(chain.segments):
            span = slice(segment.start, segment.stop)
            centre, factor = self.factors(
                totals[2 * index], totals[2 * index + 1], segment.count
            )
            link.facw[NORM_E1, index : index + 1, :] = factor
            normed = (link.n3[span, :] - centre) * factor
            link.n3[span, :] = normed
            joint = (normed * self.wide_row(NORM_E1, 0) + self.wide_row(NORM_E1, 1)) + (
                link.bypass[span, :] * self.wide_row(NORM_SC, 0) + self.wide_row(NORM_SC, 1)
            )
            logistic = jax.nn.sigmoid(joint)
            link.slq[span, :] = logistic * (1.0 + joint * (1.0 - logistic))
            widened = joint * logistic
            link.y[span, :] = widened
            link.r[span, :] = self.keep(segment, widened).astype(BF16)

        total = yield from self.scatter(link.u1, nt(link.r[...], self.weight(TENSOR_Q2)))
        link.n4[...] = total
        totals = yield from self.reduce(link.f4, self.moments(chain, total))

        def store_four(segment, values):
            start = GUARD + segment.start
            link.v1[start : start + segment.size, :] = values.astype(F32)

        self.narrow_norm(chain, link, NORM_Q2, link.n4, totals, link.n4, link.sl4, store_four)
        self.collect(chain, 1, link.v1, given.edges, link.t2)
        total = yield from self.scatter(link.u2, nt(link.t2[...], self.weight(TENSOR_S2)))
        link.n5[...] = total
        totals = yield from self.reduce(link.f5, self.moments(chain, total))
        self.narrow_norm(
            chain, link, NORM_S2, link.n5, totals, link.n5, link.sl5, into(link.v2.full)
        )
        yield from self.gather(link.v2)
        product = nn(self.joined(link.v2), self.weight(TENSOR_E2))
        link.n6[...] = product
        totals = yield from self.reduce(link.f6, self.moments(chain, product))

        terms = []
        for index, segment in enumerate(chain.segments):
            span = slice(segment.start, segment.stop)
            centre, factor = self.factors(
                totals[2 * index], totals[2 * index + 1], segment.count
            )
            link.facw[NORM_E2, index : index + 1, :] = factor
            normed = (link.n6[span, :] - centre) * factor
            link.n6[span, :] = normed
            gate = self.gates(link, span)
            final = link.y[span, :] + gate * (
                normed * self.wide_row(NORM_E2, 0) + self.wide_row(NORM_E2, 1)
            )
            logistic = jax.nn.sigmoid(final)
            made.out[span, :] = final * logistic
            slope = logistic * (1.0 + final * (1.0 - logistic))
            change = slope * given.cotangent[span, :].astype(F32)
            link.d2[span, :] = change
            gated = gate * change
            terms.append(self.sum_rows(gated))
            terms.append(self.sum_rows(gated * normed))
        totals = yield from self.reduce(link.r6, terms)
        gain_total = None
        offset_total = None
        for index, segment in enumerate(chain.segments):
            span = slice(segment.start, segment.stop)
            factor = link.facw[NORM_E2, index : index + 1, :]
            first, second = totals[2 * index], totals[2 * index + 1]
            gain_total = second if gain_total is None else gain_total + second
            offset_total = first if offset_total is None else offset_total + first
            change = (self.wide_row(NORM_E2, 0) * factor) * (
                self.gates(link, span) * link.d2[span, :]
                - first / segment.count
                - link.n6[span, :] * (second / segment.count)
            )
            link.du3[span, :] = self.keep(segment, change).astype(BF16)
        link.gw[4:5, :] = gain_total
        link.gw[5:6, :] = offset_total
        total = yield from self.scatter(link.b2, nt(link.du3[...], self.weight(TENSOR_E2)))
        gradients = total * link.sl5[...]
        link.d[0] = gradients
        totals = yield from self.reduce(link.r5, self.narrow_terms(chain, gradients, link.n5))
        self.narrow_back(
            chain, link, NORM_S2, link.d.at[0], totals, link.n5, into(link.g2.full)
        )
        yield from self.gather(link.g2)
        link.dt[GUARD : GUARD + rows, :] = nn(self.joined(link.g2), self.weight(TENSOR_S2))
        for segment, _, values in self.spread(chain, 1, link.dt, given.edges):
            span = slice(segment.start, segment.stop)
            link.d[0, span, :] = values * link.sl4[span, :]
        totals = yield from self.reduce(
            link.r4, self.narrow_terms(chain, link.d.at[0], link.n4)
        )
        self.narrow_back(
            chain, link, NORM_Q2, link.d.at[0], totals, link.n4, into(link.g1.full)
        )
        yield from self.gather(link.g1)

        link.d2[...] = (
            link.d2[...] + nn(self.joined(link.g1), self.weight(TENSOR_Q2))
        ) * link.slq[...]
        terms = []
        for segment in chain.segments:
            span = slice(segment.start, segment.stop)
            part = link.d2[span, :]
            terms.append(self.sum_rows(part))
            terms.append(self.sum_rows(part * link.n3[span, :]))
            terms.append(self.sum_rows(part * link.bypass[span, :]))
        totals = yield from self.reduce(link.r3, terms)
        sums = [None] * 3
        for index, segment in enumerate(chain.segments):
            span = slice(segment.start, segment.stop)
            part = link.d2[span, :]
            first = totals[3 * index]
            for which in range(3):
                value = totals[3 * index + which]
                sums[which] = value if sums[which] is None else sums[which] + value
            for norm, normed, target in (
                (NORM_E1, link.n3, link.dz3),
                (NORM_SC, link.bypass, link.dzp),
            ):
                factor = link.facw[norm, index : index + 1, :]
                second = totals[3 * index + 1 + norm]
                change = (self.wide_row(norm, 0) * factor) * (
                    part - first / segment.count - normed[span, :] * (second / segment.count)
                )
                target[span, :] = self.keep(segment, change).astype(BF16)
        link.gw[0:1, :] = sums[1]
        link.gw[1:2, :] = sums[0]
        link.gw[2:3, :] = sums[2]
        link.gw[3:4, :] = sums[0]
        total = yield from self.scatter(link.b1, nt(link.dz3[...], self.weight(TENSOR_E1)))
        gradients = total * link.sl2[...]
        link.d[0] = gradients
        totals = yield from self.reduce(link.r2, self.narrow_terms(chain, gradients, link.n2))
        self.narrow_back(
            chain, link, NORM_S1, link.d.at[0], totals, link.n2, into(link.k2.full)
        )
        yield from self.gather(link.k2)
        link.dt[GUARD : GUARD + rows, :] = nn(self.joined(link.k2), self.weight(TENSOR_S1))
        for segment, plane, values in self.spread(chain, 2, link.dt, given.edges):
            span = slice(segment.start, segment.stop)
            link.d[plane, span, :] = values * link.sl1[plane, span, :]
        totals = yield from self.reduce(link.r1, self.narrow_terms(chain, link.d, link.n1))

        def store_back_one(segment, values):
            for plane in range(4):
                start = plane * rows + segment.start
                link.k1.full[self.mp, start : start + segment.size, :] = values[plane]

        self.narrow_back(chain, link, NORM_Q1, link.d, totals, link.n1, store_back_one)
        yield from self.gather(link.k1)
        product = nn(self.joined(link.k1), self.weight(TENSOR_Q1))
        made.back[...] = product.reshape(4, rows, self.inner)

    def bypass_back(self, link):
        product = nt(link.dzp[...], self.weight(TENSOR_SC))
        total = yield from self.scatter(link.bx, product)
        link.back[...] = total


    def weight_product(self, tensor):
        total = None
        for link, given in zip(self.links, self.given.chains, strict=True):
            if tensor == TENSOR_Q1:
                pixels = given.pixels[...]
                part = tn(self.joined(link.k1), pixels.reshape(-1, self.inner))
            else:
                left, right = {
                    TENSOR_S1: (link.k2, link.t1),
                    TENSOR_E1: (link.h2, link.dz3),
                    TENSOR_SC: (link.xs, link.dzp),
                    TENSOR_Q2: (link.g1, link.r),
                    TENSOR_S2: (link.g2, link.t2),
                    TENSOR_E2: (link.v2, link.du3),
                }[tensor]
                part = tn(self.joined(left), right[...])
            total = part if total is None else total + part
        return total

    def weight_gradient(self, tensor):
        weight = self.weights[tensor]
        held = self.held[tensor]
        block, width, piece = weight.block, weight.width, weight.piece
        product = self.weight_product(tensor).astype(BF16)
        for tap in range(weight.taps):
            columns = product[:, tap * width : (tap + 1) * width]
            held.part[:, tap] = columns.reshape(self.mpn, block, width)
        theirs = self.half(block, 0, 1 - self.core)
        copy = self.remote(
            held.part.at[:, :, theirs, :],
            held.twin,
            held.twins.at[0],
            held.twins.at[1],
            (self.twin, self.mp),
        )
        copy.start()
        yield
        copy.wait()
        mine = held.part[:, :, self.half(block, 0, self.core), :]
        both = mine.astype(F32) + held.twin[...].astype(F32)
        for way in range(weight.ways):
            held.sums[way] = both[:, :, way * piece : (way + 1) * piece, :].astype(BF16)
        yield from (self.direct(held) if weight.direct else self.climb(held))
        copy = self.remote(
            held.fin, held.swap, held.swaps.at[0], held.swaps.at[1], (self.twin, self.mp)
        )
        copy.start()
        yield
        copy.wait()
        out = self.made.weights[tensor]
        copies = (
            pltpu.make_async_copy(held.fin, out.at[self.core], held.outs.at[0]),
            pltpu.make_async_copy(held.swap, out.at[1 - self.core], held.outs.at[1]),
        )
        for copy in copies:
            copy.start()
        yield
        for copy in copies:
            copy.wait()

    def mix(self, held, way, step, peer):
        return self.remote(
            held.sums.at[way, peer],
            held.fin.at[way, self.mp],
            held.mix_sent.at[step],
            held.mix_came.at[step],
            (self.dp, peer),
        )

    def mixed(self, held, way):
        for step, peer in enumerate(self.peers):
            self.mix(held, way, step, peer).wait_send()
            slot = held.fin.at[way, peer]
            self.remote(
                slot, slot, held.mix_sent.at[step], held.mix_came.at[step], (self.dp, peer)
            ).wait_recv()

    def direct(self, held):
        def above(level):
            return (level * 2 + self.core, self.mp)

        copies = []
        for step, level in enumerate(self.stack):
            copy = self.remote(
                held.sums.at[level],
                held.hop.at[self.z],
                held.hop_sent.at[step],
                held.hop_came.at[self.z],
                above(level),
            )
            copy.start()
            copies.append(copy)
        yield
        total = held.sums[self.z].astype(F32)
        for step, level in enumerate(self.stack):
            copies[step].wait_send()
            slot = held.hop.at[level]
            self.remote(
                slot, slot, held.hop_sent.at[step], held.hop_came.at[level], above(level)
            ).wait_recv()
            total = total + held.hop[level].astype(F32)
        held.sums[self.z] = total.astype(BF16)
        for step, peer in enumerate(self.peers):
            self.mix(held, self.z, step, peer).start()
        held.fin[self.z, self.mp] = held.sums[self.z, self.mp]
        yield
        self.mixed(held, self.z)
        mine = held.fin.at[self.z]
        copies = []
        for step, level in enumerate(self.stack):
            copy = self.remote(
                mine, mine, held.cast_sent.at[step], held.cast_came.at[self.z], above(level)
            )
            copy.start()
            copies.append(copy)
        yield
        for step, level in enumerate(self.stack):
            copies[step].wait_send()
            slot = held.fin.at[level]
            self.remote(
                slot, slot, held.cast_sent.at[step], held.cast_came.at[level], above(level)
            ).wait_recv()

    def climb(self, held):
        last = self.levels - 1

        def place(way, step):
            return step if way else last - step

        def onward(way):
            target = self.z + 1 if way else self.z - 1
            return (target * 2 + self.core, self.mp)

        def backward(way):
            target = self.z - 1 if way else self.z + 1
            return (target * 2 + self.core, self.mp)

        def hop(way, device):
            return self.remote(
                held.sums.at[way],
                held.hop.at[way],
                held.hop_sent.at[way],
                held.hop_came.at[way],
                device,
            )

        def cast(way, device):
            slot = held.fin.at[way]
            return self.remote(
                slot, slot, held.cast_sent.at[way], held.cast_came.at[way], device
            )

        for step in range(last + 1):
            for way in (0, 1):

                @pl.when(self.z == place(way, step))
                def _(way=way, step=step):
                    if step > 0:
                        hop(way, backward(way)).wait_recv()
                        total = held.sums[way].astype(F32) + held.hop[way].astype(F32)
                        held.sums[way] = total.astype(BF16)
                    if step < last:
                        hop(way, onward(way)).start()
                    else:
                        for index, peer in enumerate(self.peers):
                            self.mix(held, way, index, peer).start()
                        held.fin[way, self.mp] = held.sums[way, self.mp]

            yield
        for step in range(last, -1, -1):
            for way in (0, 1):

                @pl.when(self.z == place(way, step))
                def _(way=way, step=step):
                    if step == last:
                        self.mixed(held, way)
                    else:
                        hop(way, onward(way)).wait_send()
                        cast(way, onward(way)).wait_recv()
                    if step > 0:
                        cast(way, backward(way)).start()

            if step > 0:
                yield
        for way in (0, 1):

            @pl.when(self.z != place(way, 0))
            def _(way=way):
                cast(way, backward(way)).wait_send()


    def advance(self, tasks):
        for task in list(tasks):
            if next(task, self) is self:
                tasks.remove(task)

    def run(self):
        self.barrier()
        for tensor in (TENSOR_Q1, TENSOR_S1):
            self.weight_start(tensor)
        for chain, link in zip(self.chains, self.links, strict=True):
            self.clear(chain, link)
        parts = list(
            zip(self.chains, self.links, self.given.chains, self.made.chains, strict=True)
        )
        tasks = [self.chain(*part) for part in parts]
        background = []

        def start(tensor):
            return lambda: self.weight_start(tensor)

        def hand(tensor):
            return lambda: self.weight_pass(tensor)

        def grad(tensor):
            return lambda: background.append(self.weight_gradient(tensor))

        def bypass():
            for chain, link, given, _ in parts:
                background.append(self.bypass(chain, link, given.pixels))

        def bypass_back():
            for link in self.links:
                background.append(self.bypass_back(link))

        events = {
            1: (start(TENSOR_SC), bypass, start(TENSOR_E1)),
            2: (hand(TENSOR_S1), start(TENSOR_Q2)),
            4: (hand(TENSOR_SC), hand(TENSOR_E1), start(TENSOR_S2)),
            6: (hand(TENSOR_Q2), start(TENSOR_E2)),
            8: (hand(TENSOR_S2),),
            10: (hand(TENSOR_E2),),
            14: (grad(TENSOR_E2),),
            17: (grad(TENSOR_S2),),
            19: (grad(TENSOR_Q2),),
            20: (bypass_back, grad(TENSOR_E1), grad(TENSOR_SC)),
            23: (grad(TENSOR_S1),),
        }
        slot = 0
        while tasks:
            self.advance(tasks)
            slot += 1
            for event in events.get(slot, ()):
                event()
            self.advance(background)
        background.append(self.weight_gradient(TENSOR_Q1))
        self.advance(background)
        for link, made in zip(self.links, self.made.chains, strict=True):
            made.back[0] = made.back[0] + link.back[...]
        first, second = self.links
        self.made.mids[...] = first.gm[...] + second.gm[...]
        self.made.wides[...] = first.gw[...] + second.gw[...]
        while background:
            self.advance(background)


def kernel_text(trees, chains, weights, sizes, *refs):
    given_tree, made_tree, scratch_tree = trees
    given_size = given_tree.num_leaves
    made_size = made_tree.num_leaves
    given = jax.tree.unflatten(given_tree, refs[:given_size])
    made = jax.tree.unflatten(made_tree, refs[given_size : given_size + made_size])
    scratch = jax.tree.unflatten(scratch_tree, refs[given_size + made_size :])
    given = {**given, **dict(chains=[bag(value) for value in given["chains"]])}
    made = {**made, **dict(chains=[bag(value) for value in made["chains"]])}
    scratch = dict(
        chains=[bag(value) for value in scratch["chains"]],
        weights=[bag(value) for value in scratch["weights"]],
    )
    Body(bag(given), bag(made), bag(scratch), chains, weights, sizes).run()


def finish_text(chains, weights, sizes, *refs):
    mid, wide, inner, mpn = sizes
    count = len(weights)
    take = iter(refs)
    pieces = [next(take) for _ in range(count)]
    chain_in = [(next(take), next(take)) for _ in chains]
    mids, wides = next(take), next(take)
    outs = [next(take) for _ in range(count)]
    groups = [(next(take), next(take)) for _ in range(3)]
    mid_outs = [next(take) for _ in range(8)]
    wide_outs = [next(take) for _ in range(6)]
    near = [next(take) for _ in range(count)]
    wided = [next(take) for _ in range(count)]
    woven, came, gone, weave = next(take), next(take), next(take), next(take)
    arrivals = []
    for index in range(count):
        copy = pltpu.make_async_copy(pieces[index], near[index], came.at[index])
        copy.start()
        arrivals.append(copy)
    for row, out in enumerate(mid_outs):
        out[...] = mids[row, :]
    for row, out in enumerate(wide_outs):
        out[...] = wides[row, :]
    leaving = []
    for index, weight in enumerate(weights):
        arrivals[index].wait()
        width, piece = weight.width, weight.piece
        for core in range(2):
            for way in range(weight.ways):
                first = core * (weight.block // 2) + way * piece
                for source in range(mpn):
                    for tap in range(weight.taps):
                        wided[index][
                            tap, first : first + piece, source * width : (source + 1) * width
                        ] = near[index][core, way, source, tap].astype(F32)
        copy = pltpu.make_async_copy(wided[index], outs[index], gone.at[index])
        copy.start()
        leaving.append(copy)
    for chain, (out_rows, back_rows) in zip(chains, chain_in, strict=True):
        for segment in chain.segments:
            out, back = groups[segment.group]
            side = segment.side
            for i in range(side):
                if segment.inside:
                    for j in range(side):
                        start = segment.start + i * segment.down + j * segment.right
                        rows = slice(start, start + segment.images)
                        out[i, j] = out_rows[rows, :]
                        for plane in range(4):
                            back[2 * i + plane // 2, 2 * j + plane % 2] = back_rows[
                                plane, rows, :
                            ]
                    continue
                for image in range(segment.images):
                    start = segment.start + image * side * side + i * side
                    rows = slice(start, start + side)
                    out[image, i] = out_rows[rows, :]
                    for plane in range(4):
                        for lane in range(inner // LANE):
                            woven[
                                lane,
                                image,
                                2 * i + plane // 2,
                                pl.ds(plane % 2, side, stride=2),
                                :,
                            ] = back_rows[plane, rows, lane * LANE : (lane + 1) * LANE]
            if segment.inside:
                continue
            for lane in range(inner // LANE):
                copy = pltpu.make_async_copy(
                    woven.at[lane],
                    back.at[:, :, :, pl.ds(lane * LANE, LANE)],
                    weave.at[lane],
                )
                copy.start()
                leaving.append(copy)
    for copy in leaving:
        copy.wait()


def padded_rows(values, size):
    extra = size - values.shape[-2]
    if extra == 0:
        return values
    widths = [(0, 0)] * (values.ndim - 2) + [(0, extra), (0, 0)]
    return jnp.pad(values, widths)


def planes_of(segment, images):
    side = segment.side
    channels = images.shape[3]
    values = segment.pixel_first(images)
    if segment.inside:
        split = values.reshape(side, 2, side, 2, segment.images, channels)
        split = split.transpose(1, 3, 0, 2, 4, 5)
    else:
        split = values.reshape(segment.images, side, 2, side, 2, channels)
        split = split.transpose(2, 4, 0, 1, 3, 5)
    return padded_rows(split.reshape(4, segment.real, channels), segment.size)


def edge_masks(chain):
    masks = np.zeros((len(chain.segments), 4, chain.padded, LANE), np.float32)
    for place, segment in enumerate(chain.segments):
        index = np.arange(segment.real)
        down = index // segment.down % segment.side
        right = index // segment.right % segment.side
        start = GUARD + segment.start
        last = segment.side - 1
        for which, inside in enumerate((down > 0, down < last, right > 0, right < last)):
            masks[place, which, start : start + segment.real] = inside[:, None]
    return jnp.asarray(masks)


def fused_device(dpn, mpn, *args):
    images, widths, gates, cotangents = args[0:3], args[3], args[4:7], args[7:10]
    q1, s1, e1, sc, q2, s2, e2 = (args[index] for index in (10, 13, 16, 19, 22, 25, 28))
    mids = [args[index] for index in (11, 12, 14, 15, 23, 24, 26, 27)]
    wides = [args[index] for index in (17, 18, 20, 21, 29, 30)]
    mid = q1.shape[0]
    wide = wides[0].shape[0]
    inner = images[0].shape[3]
    shapes = [(values.shape[0], values.shape[1]) for values in images]
    chains = [Chain((2, 0), shapes, dpn), Chain((1,), shapes, dpn)]
    weights = weight_table(mid, wide, inner)
    sizes = (mid, wide, inner, dpn, mpn)
    vmem = pl.BlockSpec(memory_space=VMEM)
    smem = pl.BlockSpec(memory_space=pltpu.SMEM)
    anywhere = pl.BlockSpec(memory_space=pl.ANY)

    def by_tap(spatial):
        return spatial.transpose(1, 2, 0, 3).reshape(9, mid, mpn * mid)

    def rows_of(chain, build):
        return jnp.concatenate([build(s) for s in chain.segments], axis=-2)

    given = dict(
        chains=[
            dict(
                pixels=rows_of(chain, lambda s: planes_of(s, images[s.group])),
                cotangent=rows_of(
                    chain,
                    lambda s: padded_rows(
                        s.pixel_first(cotangents[s.group]).reshape(s.real, wide), s.size
                    ),
                ),
                edges=edge_masks(chain),
            )
            for chain in chains
        ],
        mids=mids,
        wides=wides,
        widths=widths,
        gates=list(gates),
        weights=[q1[None], by_tap(s1), e1[None], sc[None], q2[None], by_tap(s2), e2[None]],
    )
    given_specs = dict(
        chains=[dict(pixels=vmem, cotangent=vmem, edges=vmem) for _ in chains],
        mids=[vmem] * len(mids),
        wides=[vmem] * len(wides),
        widths=smem,
        gates=[smem] * 3,
        weights=[anywhere] * WEIGHTS,
    )
    shape = jax.ShapeDtypeStruct
    made = dict(
        chains=[
            dict(
                out=shape((chain.rows, wide), F32), back=shape((4, chain.rows, inner), F32)
            )
            for chain in chains
        ],
        mids=shape((8, mid), F32),
        wides=shape((8, wide), F32),
        weights=[
            shape((2, w.ways, mpn, w.taps, w.piece, w.width), BF16) for w in weights
        ],
    )
    made_specs = dict(
        chains=[dict(out=vmem, back=vmem) for _ in chains],
        mids=vmem,
        wides=vmem,
        weights=[anywhere] * WEIGHTS,
    )
    scratch = dict(
        chains=[chain_scratch(chain, mid, wide, inner, dpn, mpn) for chain in chains],
        weights=[weight_scratch(weight, dpn, mpn) for weight in weights],
    )
    trees = tuple(jax.tree.structure(tree) for tree in (given_specs, made_specs, scratch))
    results = pl.pallas_call(
        functools.partial(kernel_text, trees, chains, weights, sizes),
        out_shape=jax.tree.leaves(made),
        in_specs=jax.tree.leaves(given_specs),
        out_specs=jax.tree.leaves(made_specs),
        scratch_shapes=jax.tree.leaves(scratch),
        compiler_params=pltpu.CompilerParams(
            collective_id=0, has_side_effects=True, vmem_limit_bytes=62 * 2**20
        ),
        name="bottlenecks",
    )(*jax.tree.leaves(given))
    got = bag(jax.tree.unflatten(trees[1], results))

    final_shapes = [shape((w.taps, w.block, mpn * w.width), F32) for w in weights]
    segments = sorted((s for chain in chains for s in chain.segments), key=lambda s: s.group)

    def laid(s, side, channels):
        if s.inside:
            return shape((side, side, s.images, channels), F32)
        return shape((s.images, side, side, channels), F32)

    group_shapes = []
    for s in segments:
        group_shapes += [laid(s, s.side, wide), laid(s, 2 * s.side, inner)]
    woven = [laid(s, 2 * s.side, inner) for s in segments if not s.inside]
    vector_shapes = [shape((mid,), F32)] * 8 + [shape((wide,), F32)] * 6
    chain_in = []
    for value in got.chains:
        chain_in += [value["out"], value["back"]]
    final = pl.pallas_call(
        functools.partial(finish_text, chains, weights, (mid, wide, inner, mpn)),
        out_shape=final_shapes + group_shapes + vector_shapes,
        in_specs=[anywhere] * WEIGHTS + [vmem] * (len(chain_in) + 2),
        out_specs=[anywhere] * WEIGHTS
        + [spec for s in segments for spec in (vmem, vmem if s.inside else anywhere)]
        + [vmem] * len(vector_shapes),
        scratch_shapes=[VMEM(value.shape, BF16) for value in made["weights"]]
        + [VMEM(value.shape, F32) for value in final_shapes]
        + [VMEM((inner // LANE, *woven[0].shape[:3], LANE), F32)]
        + [DMA((WEIGHTS,)), DMA((WEIGHTS,)), DMA((inner // LANE,))],
        compiler_params=pltpu.CompilerParams(vmem_limit_bytes=48 * 2**20),
        name="finish",
    )(*got.weights, *chain_in, got.mids, got.wides)
    tensors = final[:WEIGHTS]
    grads = [value[0] for value in tensors]
    for place in (TENSOR_S1, TENSOR_S2):
        split = tensors[place].reshape(3, 3, mid, mpn * mid)
        grads[place] = split.transpose(2, 0, 1, 3)
    laid_out = final[WEIGHTS : WEIGHTS + 6]
    outputs = [s.image_first(laid_out[2 * s.group]) for s in segments]
    input_grads = [s.image_first(laid_out[2 * s.group + 1]) for s in segments]
    gm = final[WEIGHTS + 6 : WEIGHTS + 14]
    gw = final[WEIGHTS + 14 :]
    return (
        *outputs,
        *input_grads,
        grads[TENSOR_Q1],
        gm[0],
        gm[1],
        grads[TENSOR_S1],
        gm[2],
        gm[3],
        grads[TENSOR_E1],
        gw[0],
        gw[1],
        grads[TENSOR_SC],
        gw[2],
        gw[3],
        grads[TENSOR_Q2],
        gm[4],
        gm[5],
        grads[TENSOR_S2],
        gm[6],
        gm[7],
        grads[TENSOR_E2],
        gw[4],
        gw[5],
    )


def fits_kernel(mesh, args):
    mid = args[10].shape[0]
    inner = args[0].shape[3]
    wide = args[17].shape[0]
    return (
        mesh.shape["mp"] == 4
        and mesh.shape["dp"] == 8
        and mid == LANE
        and inner % LANE == 0
        and wide % LANE == 0
    )


def per_device(mesh, *args):
    if fits_kernel(mesh, args):
        return fused_device(mesh.shape["dp"], mesh.shape["mp"], *args)
    return on_device(*args)


def solution(mesh):
    in_specs = (
        P("dp", None, None, "mp"),
        P("dp", None, None, "mp"),
        P("dp", None, None, "mp"),
        P(),
        P("dp"),
        P("dp"),
        P("dp"),
        P("dp", None, None, "mp"),
        P("dp", None, None, "mp"),
        P("dp", None, None, "mp"),
        P("mp", None),
        P("mp"),
        P("mp"),
        P("mp", None, None, None),
        P("mp"),
        P("mp"),
        P("mp", None),
        P("mp"),
        P("mp"),
        P("mp", None),
        P("mp"),
        P("mp"),
        P("mp", None),
        P("mp"),
        P("mp"),
        P("mp", None, None, None),
        P("mp"),
        P("mp"),
        P("mp", None),
        P("mp"),
        P("mp"),
    )
    out_specs = (
        P("dp", None, None, "mp"),
        P("dp", None, None, "mp"),
        P("dp", None, None, "mp"),
        P("dp", None, None, "mp"),
        P("dp", None, None, "mp"),
        P("dp", None, None, "mp"),
        P("mp", None),
        P("mp"),
        P("mp"),
        P("mp", None, None, None),
        P("mp"),
        P("mp"),
        P("mp", None),
        P("mp"),
        P("mp"),
        P("mp", None),
        P("mp"),
        P("mp"),
        P("mp", None),
        P("mp"),
        P("mp"),
        P("mp", None, None, None),
        P("mp"),
        P("mp"),
        P("mp", None),
        P("mp"),
        P("mp"),
    )
    return jax.shard_map(
        functools.partial(per_device, mesh),
        mesh=mesh,
        in_specs=in_specs,
        out_specs=out_specs,
        check_vma=False,
    )
```

```python
import functools
import types

import jax
import jax.numpy as jnp
import numpy as np
from jax import lax
from jax.experimental import pallas as pl
from jax.experimental.pallas import tpu as pltpu
from jax.sharding import PartitionSpec as P

EPSILON = 1e-05


def sigmoid_linear(values):
    return values * jax.nn.sigmoid(values)


def sigmoid_slope(values):
    logistic = jax.nn.sigmoid(values)
    return logistic * (1.0 + values * (1.0 - logistic))


def pointwise(hidden, weight):
    return jnp.einsum("nhwc,cd->nhwd", hidden, weight, preferred_element_type=jnp.float32)


def back_pointwise(gradients, weight):
    return jnp.einsum("nhwd,cd->nhwc", gradients, weight, preferred_element_type=jnp.float32)


def weight_term(activations, gradients):
    return jnp.einsum("nhwc,nhwd->cd", activations, gradients, preferred_element_type=jnp.float32)


def reduce_pointwise(hidden, weight):
    return jnp.einsum("nhwc,dc->nhwd", hidden, weight, preferred_element_type=jnp.float32)


def reduce_back(gradients, weight):
    return jnp.einsum("nhwd,dc->nhwc", gradients, weight, preferred_element_type=jnp.float32)


def reduce_term(gradients, activations):
    return jnp.einsum("nhwd,nhwc->dc", gradients, activations, preferred_element_type=jnp.float32)


def gather_taps(hidden, stride):
    extent = hidden.shape[1] // stride
    span_end = stride * (extent - 1) + 1
    padded = jnp.pad(hidden, ((0, 0), (1, 1), (1, 1), (0, 0)))
    pieces = [
        padded[:, vertical : vertical + span_end : stride, lateral : lateral + span_end : stride, :]
        for vertical in range(3)
        for lateral in range(3)
    ]
    return jnp.concatenate(pieces, axis=3)


def spread_taps(columns, stride, edge_size, channels):
    extent = columns.shape[1]
    span_end = stride * (extent - 1) + 1
    padded = jnp.zeros((columns.shape[0], edge_size + 2, edge_size + 2, channels), jnp.float32)
    for position in range(9):
        vertical = position // 3
        lateral = position % 3
        padded = padded.at[
            :, vertical : vertical + span_end : stride, lateral : lateral + span_end : stride, :
        ].add(columns[..., position * channels : (position + 1) * channels])
    return padded[:, 1:-1, 1:-1, :]


def stat_terms(values):
    return jnp.stack([jnp.sum(values, axis=(0, 1, 2)), jnp.sum(values * values, axis=(0, 1, 2))])


def grad_terms(gradients, normed):
    return jnp.stack(
        [jnp.sum(gradients, axis=(0, 1, 2)), jnp.sum(gradients * normed, axis=(0, 1, 2))]
    )


def samples_of(values):
    return values.shape[0] * values.shape[1] * values.shape[2] * lax.axis_size("dp")


def norm_apply(values, totals, samples, norm_gain, offset):
    centre = totals[0] / samples
    spread = totals[1] / samples - centre * centre
    factor = lax.rsqrt(spread + EPSILON)
    normed = (values - centre) * factor
    return (normed, factor, normed * norm_gain + offset)


def norm_back(gradients, normed, factor, totals, samples, norm_gain):
    return norm_gain * factor * (gradients - totals[0] / samples - normed * (totals[1] / samples))


def forward_totals(partials):
    return lax.psum(jnp.stack(partials), "dp")


def backward_totals(partials):
    return lax.psum(jnp.stack(partials), "dp")


def gather_channels(pieces):
    return (
        lax.all_gather(pieces[0], "mp", axis=3, tiled=True),
        lax.all_gather(pieces[1], "mp", axis=3, tiled=True),
        lax.all_gather(pieces[2], "mp", axis=3, tiled=True),
    )


def gather_hidden(pieces):
    return (
        lax.all_gather(pieces[0], "mp", axis=3, tiled=True),
        lax.all_gather(pieces[1], "mp", axis=3, tiled=True),
        lax.all_gather(pieces[2], "mp", axis=3, tiled=True),
    )


def gather_spatial_grads(pieces):
    return (
        lax.all_gather(pieces[0], "mp", axis=3, tiled=True),
        lax.all_gather(pieces[1], "mp", axis=3, tiled=True),
        lax.all_gather(pieces[2], "mp", axis=3, tiled=True),
    )


def gather_entry_grads(pieces):
    return (
        lax.all_gather(pieces[0], "mp", axis=3, tiled=True),
        lax.all_gather(pieces[1], "mp", axis=3, tiled=True),
        lax.all_gather(pieces[2], "mp", axis=3, tiled=True),
    )


def front_forward(gathered, stride, params, width_masks):
    squeeze, squeeze_gain, squeeze_offset, spatial_conv, spatial_gain, spatial_offset = params
    entry = [reduce_pointwise(values, squeeze) for values in gathered]
    entry_totals = forward_totals([stat_terms(values) for values in entry])
    entry_norm = [
        norm_apply(
            entry[member],
            entry_totals[member],
            samples_of(entry[member]),
            squeeze_gain,
            squeeze_offset,
        )
        for member in range(3)
    ]
    hidden = [
        (width_masks[member] * sigmoid_linear(entry_norm[member][2])).astype(jnp.bfloat16)
        for member in range(3)
    ]
    hidden_full = gather_hidden(hidden)
    taps = [gather_taps(values, stride) for values in hidden_full]
    spatial_rows = spatial_conv.reshape(spatial_conv.shape[0], -1)
    middle = [reduce_pointwise(values, spatial_rows) for values in taps]
    middle_totals = forward_totals([stat_terms(values) for values in middle])
    middle_norm = [
        norm_apply(
            middle[member],
            middle_totals[member],
            samples_of(middle[member]),
            spatial_gain,
            spatial_offset,
        )
        for member in range(3)
    ]
    narrow = [
        (width_masks[member] * sigmoid_linear(middle_norm[member][2])).astype(jnp.bfloat16)
        for member in range(3)
    ]
    return (entry_norm, taps, middle_norm, narrow)


def front_backward(narrow_grads, saved, gathered, stride, params, width_masks, column_weights):
    squeeze, squeeze_gain, squeeze_offset, spatial_conv, spatial_gain, spatial_offset = params
    entry_norm, taps, middle_norm, narrow = saved
    middle_out = [
        narrow_grads[member] * width_masks[member] * sigmoid_slope(middle_norm[member][2])
        for member in range(3)
    ]
    middle_totals = backward_totals(
        [grad_terms(middle_out[member], middle_norm[member][0]) for member in range(3)]
    )
    middle_grads = [
        norm_back(
            middle_out[member],
            middle_norm[member][0],
            middle_norm[member][1],
            middle_totals[member],
            samples_of(middle_out[member]),
            spatial_gain,
        ).astype(jnp.bfloat16)
        for member in range(3)
    ]
    spatial_grad = sum(
        (reduce_term(middle_grads[member], taps[member]) for member in range(3))
    ).reshape(spatial_conv.shape)
    squeeze_cols, spatial_cols = column_weights
    channels = spatial_cols.shape[3]
    spatial_flat = spatial_cols.reshape(spatial_cols.shape[0], -1)
    middle_full = gather_spatial_grads(middle_grads)
    hidden_grads = [
        spread_taps(
            reduce_back(middle_full[member], spatial_flat),
            stride,
            gathered[member].shape[1],
            channels,
        )
        for member in range(3)
    ]
    entry_out = [
        hidden_grads[member] * width_masks[member] * sigmoid_slope(entry_norm[member][2])
        for member in range(3)
    ]
    entry_totals = backward_totals(
        [grad_terms(entry_out[member], entry_norm[member][0]) for member in range(3)]
    )
    entry_grads = [
        norm_back(
            entry_out[member],
            entry_norm[member][0],
            entry_norm[member][1],
            entry_totals[member],
            samples_of(entry_out[member]),
            squeeze_gain,
        ).astype(jnp.bfloat16)
        for member in range(3)
    ]
    squeeze_grad = sum((reduce_term(entry_grads[member], gathered[member]) for member in range(3)))
    entry_full = gather_entry_grads(entry_grads)
    squeeze_flat = squeeze_cols.reshape(squeeze_cols.shape[0], -1)
    input_part = [reduce_back(entry_full[member], squeeze_flat) for member in range(3)]
    gain_grads = (
        jnp.sum(entry_totals[:, 1], axis=0),
        jnp.sum(entry_totals[:, 0], axis=0),
        jnp.sum(middle_totals[:, 1], axis=0),
        jnp.sum(middle_totals[:, 0], axis=0),
    )
    return (input_part, squeeze_grad, spatial_grad, gain_grads)


def tail_forward(narrow, bypass_inputs, expand, shortcut):
    partials = []
    for member in range(3):
        pieces = [pointwise(narrow[member], expand)]
        if shortcut is not None:
            pieces.append(pointwise(bypass_inputs[member], shortcut))
        partials.append(jnp.stack(pieces))
    partials = (
        lax.psum_scatter(
            partials[0].astype(jnp.bfloat16), "mp", scatter_dimension=4, tiled=True
        ).astype(jnp.float32),
        lax.psum_scatter(
            partials[1].astype(jnp.bfloat16), "mp", scatter_dimension=4, tiled=True
        ).astype(jnp.float32),
        lax.psum_scatter(
            partials[2].astype(jnp.bfloat16), "mp", scatter_dimension=4, tiled=True
        ).astype(jnp.float32),
    )
    return (partials, narrow)


def tail_backward(gradients, sources, bypass_inputs, expand, shortcut):
    arriving = (
        lax.all_gather(gradients[0], "mp", axis=4, tiled=True),
        lax.all_gather(gradients[1], "mp", axis=4, tiled=True),
        lax.all_gather(gradients[2], "mp", axis=4, tiled=True),
    )
    expand_grad = sum((weight_term(sources[member], arriving[member][0]) for member in range(3)))
    narrow_terms = [back_pointwise(arriving[member][0], expand) for member in range(3)]
    if shortcut is None:
        return (narrow_terms, expand_grad, None, None)
    shortcut_grad = sum(
        (weight_term(bypass_inputs[member], arriving[member][1]) for member in range(3))
    )
    bypass_terms = [back_pointwise(arriving[member][1], shortcut) for member in range(3)]
    return (narrow_terms, expand_grad, shortcut_grad, bypass_terms)


def on_device(
    images_small,
    images_medium,
    images_large,
    width_choice,
    gates_small,
    gates_medium,
    gates_large,
    cotangent_small,
    cotangent_medium,
    cotangent_large,
    squeeze_one,
    squeeze_gain_one,
    squeeze_offset_one,
    spatial_one,
    spatial_gain_one,
    spatial_offset_one,
    expand_one,
    expand_gain_one,
    expand_offset_one,
    shortcut_one,
    shortcut_gain,
    shortcut_offset,
    squeeze_two,
    squeeze_gain_two,
    squeeze_offset_two,
    spatial_two,
    spatial_gain_two,
    spatial_offset_two,
    expand_two,
    expand_gain_two,
    expand_offset_two,
):
    images = [images_small, images_medium, images_large]
    depth_gates = [
        flags.astype(jnp.float32)[:, None, None, None]
        for flags in (gates_small, gates_medium, gates_large)
    ]
    cotangents = [
        values.astype(jnp.float32)
        for values in (cotangent_small, cotangent_medium, cotangent_large)
    ]
    mid_local = squeeze_one.shape[0]
    channel_index = lax.axis_index("mp") * mid_local + jnp.arange(mid_local, dtype=jnp.int32)
    limits = mid_local * lax.axis_size("mp") * (2 + width_choice) // 4
    width_masks = [(channel_index < limits[member]).astype(jnp.float32) for member in range(3)]
    out_local = expand_gain_one.shape[0]
    params_one = (
        squeeze_one,
        squeeze_gain_one,
        squeeze_offset_one,
        spatial_one,
        spatial_gain_one,
        spatial_offset_one,
    )
    params_two = (
        squeeze_two,
        squeeze_gain_two,
        squeeze_offset_two,
        spatial_two,
        spatial_gain_two,
        spatial_offset_two,
    )
    expand_first, bypass_weight, expand_second = (expand_one, shortcut_one, expand_two)
    squeeze_cols_one, spatial_cols_one, squeeze_cols_two, spatial_cols_two = (
        lax.all_to_all(
            squeeze_one.reshape(mid_local, 1, 1, -1), "mp", split_axis=3, concat_axis=0, tiled=True
        ),
        lax.all_to_all(spatial_one, "mp", split_axis=3, concat_axis=0, tiled=True),
        lax.all_to_all(
            squeeze_two.reshape(mid_local, 1, 1, -1), "mp", split_axis=3, concat_axis=0, tiled=True
        ),
        lax.all_to_all(spatial_two, "mp", split_axis=3, concat_axis=0, tiled=True),
    )
    columns_one = (squeeze_cols_one, spatial_cols_one)
    columns_two = (squeeze_cols_two, spatial_cols_two)
    first_full = gather_channels(images)
    first_saved = front_forward(first_full, 2, params_one, width_masks)
    bypass_inputs = [values[:, ::2, ::2, :] for values in images]
    first_tail, first_sources = tail_forward(
        first_saved[3], bypass_inputs, expand_first, bypass_weight
    )
    first_totals = forward_totals(
        [
            jnp.concatenate(
                [stat_terms(first_tail[member][0]), stat_terms(first_tail[member][1])], axis=1
            )
            for member in range(3)
        ]
    )
    widened_norm = [
        norm_apply(
            first_tail[member][0],
            first_totals[member][:, :out_local],
            samples_of(first_tail[member][0]),
            expand_gain_one,
            expand_offset_one,
        )
        for member in range(3)
    ]
    bypass_norm = [
        norm_apply(
            first_tail[member][1],
            first_totals[member][:, out_local:],
            samples_of(first_tail[member][1]),
            shortcut_gain,
            shortcut_offset,
        )
        for member in range(3)
    ]
    first_sum = [widened_norm[member][2] + bypass_norm[member][2] for member in range(3)]
    block_out = [sigmoid_linear(values) for values in first_sum]
    second_full = gather_channels([values.astype(jnp.bfloat16) for values in block_out])
    second_saved = front_forward(second_full, 1, params_two, width_masks)
    second_tail, second_sources = tail_forward(second_saved[3], None, expand_second, None)
    second_totals = forward_totals([stat_terms(second_tail[member][0]) for member in range(3)])
    final_norm = [
        norm_apply(
            second_tail[member][0],
            second_totals[member],
            samples_of(second_tail[member][0]),
            expand_gain_two,
            expand_offset_two,
        )
        for member in range(3)
    ]
    second_sum = [
        block_out[member] + depth_gates[member] * final_norm[member][2] for member in range(3)
    ]
    results = [sigmoid_linear(values) for values in second_sum]
    second_slope = [sigmoid_slope(second_sum[member]) * cotangents[member] for member in range(3)]
    final_out = [depth_gates[member] * second_slope[member] for member in range(3)]
    final_totals = backward_totals(
        [grad_terms(final_out[member], final_norm[member][0]) for member in range(3)]
    )
    final_grads = [
        norm_back(
            final_out[member],
            final_norm[member][0],
            final_norm[member][1],
            final_totals[member],
            samples_of(final_out[member]),
            expand_gain_two,
        ).astype(jnp.bfloat16)[None]
        for member in range(3)
    ]
    second_result = tail_backward(final_grads, second_sources, None, expand_second, None)
    second_input_part, squeeze_two_grad, spatial_two_grad, second_gain_grads = front_backward(
        second_result[0], second_saved, second_full, 1, params_two, width_masks, columns_two
    )
    expand_two_grad = second_result[1]
    block_grads = [second_slope[member] + second_input_part[member] for member in range(3)]
    first_slope = [sigmoid_slope(first_sum[member]) * block_grads[member] for member in range(3)]
    first_grad_totals = backward_totals(
        [
            jnp.concatenate(
                [
                    grad_terms(first_slope[member], widened_norm[member][0]),
                    grad_terms(first_slope[member], bypass_norm[member][0]),
                ],
                axis=1,
            )
            for member in range(3)
        ]
    )
    tail_grads = [
        jnp.stack(
            [
                norm_back(
                    first_slope[member],
                    widened_norm[member][0],
                    widened_norm[member][1],
                    first_grad_totals[member][:, :out_local],
                    samples_of(first_slope[member]),
                    expand_gain_one,
                ),
                norm_back(
                    first_slope[member],
                    bypass_norm[member][0],
                    bypass_norm[member][1],
                    first_grad_totals[member][:, out_local:],
                    samples_of(first_slope[member]),
                    shortcut_gain,
                ),
            ]
        ).astype(jnp.bfloat16)
        for member in range(3)
    ]
    first_result = tail_backward(
        tail_grads, first_sources, bypass_inputs, expand_first, bypass_weight
    )
    expand_one_grad = first_result[1]
    shortcut_grad = first_result[2]
    bypass_terms = first_result[3]
    first_input_part, squeeze_one_grad, spatial_one_grad, first_gain_grads = front_backward(
        first_result[0], first_saved, first_full, 2, params_one, width_masks, columns_one
    )
    input_grads = [
        first_input_part[member].at[:, ::2, ::2, :].add(bypass_terms[member]) for member in range(3)
    ]
    summed = (
        lax.psum(squeeze_one_grad.astype(jnp.bfloat16), "dp").astype(jnp.float32),
        lax.psum(spatial_one_grad.astype(jnp.bfloat16), "dp").astype(jnp.float32),
        lax.psum(expand_one_grad.astype(jnp.bfloat16), "dp").astype(jnp.float32),
        lax.psum(shortcut_grad.astype(jnp.bfloat16), "dp").astype(jnp.float32),
        lax.psum(squeeze_two_grad.astype(jnp.bfloat16), "dp").astype(jnp.float32),
        lax.psum(spatial_two_grad.astype(jnp.bfloat16), "dp").astype(jnp.float32),
        lax.psum(expand_two_grad.astype(jnp.bfloat16), "dp").astype(jnp.float32),
    )
    expand_gain_one_grad = jnp.sum(first_grad_totals[:, 1, :out_local], axis=0)
    expand_offset_one_grad = jnp.sum(first_grad_totals[:, 0, :out_local], axis=0)
    shortcut_gain_grad = jnp.sum(first_grad_totals[:, 1, out_local:], axis=0)
    shortcut_offset_grad = jnp.sum(first_grad_totals[:, 0, out_local:], axis=0)
    expand_gain_two_grad = jnp.sum(final_totals[:, 1], axis=0)
    expand_offset_two_grad = jnp.sum(final_totals[:, 0], axis=0)
    return (
        results[0],
        results[1],
        results[2],
        input_grads[0],
        input_grads[1],
        input_grads[2],
        summed[0],
        first_gain_grads[0],
        first_gain_grads[1],
        summed[1],
        first_gain_grads[2],
        first_gain_grads[3],
        summed[2],
        expand_gain_one_grad,
        expand_offset_one_grad,
        summed[3],
        shortcut_gain_grad,
        shortcut_offset_grad,
        summed[4],
        second_gain_grads[0],
        second_gain_grads[1],
        summed[5],
        second_gain_grads[2],
        second_gain_grads[3],
        summed[6],
        expand_gain_two_grad,
        expand_offset_two_grad,
    )


LANE = 128
GUARD = 32
MESH_ID = pl.DeviceIdType.MESH
DMA = pltpu.SemaphoreType.DMA
VMEM = pltpu.VMEM
F32 = jnp.float32
BF16 = jnp.bfloat16
WEIGHTS = 7
TENSOR_Q1, TENSOR_S1, TENSOR_E1, TENSOR_SC, TENSOR_Q2, TENSOR_S2, TENSOR_E2 = range(WEIGHTS)
NORM_Q1, NORM_S1, NORM_Q2, NORM_S2 = range(4)
NORM_E1, NORM_SC, NORM_E2 = range(3)


def nn(left, right):
    return lax.dot_general(left, right, (((1,), (0,)), ((), ())), preferred_element_type=F32)


def nt(left, right):
    return lax.dot_general(left, right, (((1,), (1,)), ((), ())), preferred_element_type=F32)


def tn(left, right):
    return lax.dot_general(left, right, (((0,), (0,)), ((), ())), preferred_element_type=F32)


def bag(tree):
    if isinstance(tree, dict):
        return types.SimpleNamespace(**{name: bag(value) for name, value in tree.items()})
    return tree


class Segment:
    def __init__(self, group, start, images, side, replicas):
        self.group = group
        self.side = side
        self.images = images
        self.inside = images <= 4
        self.right = images if self.inside else 1
        self.down = self.right * side
        self.start = start
        self.real = images * side * side
        self.size = -(-self.real // 16) * 16
        self.stop = start + self.size
        self.count = float(self.real * replicas)

    def pixel_first(self, values):
        return values.transpose(1, 2, 0, 3) if self.inside else values

    def image_first(self, values):
        return values.transpose(2, 0, 1, 3) if self.inside else values


class Chain:
    def __init__(self, groups, shapes, replicas):
        self.segments = []
        start = 0
        for group in groups:
            images, side = shapes[group]
            segment = Segment(group, start, images, side // 2, replicas)
            self.segments.append(segment)
            start = segment.stop
        self.rows = start
        self.padded = start + 2 * GUARD


class Weight:
    def __init__(self, block, width, taps):
        self.block = block
        self.width = width
        self.taps = taps


def weight_table(mid, wide, inner):
    return [
        Weight(mid, inner, 1),
        Weight(mid, mid, 9),
        Weight(mid, wide, 1),
        Weight(inner, wide, 1),
        Weight(mid, wide, 1),
        Weight(mid, mid, 9),
        Weight(mid, wide, 1),
    ]


class Unit:
    def __init__(self, tensor, weight, part, parts, direct=False):
        self.tensor = tensor
        self.block = weight.block
        self.taps = weight.taps // parts if weight.taps > 1 else 1
        self.width = weight.width if weight.taps > 1 else weight.width // parts
        self.first_tap = part * self.taps if weight.taps > 1 else 0
        self.first_column = 0 if weight.taps > 1 else part * self.width
        self.span = self.taps * self.width
        self.columns = slice(part * self.span, (part + 1) * self.span)
        self.direct = direct
        self.ways = 4 if direct else 2
        self.piece = weight.block // (2 * self.ways)


def unit_table(weights):
    units = []
    for tensor, parts in (
        (TENSOR_E2, 1),
        (TENSOR_S2, 3),
        (TENSOR_Q2, 1),
        (TENSOR_E1, 1),
        (TENSOR_SC, 2),
        (TENSOR_S1, 3),
        (TENSOR_Q1, 1),
    ):
        for part in range(parts):
            units.append(
                Unit(tensor, weights[tensor], part, parts, direct=tensor == TENSOR_Q1)
            )
    return units


def chain_scratch(chain, mid, wide, inner, dpn, mpn):
    rows = chain.rows
    padded = chain.padded
    near = mpn - 1

    def summed(lead, width):
        return dict(
            send=VMEM((mpn, lead, width), BF16),
            recv=VMEM((near, lead, width), BF16),
            sems=DMA((2,)),
        )

    def gathered(lead, width):
        return dict(full=VMEM((mpn, lead, width), BF16), sems=DMA((2,)))

    def reduced(terms, width):
        depth = -(-(len(chain.segments) * terms * width // LANE) // 8) * 8
        return dict(stat=VMEM((dpn, depth, LANE), F32), sems=DMA((2,)))

    return dict(
        z1=summed(4 * rows, mid),
        z2=summed(rows, mid),
        u1=summed(rows, mid),
        u2=summed(rows, mid),
        b2=summed(rows, mid),
        b1=summed(rows, mid),
        bx=summed(rows, inner),
        xs=gathered(rows, inner),
        h2=gathered(rows, mid),
        v2=gathered(rows, mid),
        g2=gathered(rows, mid),
        g1=gathered(rows, mid),
        k2=gathered(rows, mid),
        k1=gathered(4 * rows, mid),
        f1=reduced(2, mid),
        f2=reduced(2, mid),
        f3=reduced(2, wide),
        fp=reduced(2, wide),
        f4=reduced(2, mid),
        f5=reduced(2, mid),
        f6=reduced(2, wide),
        r6=reduced(2, wide),
        r5=reduced(2, mid),
        r4=reduced(2, mid),
        r3=reduced(3, wide),
        r2=reduced(2, mid),
        r1=reduced(2, mid),
        n1=VMEM((4, rows, mid), F32),
        sl1=VMEM((4, rows, mid), F32),
        h1=VMEM((4, padded, mid), F32),
        t1=VMEM((rows, 9 * mid), BF16),
        n2=VMEM((rows, mid), F32),
        sl2=VMEM((rows, mid), F32),
        n3=VMEM((rows, wide), F32),
        bypass=VMEM((rows, wide), F32),
        y=VMEM((rows, wide), F32),
        slq=VMEM((rows, wide), F32),
        r=VMEM((rows, wide), BF16),
        n4=VMEM((rows, mid), F32),
        sl4=VMEM((rows, mid), F32),
        v1=VMEM((padded, mid), F32),
        t2=VMEM((rows, 9 * mid), BF16),
        n5=VMEM((rows, mid), F32),
        sl5=VMEM((rows, mid), F32),
        n6=VMEM((rows, wide), F32),
        d2=VMEM((rows, wide), F32),
        du3=VMEM((rows, wide), BF16),
        dz3=VMEM((rows, wide), BF16),
        dzp=VMEM((rows, wide), BF16),
        dt=VMEM((padded, 9 * mid), F32),
        d=VMEM((4, rows, mid), F32),
        back=VMEM((rows, inner), F32),
        gate=VMEM((rows, LANE), F32),
        facm=VMEM((4, 8, mid), F32),
        facw=VMEM((3, 8, wide), F32),
        gm=VMEM((8, mid), F32),
        gw=VMEM((8, wide), F32),
    )


def weight_scratch(weight, mpn):
    return dict(
        full=VMEM((weight.taps, mpn * weight.block, weight.width), BF16),
        fetch=DMA((2,)),
        lift=DMA((2,)),
        hand=DMA((2,)),
        own=DMA((1,)),
    )


def unit_scratch(unit, mpn):
    spread = (mpn, unit.taps, unit.block // 2, unit.width)
    pieces = (unit.ways, mpn, unit.taps, unit.piece, unit.width)
    return dict(
        part=VMEM((mpn, unit.taps, unit.block, unit.width), BF16),
        twin=VMEM(spread, BF16),
        sums=VMEM(pieces, BF16),
        hop=VMEM(pieces, BF16),
        fin=VMEM(pieces, BF16),
        swap=VMEM(pieces, BF16),
        twins=DMA((2,)),
        swaps=DMA((2,)),
        outs=DMA((2,)),
        hop_sent=DMA((2,)),
        hop_came=DMA((2,)),
        mix=DMA((2,)),
        cast_sent=DMA((2,)),
        cast_came=DMA((2,)),
    )


class Body:
    def __init__(self, given, made, scratch, chains, weights, units, sizes):
        self.given = given
        self.made = made
        self.links = scratch.chains
        self.weights = weights
        self.held = scratch.weights
        self.units = units
        self.places = classes(units)[2]
        self.rows = Rows(chains, sizes[1], sizes[2])
        self.sums = scratch.units
        self.chains = chains
        self.mid, self.wide, self.inner, self.dpn, self.mpn = sizes
        self.dp = lax.axis_index("dp")
        self.mp = lax.axis_index("mp")
        self.z = lax.div(self.dp, 2)
        self.core = lax.rem(self.dp, 2)
        self.levels = self.dpn // 2
        across = lax.div(self.mp, 2)
        along = lax.rem(self.mp, 2)
        self.peers = (
            across * 2 + (1 - along),
            (1 - across) * 2 + along,
            (1 - across) * 2 + (1 - along),
        )
        self.twin = self.z * 2 + (1 - self.core)
        self.others = [lax.rem(self.dp + step, self.dpn) for step in range(1, self.dpn)]
        self.stack = [lax.rem(self.z + step, self.levels) for step in range(1, self.levels)]
        self.flying = {}
        self.fetched = set()
        self.lifting = {}
        self.passing = set()
        self.present = set()
        self.background = []

    def barrier(self):
        semaphore = pltpu.get_barrier_semaphore()
        for peer in self.peers:
            pl.semaphore_signal(
                semaphore, inc=1, device_id=(self.dp, peer), device_id_type=MESH_ID
            )
        for other in self.others:
            pl.semaphore_signal(
                semaphore, inc=1, device_id=(other, self.mp), device_id_type=MESH_ID
            )
        pl.semaphore_wait(semaphore, len(self.peers) + len(self.others))

    def remote(self, source, target, sent, came, device):
        return pltpu.make_async_remote_copy(
            src_ref=source,
            dst_ref=target,
            send_sem=sent,
            recv_sem=came,
            device_id=device,
            device_id_type=MESH_ID,
        )


    def settle(self, slab, sems, device):
        copy = self.remote(slab, slab, sems.at[0], sems.at[1], device)
        copy.wait_send()
        copy.wait_recv()

    def scatter(self, link, values):
        width = link.send.shape[2]
        for block in range(self.mpn):
            link.send[block] = values[:, block * width : (block + 1) * width].astype(BF16)
        for step, peer in enumerate(self.peers):
            self.remote(
                link.send.at[peer],
                link.recv.at[step],
                link.sems.at[0],
                link.sems.at[1],
                (self.dp, peer),
            ).start()
        yield
        self.settle(link.recv, link.sems, (self.dp, self.peers[0]))
        total = link.send[self.mp].astype(F32)
        for step in range(self.mpn - 1):
            total = total + link.recv[step].astype(F32)
        return total

    def gather(self, link):
        mine = link.full.at[self.mp]
        for peer in self.peers:
            self.remote(
                mine, mine, link.sems.at[0], link.sems.at[1], (self.dp, peer)
            ).start()
        yield
        slab = link.full.at[pl.ds(0, self.mpn - 1)]
        self.settle(slab, link.sems, (self.dp, self.peers[0]))

    def joined(self, link):
        return jnp.concatenate([link.full[block] for block in range(self.mpn)], axis=1)

    def reduce(self, link, terms):
        stat = link.stat
        depth = stat.shape[1]
        lanes = terms[0].shape[1] // LANE
        lines = [
            term[:, lane * LANE : (lane + 1) * LANE] for term in terms for lane in range(lanes)
        ]
        if depth > len(lines):
            lines.append(jnp.zeros((depth - len(lines), LANE), F32))
        stat[self.dp] = jnp.concatenate(lines, axis=0)
        mine = stat.at[self.dp]
        for other in self.others:
            self.remote(
                mine, mine, link.sems.at[0], link.sems.at[1], (other, self.mp)
            ).start()
        yield
        slab = stat.at[pl.ds(0, self.dpn - 1)]
        self.settle(slab, link.sems, (self.others[0], self.mp))
        total = stat[0]
        for source in range(1, self.dpn):
            total = total + stat[source]
        rows = []
        for index in range(len(terms)):
            first = index * lanes
            pieces = [total[first + lane : first + lane + 1] for lane in range(lanes)]
            rows.append(pieces[0] if lanes == 1 else jnp.concatenate(pieces, axis=1))
        return rows


    def half(self, block, first, core):
        return pl.ds(pl.multiple_of(first + core * (block // 2), 16), block // 2)

    def eighth(self, block, first, core, level):
        size = block // (2 * self.levels)
        return pl.ds(pl.multiple_of(first + core * (block // 2) + level * size, 16), size)

    def shared(self, tensor):
        return tensor != TENSOR_Q1

    def mine(self, tensor, first):
        block = self.weights[tensor].block
        if self.shared(tensor):
            return self.eighth(block, first, self.core, self.z)
        return self.half(block, first, self.core)

    def weight_start(self, tensor):
        weight = self.weights[tensor]
        held = self.held[tensor]
        source = self.given.weights[tensor]
        block, width = weight.block, weight.width

        def columns(device):
            return pl.ds(pl.multiple_of(device * width, LANE), width)

        for peer in self.peers:
            self.remote(
                source.at[:, self.mine(tensor, 0), columns(peer)],
                held.full.at[:, self.mine(tensor, self.mp * block), :],
                held.fetch.at[0],
                held.fetch.at[1],
                (self.dp, peer),
            ).start()
        own = pltpu.make_async_copy(
            source.at[:, :, columns(self.mp)],
            held.full.at[:, pl.ds(pl.multiple_of(self.mp * block, 16), block), :],
            held.own.at[0],
        )
        own.start()
        self.flying[tensor] = own

    def slab(self, tensor, rows):
        return self.held[tensor].full.at[:, pl.ds(0, rows), :]

    def weight_fetched(self, tensor):
        if tensor in self.fetched:
            return
        block = self.weights[tensor].block
        rows = block // (2 * self.levels) if self.shared(tensor) else block // 2
        held = self.held[tensor]
        slab = self.slab(tensor, len(self.peers) * rows)
        self.settle(slab, held.fetch, (self.dp, self.peers[0]))
        self.flying[tensor].wait()
        self.fetched.add(tensor)

    def weight_lift(self, tensor, steps=(0, 1, 2)):
        self.weight_fetched(tensor)
        block = self.weights[tensor].block
        held = self.held[tensor]
        for step in steps:
            came = held.full.at[:, self.mine(tensor, self.peers[step] * block), :]
            for level in self.stack:
                self.remote(
                    came,
                    came,
                    held.lift.at[0],
                    held.lift.at[1],
                    (level * 2 + self.core, self.mp),
                ).start()
        self.lifting[tensor] = self.lifting.get(tensor, ()) + tuple(steps)

    def weight_pass(self, tensor):
        if tensor in self.passing:
            return
        self.passing.add(tensor)
        self.weight_fetched(tensor)
        block = self.weights[tensor].block
        held = self.held[tensor]
        if self.shared(tensor):
            rest = [step for step in range(3) if step not in self.lifting.get(tensor, ())]
            if rest:
                self.weight_lift(tensor, rest)
            rows = block // (2 * self.levels) * len(self.peers) * len(self.stack)
            slab = self.slab(tensor, rows)
            self.settle(slab, held.lift, (self.stack[0] * 2 + self.core, self.mp))
        for peer in self.peers:
            came = held.full.at[:, self.half(block, peer * block, self.core), :]
            self.remote(
                came, came, held.hand.at[0], held.hand.at[1], (self.twin, self.mp)
            ).start()

    def weight(self, tensor):
        held = self.held[tensor]
        weight = self.weights[tensor]
        if tensor not in self.present:
            self.weight_pass(tensor)
            slab = self.slab(tensor, len(self.peers) * (weight.block // 2))
            self.settle(slab, held.hand, (self.twin, self.mp))
            self.present.add(tensor)
        if weight.taps == 1:
            return held.full[0]
        return jnp.concatenate([held.full[tap] for tap in range(weight.taps)], axis=1)


    def keep(self, segment, values):
        if segment.real == segment.size:
            return values
        rows = lax.broadcasted_iota(jnp.int32, values.shape, values.ndim - 2)
        return jnp.where(rows < segment.real, values, 0.0)

    def factors(self, sums, squares, count):
        centre = sums / count
        spread = squares / count - centre * centre
        return centre, lax.rsqrt(spread + EPSILON)

    def sum_rows(self, values):
        return jnp.sum(values.reshape(-1, values.shape[-1]), axis=0, keepdims=True)

    def moments(self, chain, values):
        terms = []
        for segment in chain.segments:
            part = values[..., segment.start : segment.stop, :]
            terms.append(self.sum_rows(part))
            terms.append(self.sum_rows(part * part))
        return terms

    def mid_row(self, norm, what):
        return self.given.mids[norm * 2 + what][...].reshape(1, self.mid)

    def wide_row(self, norm, what):
        return self.given.wides[norm * 2 + what][...].reshape(1, self.wide)

    def width_mask(self, group):
        limit = lax.div(self.mid * self.mpn * (2 + self.given.widths[group]), 4)
        index = lax.broadcasted_iota(jnp.int32, (1, self.mid), 1) + self.mp * self.mid
        return (index < limit).astype(F32)

    def narrow_norm(self, chain, link, norm, values, totals, normed_ref, slope_ref, store):
        gain = self.mid_row(norm, 0)
        offset = self.mid_row(norm, 1)
        for index, segment in enumerate(chain.segments):
            rows = slice(segment.start, segment.stop)
            count = segment.count * (4 if norm == NORM_Q1 else 1)
            centre, factor = self.factors(totals[2 * index], totals[2 * index + 1], count)
            link.facm[norm, index : index + 1, :] = factor
            mask = self.width_mask(segment.group)
            normed = (values[..., rows, :] - centre) * factor
            normed_ref[..., rows, :] = normed
            affine = normed * gain + offset
            logistic = jax.nn.sigmoid(affine)
            slope_ref[..., rows, :] = mask * (logistic * (1.0 + affine * (1.0 - logistic)))
            store(segment, self.keep(segment, mask * (affine * logistic)).astype(BF16))

    def narrow_terms(self, chain, gradients, normed_ref):
        terms = []
        for segment in chain.segments:
            rows = slice(segment.start, segment.stop)
            part = gradients[..., rows, :]
            terms.append(self.sum_rows(part))
            terms.append(self.sum_rows(part * normed_ref[..., rows, :]))
        return terms

    def narrow_back(self, chain, link, norm, gradients_ref, totals, normed_ref, store):
        gain = self.mid_row(norm, 0)
        gain_total = None
        offset_total = None
        for index, segment in enumerate(chain.segments):
            rows = slice(segment.start, segment.stop)
            count = segment.count * (4 if norm == NORM_Q1 else 1)
            factor = link.facm[norm, index : index + 1, :]
            first, second = totals[2 * index], totals[2 * index + 1]
            gain_total = second if gain_total is None else gain_total + second
            offset_total = first if offset_total is None else offset_total + first
            change = (gain * factor) * (
                gradients_ref[..., rows, :]
                - first / count
                - normed_ref[..., rows, :] * (second / count)
            )
            store(segment, self.keep(segment, change).astype(BF16))
        link.gm[2 * norm : 2 * norm + 1, :] = gain_total
        link.gm[2 * norm + 1 : 2 * norm + 2, :] = offset_total


    def edge(self, edges, start, size, down, right):
        mask = None
        for shift, first in ((down, 0), (right, 2)):
            if shift == 0:
                continue
            values = edges[first + (0 if shift < 0 else 1), start : start + size, :]
            mask = values if mask is None else mask * values
        return mask

    def tap_list(self, stride):
        taps = []
        for vertical in range(3):
            for lateral in range(3):
                if stride == 2:
                    plane = 2 * (vertical != 1) + (lateral != 1)
                    taps.append((plane, -(vertical == 0), -(lateral == 0)))
                else:
                    taps.append((0, vertical - 1, lateral - 1))
        return taps

    def collect(self, chain, stride, padded, edges, taps_ref):
        mid = self.mid
        for position, (plane, down, right) in enumerate(self.tap_list(stride)):
            for index, segment in enumerate(chain.segments):
                shift = down * segment.down + right * segment.right
                base = GUARD + segment.start
                rows = slice(base + shift, base + shift + segment.size)
                values = padded[plane, rows, :] if stride == 2 else padded[rows, :]
                mask = self.edge(edges.at[index], base, segment.size, down, right)
                if mask is not None:
                    values = values * mask
                taps_ref[
                    segment.start : segment.stop, position * mid : (position + 1) * mid
                ] = values.astype(BF16)

    def spread(self, chain, stride, columns, edges):
        mid = self.mid
        taps = self.tap_list(stride)
        results = []
        for index, segment in enumerate(chain.segments):
            base = GUARD + segment.start
            for plane in range(4 if stride == 2 else 1):
                total = None
                for position, (where, down, right) in enumerate(taps):
                    if where != plane:
                        continue
                    start = base - (down * segment.down + right * segment.right)
                    values = columns[
                        start : start + segment.size, position * mid : (position + 1) * mid
                    ]
                    mask = self.edge(edges.at[index], start, segment.size, down, right)
                    if mask is not None:
                        values = values * mask
                    total = values if total is None else total + values
                results.append((segment, plane, self.keep(segment, total)))
        return results


    def clear(self, chain, link):
        rows = chain.rows
        for array in (link.h1, link.v1, link.dt):
            blank = jnp.zeros(array.shape[:-2] + (GUARD, array.shape[-1]), array.dtype)
            array[..., 0:GUARD, :] = blank
            array[..., GUARD + rows : 2 * GUARD + rows, :] = blank
        link.gm[...] = jnp.zeros_like(link.gm)
        link.gw[...] = jnp.zeros_like(link.gw)
        for segment in chain.segments:
            flags = [
                self.given.gates[segment.group][image].astype(F32)
                for image in range(segment.images)
            ]
            area = segment.side * segment.side
            link.gate[segment.start : segment.stop, :] = jnp.zeros((segment.size, LANE), F32)
            if segment.inside:
                rows = lax.broadcasted_iota(jnp.int32, (segment.size, LANE), 0)
                place = lax.rem(rows, segment.images)
                total = jnp.zeros((segment.size, LANE), F32)
                for image, flag in enumerate(flags):
                    total = jnp.where(place == image, flag, total)
                link.gate[segment.start : segment.stop, :] = total
            else:
                for image, flag in enumerate(flags):
                    start = segment.start + image * area
                    link.gate[start : start + area, :] = jnp.full((area, LANE), flag, F32)

    def gates(self, link, rows):
        return jnp.concatenate([link.gate[rows, :]] * (self.wide // LANE), axis=1)

    def bypass(self, chain, link, pixels):
        link.xs.full[self.mp] = pixels[0]
        yield from self.gather(link.xs)
        product = nn(self.joined(link.xs), self.weight(TENSOR_SC))
        link.bypass[...] = product
        totals = yield from self.reduce(link.fp, self.moments(chain, product))
        for index, segment in enumerate(chain.segments):
            rows = slice(segment.start, segment.stop)
            centre, factor = self.factors(
                totals[2 * index], totals[2 * index + 1], segment.count
            )
            link.facw[NORM_SC, index : index + 1, :] = factor
            link.bypass[rows, :] = (link.bypass[rows, :] - centre) * factor

    def chain(self, chain, link, given, place):
        rows = chain.rows
        start = self.rows.start[place]
        mid = self.mid

        def into(full):
            def store(segment, values):
                full[self.mp, segment.start : segment.stop, :] = values

            return store

        pixels = given.pixels[...].reshape(4 * rows, self.inner)
        total = yield from self.scatter(link.z1, nt(pixels, self.weight(TENSOR_Q1)))
        total = total.reshape(4, rows, mid)
        link.n1[...] = total
        totals = yield from self.reduce(link.f1, self.moments(chain, total))

        def store_one(segment, values):
            start = GUARD + segment.start
            link.h1[:, start : start + segment.size, :] = values.astype(F32)

        self.narrow_norm(chain, link, NORM_Q1, link.n1, totals, link.n1, link.sl1, store_one)
        self.collect(chain, 2, link.h1, given.edges, link.t1)
        total = yield from self.scatter(link.z2, nt(link.t1[...], self.weight(TENSOR_S1)))
        link.n2[...] = total
        totals = yield from self.reduce(link.f2, self.moments(chain, total))
        self.narrow_norm(
            chain, link, NORM_S1, link.n2, totals, link.n2, link.sl2, into(link.h2.full)
        )
        yield from self.gather(link.h2)
        product = nn(self.joined(link.h2), self.weight(TENSOR_E1))
        link.n3[...] = product
        totals = yield from self.reduce(link.f3, self.moments(chain, product))
        for index, segment in enumerate(chain.segments):
            span = slice(segment.start, segment.stop)
            centre, factor = self.factors(
                totals[2 * index], totals[2 * index + 1], segment.count
            )
            link.facw[NORM_E1, index : index + 1, :] = factor
            normed = (link.n3[span, :] - centre) * factor
            link.n3[span, :] = normed
            joint = (normed * self.wide_row(NORM_E1, 0) + self.wide_row(NORM_E1, 1)) + (
                link.bypass[span, :] * self.wide_row(NORM_SC, 0) + self.wide_row(NORM_SC, 1)
            )
            logistic = jax.nn.sigmoid(joint)
            link.slq[span, :] = logistic * (1.0 + joint * (1.0 - logistic))
            widened = joint * logistic
            link.y[span, :] = widened
            link.r[span, :] = self.keep(segment, widened).astype(BF16)

        total = yield from self.scatter(link.u1, nt(link.r[...], self.weight(TENSOR_Q2)))
        link.n4[...] = total
        totals = yield from self.reduce(link.f4, self.moments(chain, total))

        def store_four(segment, values):
            start = GUARD + segment.start
            link.v1[start : start + segment.size, :] = values.astype(F32)

        self.narrow_norm(chain, link, NORM_Q2, link.n4, totals, link.n4, link.sl4, store_four)
        self.collect(chain, 1, link.v1, given.edges, link.t2)
        total = yield from self.scatter(link.u2, nt(link.t2[...], self.weight(TENSOR_S2)))
        link.n5[...] = total
        totals = yield from self.reduce(link.f5, self.moments(chain, total))
        self.narrow_norm(
            chain, link, NORM_S2, link.n5, totals, link.n5, link.sl5, into(link.v2.full)
        )
        yield from self.gather(link.v2)
        product = nn(self.joined(link.v2), self.weight(TENSOR_E2))
        link.n6[...] = product
        totals = yield from self.reduce(link.f6, self.moments(chain, product))

        terms = []
        for index, segment in enumerate(chain.segments):
            span = slice(segment.start, segment.stop)
            centre, factor = self.factors(
                totals[2 * index], totals[2 * index + 1], segment.count
            )
            link.facw[NORM_E2, index : index + 1, :] = factor
            normed = (link.n6[span, :] - centre) * factor
            link.n6[span, :] = normed
            gate = self.gates(link, span)
            final = link.y[span, :] + gate * (
                normed * self.wide_row(NORM_E2, 0) + self.wide_row(NORM_E2, 1)
            )
            logistic = jax.nn.sigmoid(final)
            self.made.rows[start + segment.start : start + segment.stop, :] = final * logistic
            slope = logistic * (1.0 + final * (1.0 - logistic))
            change = slope * given.cotangent[span, :].astype(F32)
            link.d2[span, :] = change
            gated = gate * change
            terms.append(self.sum_rows(gated))
            terms.append(self.sum_rows(gated * normed))
        totals = yield from self.reduce(link.r6, terms)
        gain_total = None
        offset_total = None
        for index, segment in enumerate(chain.segments):
            span = slice(segment.start, segment.stop)
            factor = link.facw[NORM_E2, index : index + 1, :]
            first, second = totals[2 * index], totals[2 * index + 1]
            gain_total = second if gain_total is None else gain_total + second
            offset_total = first if offset_total is None else offset_total + first
            change = (self.wide_row(NORM_E2, 0) * factor) * (
                self.gates(link, span) * link.d2[span, :]
                - first / segment.count
                - link.n6[span, :] * (second / segment.count)
            )
            link.du3[span, :] = self.keep(segment, change).astype(BF16)
        link.gw[4:5, :] = gain_total
        link.gw[5:6, :] = offset_total
        total = yield from self.scatter(link.b2, nt(link.du3[...], self.weight(TENSOR_E2)))
        gradients = total * link.sl5[...]
        link.d[0] = gradients
        totals = yield from self.reduce(link.r5, self.narrow_terms(chain, gradients, link.n5))
        self.narrow_back(
            chain, link, NORM_S2, link.d.at[0], totals, link.n5, into(link.g2.full)
        )
        yield from self.gather(link.g2)
        link.dt[GUARD : GUARD + rows, :] = nn(self.joined(link.g2), self.weight(TENSOR_S2))
        for segment, _, values in self.spread(chain, 1, link.dt, given.edges):
            span = slice(segment.start, segment.stop)
            link.d[0, span, :] = values * link.sl4[span, :]
        totals = yield from self.reduce(
            link.r4, self.narrow_terms(chain, link.d.at[0], link.n4)
        )
        self.narrow_back(
            chain, link, NORM_Q2, link.d.at[0], totals, link.n4, into(link.g1.full)
        )
        yield from self.gather(link.g1)

        link.d2[...] = (
            link.d2[...] + nn(self.joined(link.g1), self.weight(TENSOR_Q2))
        ) * link.slq[...]
        terms = []
        for segment in chain.segments:
            span = slice(segment.start, segment.stop)
            part = link.d2[span, :]
            terms.append(self.sum_rows(part))
            terms.append(self.sum_rows(part * link.n3[span, :]))
            terms.append(self.sum_rows(part * link.bypass[span, :]))
        totals = yield from self.reduce(link.r3, terms)
        sums = [None] * 3
        for index, segment in enumerate(chain.segments):
            span = slice(segment.start, segment.stop)
            part = link.d2[span, :]
            first = totals[3 * index]
            for which in range(3):
                value = totals[3 * index + which]
                sums[which] = value if sums[which] is None else sums[which] + value
            for norm, normed, target in (
                (NORM_E1, link.n3, link.dz3),
                (NORM_SC, link.bypass, link.dzp),
            ):
                factor = link.facw[norm, index : index + 1, :]
                second = totals[3 * index + 1 + norm]
                change = (self.wide_row(norm, 0) * factor) * (
                    part - first / segment.count - normed[span, :] * (second / segment.count)
                )
                target[span, :] = self.keep(segment, change).astype(BF16)
        link.gw[0:1, :] = sums[1]
        link.gw[1:2, :] = sums[0]
        link.gw[2:3, :] = sums[2]
        link.gw[3:4, :] = sums[0]
        total = yield from self.scatter(link.b1, nt(link.dz3[...], self.weight(TENSOR_E1)))
        gradients = total * link.sl2[...]
        link.d[0] = gradients
        totals = yield from self.reduce(link.r2, self.narrow_terms(chain, gradients, link.n2))
        self.narrow_back(
            chain, link, NORM_S1, link.d.at[0], totals, link.n2, into(link.k2.full)
        )
        yield from self.gather(link.k2)
        link.dt[GUARD : GUARD + rows, :] = nn(self.joined(link.k2), self.weight(TENSOR_S1))
        for segment, plane, values in self.spread(chain, 2, link.dt, given.edges):
            span = slice(segment.start, segment.stop)
            link.d[plane, span, :] = values * link.sl1[plane, span, :]
        totals = yield from self.reduce(link.r1, self.narrow_terms(chain, link.d, link.n1))

        def store_back_one(segment, values):
            for plane in range(4):
                start = plane * rows + segment.start
                link.k1.full[self.mp, start : start + segment.size, :] = values[plane]

        self.narrow_back(chain, link, NORM_Q1, link.d, totals, link.n1, store_back_one)
        yield from self.gather(link.k1)
        product = nn(self.joined(link.k1), self.weight(TENSOR_Q1))
        for plane in range(4):
            first, columns = self.rows.plane(place, plane)
            values = product[plane * rows : (plane + 1) * rows, :]
            if plane == 0:
                values = values + link.back[...]
            self.made.rows[first : first + rows, columns] = values

    def bypass_back(self, link):
        product = nt(link.dzp[...], self.weight(TENSOR_SC))
        total = yield from self.scatter(link.bx, product)
        link.back[...] = total


    def unit_product(self, unit):
        total = None
        for link, given in zip(self.links, self.given.chains, strict=True):
            if unit.tensor == TENSOR_Q1:
                pixels = given.pixels[...]
                part = tn(self.joined(link.k1), pixels.reshape(-1, self.inner))
            else:
                left, right = {
                    TENSOR_S1: (link.k2, link.t1),
                    TENSOR_E1: (link.h2, link.dz3),
                    TENSOR_SC: (link.xs, link.dzp),
                    TENSOR_Q2: (link.g1, link.r),
                    TENSOR_S2: (link.g2, link.t2),
                    TENSOR_E2: (link.v2, link.du3),
                }[unit.tensor]
                part = tn(self.joined(left), right[:, unit.columns])
            total = part if total is None else total + part
        return total

    def unit_gradient(self, index):
        unit = self.units[index]
        held = self.sums[index]
        block, width, piece = unit.block, unit.width, unit.piece
        product = self.unit_product(unit).astype(BF16)
        for tap in range(unit.taps):
            columns = product[:, tap * width : (tap + 1) * width]
            held.part[:, tap] = columns.reshape(self.mpn, block, width)
        theirs = self.half(block, 0, 1 - self.core)
        copy = self.remote(
            held.part.at[:, :, theirs, :],
            held.twin,
            held.twins.at[0],
            held.twins.at[1],
            (self.twin, self.mp),
        )
        copy.start()
        yield 1
        copy.wait()
        mine = held.part[:, :, self.half(block, 0, self.core), :]
        both = mine.astype(F32) + held.twin[...].astype(F32)
        for way in range(unit.ways):
            held.sums[way] = both[:, :, way * piece : (way + 1) * piece, :].astype(BF16)
        yield from (self.direct(held) if unit.direct else self.climb(held))
        copy = self.remote(
            held.fin, held.swap, held.swaps.at[0], held.swaps.at[1], (self.twin, self.mp)
        )
        copy.start()
        yield 1
        copy.wait()
        which, place = self.places[index]
        out = self.made.units[which].at[place]
        copies = (
            pltpu.make_async_copy(held.fin, out.at[self.core], held.outs.at[0]),
            pltpu.make_async_copy(held.swap, out.at[1 - self.core], held.outs.at[1]),
        )
        for copy in copies:
            copy.start()
        yield 1
        for copy in copies:
            copy.wait()

    def mix(self, held, way):
        for peer in self.peers:
            self.remote(
                held.sums.at[way, peer],
                held.fin.at[way, self.mp],
                held.mix.at[0],
                held.mix.at[1],
                (self.dp, peer),
            ).start()
        held.fin[way, self.mp] = held.sums[way, self.mp]

    def mixed(self, held, way):
        slab = held.fin.at[way, pl.ds(0, len(self.peers))]
        self.settle(slab, held.mix, (self.dp, self.peers[0]))

    def direct(self, held):
        def above(level):
            return (level * 2 + self.core, self.mp)

        first = above(self.stack[0])
        others = pl.ds(0, len(self.stack))
        for level in self.stack:
            self.remote(
                held.sums.at[level],
                held.hop.at[self.z],
                held.hop_sent.at[0],
                held.hop_came.at[0],
                above(level),
            ).start()
        yield 2
        slab = held.hop.at[others]
        copy = self.remote(slab, slab, held.hop_sent.at[0], held.hop_came.at[0], first)
        copy.wait_send()
        copy.wait_recv()
        total = held.sums[self.z].astype(F32)
        for level in self.stack:
            total = total + held.hop[level].astype(F32)
        held.sums[self.z] = total.astype(BF16)
        self.mix(held, self.z)
        yield 2
        self.mixed(held, self.z)
        mine = held.fin.at[self.z]
        for level in self.stack:
            self.remote(
                mine, mine, held.cast_sent.at[0], held.cast_came.at[0], above(level)
            ).start()
        yield 2
        slab = held.fin.at[others]
        copy = self.remote(slab, slab, held.cast_sent.at[0], held.cast_came.at[0], first)
        copy.wait_send()
        copy.wait_recv()

    def climb(self, held):
        last = self.levels - 1

        def place(way, step):
            return step if way else last - step

        def onward(way):
            target = self.z + 1 if way else self.z - 1
            return (target * 2 + self.core, self.mp)

        def backward(way):
            target = self.z - 1 if way else self.z + 1
            return (target * 2 + self.core, self.mp)

        def hop(way, device):
            return self.remote(
                held.sums.at[way],
                held.hop.at[way],
                held.hop_sent.at[way],
                held.hop_came.at[way],
                device,
            )

        def cast(way, device):
            slot = held.fin.at[way]
            return self.remote(
                slot, slot, held.cast_sent.at[way], held.cast_came.at[way], device
            )

        for step in range(last + 1):
            for way in (0, 1):

                @pl.when(self.z == place(way, step))
                def _(way=way, step=step):
                    if step > 0:
                        hop(way, backward(way)).wait_recv()
                        total = held.sums[way].astype(F32) + held.hop[way].astype(F32)
                        held.sums[way] = total.astype(BF16)
                    if step < last:
                        hop(way, onward(way)).start()
                    else:
                        self.mix(held, way)

            yield 2
        for step in range(last, -1, -1):
            for way in (0, 1):

                @pl.when(self.z == place(way, step))
                def _(way=way, step=step):
                    if step == last:
                        self.mixed(held, way)
                    else:
                        hop(way, onward(way)).wait_send()
                        cast(way, onward(way)).wait_recv()
                    if step > 0:
                        cast(way, backward(way)).start()

            if step > 0:
                yield 2
        for way in (0, 1):

            @pl.when(self.z != place(way, 0))
            def _(way=way):
                cast(way, backward(way)).wait_send()


    def launch(self, task):
        self.background.append([task, 0])

    def advance(self):
        for entry in list(self.background):
            entry[1] -= 1
            if entry[1] > 0:
                continue
            pause = next(entry[0], self)
            if pause is self:
                self.background.remove(entry)
            else:
                entry[1] = pause or 1

    def run(self):
        self.barrier()
        for tensor in (TENSOR_Q1, TENSOR_S1, TENSOR_E1, TENSOR_SC, TENSOR_Q2):
            self.weight_start(tensor)
        for chain, link in zip(self.chains, self.links, strict=True):
            self.clear(chain, link)
        parts = [
            (chain, link, given, place)
            for place, (chain, link, given) in enumerate(
                zip(self.chains, self.links, self.given.chains, strict=True)
            )
        ]
        tasks = [self.chain(*part) for part in parts]

        def start(tensor):
            return lambda: self.weight_start(tensor)

        def lift(tensor, steps=(0, 1, 2)):
            return lambda: self.weight_lift(tensor, steps)

        def hand(tensor):
            return lambda: self.weight_pass(tensor)

        def grad(tensor, part=0):
            places = [place for place, unit in enumerate(self.units) if unit.tensor == tensor]
            return lambda: self.launch(self.unit_gradient(places[part]))

        def bypass(index):
            chain, link, given, _ = parts[index]
            return lambda: self.launch(self.bypass(chain, link, given.pixels))

        def bypass_back(index):
            return lambda: self.launch(self.bypass_back(self.links[index]))

        events = {
            1: (lift(TENSOR_S1), lift(TENSOR_E1), lift(TENSOR_SC), lift(TENSOR_Q2)),
            2: (bypass(0), start(TENSOR_S2), start(TENSOR_E2), hand(TENSOR_S1)),
            3: (lift(TENSOR_S2, (0, 1)),),
            4: (bypass(1), hand(TENSOR_E1), hand(TENSOR_SC)),
            5: (lift(TENSOR_S2, (2,)),),
            6: (hand(TENSOR_Q2),),
            7: (lift(TENSOR_E2),),
            8: (hand(TENSOR_S2),),
            10: (hand(TENSOR_E2),),
            14: (grad(TENSOR_E2),),
            17: (grad(TENSOR_S2, 0),),
            18: (grad(TENSOR_S2, 1),),
            19: (grad(TENSOR_S2, 2), grad(TENSOR_Q2)),
            20: (grad(TENSOR_E1),),
            21: (bypass_back(0), grad(TENSOR_SC, 0)),
            22: (grad(TENSOR_SC, 1),),
            23: (
                bypass_back(1),
                grad(TENSOR_S1, 0),
                grad(TENSOR_S1, 1),
                grad(TENSOR_S1, 2),
            ),
        }
        slot = 0
        while tasks:
            slot += 1
            for place, task in enumerate(list(tasks)):
                if next(task, self) is self:
                    tasks.remove(task)
                if place == 0:
                    self.advance()
            for event in events.get(slot, ()):
                event()
            self.advance()
            if slot == 24:
                for _ in range(8):
                    self.advance()
        self.launch(self.unit_gradient(len(self.units) - 1))
        self.advance()
        first, second = self.links
        mids, wides = self.rows.mids, self.rows.wides
        self.made.rows[mids : mids + 8, : self.mid] = first.gm[...] + second.gm[...]
        self.made.rows[wides : wides + 8, :] = first.gw[...] + second.gw[...]
        while self.background:
            self.advance()


class Rows:
    def __init__(self, chains, wide, inner):
        self.total = sum(chain.rows for chain in chains)
        self.start = [0]
        for chain in chains:
            self.start.append(self.start[-1] + chain.rows)
        self.mids = 3 * self.total
        self.wides = self.mids + 8
        self.shape = (self.wides + 8, wide)
        self.inner = inner

    def plane(self, place, plane):
        first = (1 + plane // 2) * self.total + self.start[place]
        column = plane % 2 * self.inner
        return first, slice(column, column + self.inner)


def classes(units):
    shapes = []
    counts = []
    places = []
    for unit in units:
        key = (unit.ways, unit.taps, unit.piece, unit.width)
        if key not in shapes:
            shapes.append(key)
            counts.append(0)
        index = shapes.index(key)
        places.append((index, counts[index]))
        counts[index] += 1
    return shapes, counts, places


def kernel_text(trees, chains, weights, units, sizes, *refs):
    given_tree, made_tree, scratch_tree = trees
    given_size = given_tree.num_leaves
    made_size = made_tree.num_leaves
    given = jax.tree.unflatten(given_tree, refs[:given_size])
    made = jax.tree.unflatten(made_tree, refs[given_size : given_size + made_size])
    scratch = jax.tree.unflatten(scratch_tree, refs[given_size + made_size :])
    given = {**given, **dict(chains=[bag(value) for value in given["chains"]])}
    scratch = dict(
        chains=[bag(value) for value in scratch["chains"]],
        weights=[bag(value) for value in scratch["weights"]],
        units=[bag(value) for value in scratch["units"]],
    )
    Body(bag(given), bag(made), bag(scratch), chains, weights, units, sizes).run()


def finish_text(chains, weights, units, sizes, *refs):
    mid, wide, inner, mpn = sizes
    count = len(weights)
    take = iter(refs)
    shapes, _, places = classes(units)
    layout = Rows(chains, wide, inner)
    pieces = [next(take) for _ in shapes]
    rows_in = next(take)
    outs = [next(take) for _ in range(count)]
    groups = [(next(take), next(take)) for _ in range(3)]
    mid_outs = [next(take) for _ in range(8)]
    wide_outs = [next(take) for _ in range(6)]
    near = [next(take) for _ in shapes]
    rows = next(take)
    wided = [next(take) for _ in range(count)]
    woven, came, gone, weave = next(take), next(take), next(take), next(take)
    arrivals = []
    for index, (which, place) in enumerate(places):
        copy = pltpu.make_async_copy(
            pieces[which].at[place], near[which].at[place], came.at[index]
        )
        copy.start()
        arrivals.append(copy)
    last = pltpu.make_async_copy(rows_in, rows, came.at[len(units)])
    last.start()
    leaving = []
    for index, unit in enumerate(units):
        arrivals[index].wait()
        which, place = places[index]
        width, piece = unit.width, unit.piece
        stride = weights[unit.tensor].width
        for core in range(2):
            for way in range(unit.ways):
                first = core * (unit.block // 2) + way * piece
                for source in range(mpn):
                    column = source * stride + unit.first_column
                    for tap in range(unit.taps):
                        wided[unit.tensor][
                            unit.first_tap + tap,
                            first : first + piece,
                            column : column + width,
                        ] = near[which][place, core, way, source, tap].astype(F32)
        if index + 1 == len(units) or units[index + 1].tensor != unit.tensor:
            whole = unit.tensor
            copy = pltpu.make_async_copy(wided[whole], outs[whole], gone.at[whole])
            copy.start()
            leaving.append(copy)
    last.wait()
    for row, out in enumerate(mid_outs):
        out[...] = rows[layout.mids + row, :mid]
    for row, out in enumerate(wide_outs):
        out[...] = rows[layout.wides + row, :]
    for place, chain in enumerate(chains):
        for segment in chain.segments:
            out, back = groups[segment.group]
            side = segment.side
            if segment.inside:
                for i in range(side):
                    for j in range(side):
                        offset = segment.start + i * segment.down + j * segment.right
                        first = layout.start[place] + offset
                        out[i, j] = rows[first : first + segment.images, :]
                        for plane in range(4):
                            first, columns = layout.plane(place, plane)
                            first += offset
                            back[2 * i + plane // 2, 2 * j + plane % 2] = rows[
                                first : first + segment.images, columns
                            ]
                continue
            for image in range(segment.images):
                for i in range(side):
                    offset = segment.start + image * side * side + i * side
                    first = layout.start[place] + offset
                    out[image, i] = rows[first : first + side, :]
                    for plane in range(4):
                        first, columns = layout.plane(place, plane)
                        first += offset
                        for lane in range(inner // LANE):
                            column = columns.start + lane * LANE
                            woven[
                                lane,
                                image,
                                2 * i + plane // 2,
                                pl.ds(plane % 2, side, stride=2),
                                :,
                            ] = rows[first : first + side, column : column + LANE]
            for lane in range(inner // LANE):
                copy = pltpu.make_async_copy(
                    woven.at[lane],
                    back.at[:, :, :, pl.ds(lane * LANE, LANE)],
                    weave.at[lane],
                )
                copy.start()
                leaving.append(copy)
    for copy in leaving:
        copy.wait()


def padded_rows(values, size):
    extra = size - values.shape[-2]
    if extra == 0:
        return values
    widths = [(0, 0)] * (values.ndim - 2) + [(0, extra), (0, 0)]
    return jnp.pad(values, widths)


def planes_of(segment, images):
    side = segment.side
    channels = images.shape[3]
    values = segment.pixel_first(images)
    if segment.inside:
        split = values.reshape(side, 2, side, 2, segment.images, channels)
        split = split.transpose(1, 3, 0, 2, 4, 5)
    else:
        split = values.reshape(segment.images, side, 2, side, 2, channels)
        split = split.transpose(2, 4, 0, 1, 3, 5)
    return padded_rows(split.reshape(4, segment.real, channels), segment.size)


def edge_masks(chain):
    masks = np.zeros((len(chain.segments), 4, chain.padded, LANE), np.float32)
    for place, segment in enumerate(chain.segments):
        index = np.arange(segment.real)
        down = index // segment.down % segment.side
        right = index // segment.right % segment.side
        start = GUARD + segment.start
        last = segment.side - 1
        for which, inside in enumerate((down > 0, down < last, right > 0, right < last)):
            masks[place, which, start : start + segment.real] = inside[:, None]
    return jnp.asarray(masks)


def fused_device(dpn, mpn, *args):
    images, widths, gates, cotangents = args[0:3], args[3], args[4:7], args[7:10]
    q1, s1, e1, sc, q2, s2, e2 = (args[index] for index in (10, 13, 16, 19, 22, 25, 28))
    mids = [args[index] for index in (11, 12, 14, 15, 23, 24, 26, 27)]
    wides = [args[index] for index in (17, 18, 20, 21, 29, 30)]
    mid = q1.shape[0]
    wide = wides[0].shape[0]
    inner = images[0].shape[3]
    shapes = [(values.shape[0], values.shape[1]) for values in images]
    chains = [Chain((2, 0), shapes, dpn), Chain((1,), shapes, dpn)]
    weights = weight_table(mid, wide, inner)
    units = unit_table(weights)
    sizes = (mid, wide, inner, dpn, mpn)
    vmem = pl.BlockSpec(memory_space=VMEM)
    smem = pl.BlockSpec(memory_space=pltpu.SMEM)
    anywhere = pl.BlockSpec(memory_space=pl.ANY)
    hbm = pl.BlockSpec(memory_space=pltpu.HBM)

    def by_tap(spatial):
        return spatial.transpose(1, 2, 0, 3).reshape(9, mid, mpn * mid)

    def rows_of(chain, build):
        return jnp.concatenate([build(s) for s in chain.segments], axis=-2)

    given = dict(
        chains=[
            dict(
                pixels=rows_of(chain, lambda s: planes_of(s, images[s.group])),
                cotangent=rows_of(
                    chain,
                    lambda s: padded_rows(
                        s.pixel_first(cotangents[s.group]).reshape(s.real, wide), s.size
                    ),
                ),
                edges=edge_masks(chain),
            )
            for chain in chains
        ],
        mids=mids,
        wides=wides,
        widths=widths,
        gates=list(gates),
        weights=[q1[None], by_tap(s1), e1[None], sc[None], q2[None], by_tap(s2), e2[None]],
    )
    given_specs = dict(
        chains=[dict(pixels=vmem, cotangent=vmem, edges=vmem) for _ in chains],
        mids=[vmem] * len(mids),
        wides=[vmem] * len(wides),
        widths=smem,
        gates=[smem] * 3,
        weights=[anywhere] * WEIGHTS,
    )
    shape = jax.ShapeDtypeStruct
    layout = Rows(chains, wide, inner)
    unit_shapes, unit_counts, _ = classes(units)
    made = dict(
        rows=shape(layout.shape, F32),
        units=[
            shape((count, 2, ways, mpn, *rest), BF16)
            for count, (ways, *rest) in zip(unit_counts, unit_shapes, strict=True)
        ],
    )
    made_specs = dict(rows=vmem, units=[anywhere] * len(unit_shapes))
    scratch = dict(
        chains=[chain_scratch(chain, mid, wide, inner, dpn, mpn) for chain in chains],
        weights=[weight_scratch(weight, mpn) for weight in weights],
        units=[unit_scratch(unit, mpn) for unit in units],
    )
    trees = tuple(jax.tree.structure(tree) for tree in (given_specs, made_specs, scratch))
    results = pl.pallas_call(
        functools.partial(kernel_text, trees, chains, weights, units, sizes),
        out_shape=jax.tree.leaves(made),
        in_specs=jax.tree.leaves(given_specs),
        out_specs=jax.tree.leaves(made_specs),
        scratch_shapes=jax.tree.leaves(scratch),
        compiler_params=pltpu.CompilerParams(
            collective_id=0, has_side_effects=True, vmem_limit_bytes=62 * 2**20
        ),
        name="bottlenecks",
    )(*jax.tree.leaves(given))
    got = bag(jax.tree.unflatten(trees[1], results))

    final_shapes = [shape((w.taps, w.block, mpn * w.width), F32) for w in weights]
    segments = sorted((s for chain in chains for s in chain.segments), key=lambda s: s.group)

    def laid(s, side, channels):
        if s.inside:
            return shape((side, side, s.images, channels), F32)
        return shape((s.images, side, side, channels), F32)

    group_shapes = []
    for s in segments:
        group_shapes += [laid(s, s.side, wide), laid(s, 2 * s.side, inner)]
    woven = [laid(s, 2 * s.side, inner) for s in segments if not s.inside]
    vector_shapes = [shape((mid,), F32)] * 8 + [shape((wide,), F32)] * 6
    final = pl.pallas_call(
        functools.partial(finish_text, chains, weights, units, (mid, wide, inner, mpn)),
        out_shape=final_shapes + group_shapes + vector_shapes,
        in_specs=[hbm] * (len(unit_shapes) + 1),
        out_specs=[hbm] * WEIGHTS
        + [spec for s in segments for spec in (vmem, vmem if s.inside else hbm)]
        + [vmem] * len(vector_shapes),
        scratch_shapes=[VMEM(value.shape, BF16) for value in made["units"]]
        + [VMEM(layout.shape, F32)]
        + [VMEM(value.shape, F32) for value in final_shapes]
        + [VMEM((inner // LANE, *woven[0].shape[:3], LANE), F32)]
        + [DMA((len(units) + 1,)), DMA((WEIGHTS,)), DMA((inner // LANE,))],
        compiler_params=pltpu.CompilerParams(vmem_limit_bytes=48 * 2**20),
        name="finish",
    )(*got.units, got.rows)
    tensors = final[:WEIGHTS]
    grads = [value[0] for value in tensors]
    for place in (TENSOR_S1, TENSOR_S2):
        split = tensors[place].reshape(3, 3, mid, mpn * mid)
        grads[place] = split.transpose(2, 0, 1, 3)
    laid_out = final[WEIGHTS : WEIGHTS + 6]
    outputs = [s.image_first(laid_out[2 * s.group]) for s in segments]
    input_grads = [s.image_first(laid_out[2 * s.group + 1]) for s in segments]
    gm = final[WEIGHTS + 6 : WEIGHTS + 14]
    gw = final[WEIGHTS + 14 :]
    return (
        *outputs,
        *input_grads,
        grads[TENSOR_Q1],
        gm[0],
        gm[1],
        grads[TENSOR_S1],
        gm[2],
        gm[3],
        grads[TENSOR_E1],
        gw[0],
        gw[1],
        grads[TENSOR_SC],
        gw[2],
        gw[3],
        grads[TENSOR_Q2],
        gm[4],
        gm[5],
        grads[TENSOR_S2],
        gm[6],
        gm[7],
        grads[TENSOR_E2],
        gw[4],
        gw[5],
    )


def fits_kernel(mesh, args):
    mid = args[10].shape[0]
    inner = args[0].shape[3]
    wide = args[17].shape[0]
    return (
        mesh.shape["mp"] == 4
        and mesh.shape["dp"] == 8
        and mid == LANE
        and inner % LANE == 0
        and wide == 2 * inner
    )


def per_device(mesh, *args):
    if fits_kernel(mesh, args):
        return fused_device(mesh.shape["dp"], mesh.shape["mp"], *args)
    return on_device(*args)


def solution(mesh):
    in_specs = (
        P("dp", None, None, "mp"),
        P("dp", None, None, "mp"),
        P("dp", None, None, "mp"),
        P(),
        P("dp"),
        P("dp"),
        P("dp"),
        P("dp", None, None, "mp"),
        P("dp", None, None, "mp"),
        P("dp", None, None, "mp"),
        P("mp", None),
        P("mp"),
        P("mp"),
        P("mp", None, None, None),
        P("mp"),
        P("mp"),
        P("mp", None),
        P("mp"),
        P("mp"),
        P("mp", None),
        P("mp"),
        P("mp"),
        P("mp", None),
        P("mp"),
        P("mp"),
        P("mp", None, None, None),
        P("mp"),
        P("mp"),
        P("mp", None),
        P("mp"),
        P("mp"),
    )
    out_specs = (
        P("dp", None, None, "mp"),
        P("dp", None, None, "mp"),
        P("dp", None, None, "mp"),
        P("dp", None, None, "mp"),
        P("dp", None, None, "mp"),
        P("dp", None, None, "mp"),
        P("mp", None),
        P("mp"),
        P("mp"),
        P("mp", None, None, None),
        P("mp"),
        P("mp"),
        P("mp", None),
        P("mp"),
        P("mp"),
        P("mp", None),
        P("mp"),
        P("mp"),
        P("mp", None),
        P("mp"),
        P("mp"),
        P("mp", None, None, None),
        P("mp"),
        P("mp"),
        P("mp", None),
        P("mp"),
        P("mp"),
    )
    return jax.shard_map(
        functools.partial(per_device, mesh),
        mesh=mesh,
        in_specs=in_specs,
        out_specs=out_specs,
        check_vma=False,
    )
```

```python
import functools
import types

import jax
import jax.numpy as jnp
import numpy as np
from jax import lax
from jax.experimental import pallas as pl
from jax.experimental.pallas import tpu as pltpu
from jax.sharding import PartitionSpec as P

EPSILON = 1e-05


def sigmoid_linear(values):
    return values * jax.nn.sigmoid(values)


def sigmoid_slope(values):
    logistic = jax.nn.sigmoid(values)
    return logistic * (1.0 + values * (1.0 - logistic))


def pointwise(hidden, weight):
    return jnp.einsum("nhwc,cd->nhwd", hidden, weight, preferred_element_type=jnp.float32)


def back_pointwise(gradients, weight):
    return jnp.einsum("nhwd,cd->nhwc", gradients, weight, preferred_element_type=jnp.float32)


def weight_term(activations, gradients):
    return jnp.einsum("nhwc,nhwd->cd", activations, gradients, preferred_element_type=jnp.float32)


def reduce_pointwise(hidden, weight):
    return jnp.einsum("nhwc,dc->nhwd", hidden, weight, preferred_element_type=jnp.float32)


def reduce_back(gradients, weight):
    return jnp.einsum("nhwd,dc->nhwc", gradients, weight, preferred_element_type=jnp.float32)


def reduce_term(gradients, activations):
    return jnp.einsum("nhwd,nhwc->dc", gradients, activations, preferred_element_type=jnp.float32)


def gather_taps(hidden, stride):
    extent = hidden.shape[1] // stride
    span_end = stride * (extent - 1) + 1
    padded = jnp.pad(hidden, ((0, 0), (1, 1), (1, 1), (0, 0)))
    pieces = [
        padded[:, vertical : vertical + span_end : stride, lateral : lateral + span_end : stride, :]
        for vertical in range(3)
        for lateral in range(3)
    ]
    return jnp.concatenate(pieces, axis=3)


def spread_taps(columns, stride, edge_size, channels):
    extent = columns.shape[1]
    span_end = stride * (extent - 1) + 1
    padded = jnp.zeros((columns.shape[0], edge_size + 2, edge_size + 2, channels), jnp.float32)
    for position in range(9):
        vertical = position // 3
        lateral = position % 3
        padded = padded.at[
            :, vertical : vertical + span_end : stride, lateral : lateral + span_end : stride, :
        ].add(columns[..., position * channels : (position + 1) * channels])
    return padded[:, 1:-1, 1:-1, :]


def stat_terms(values):
    return jnp.stack([jnp.sum(values, axis=(0, 1, 2)), jnp.sum(values * values, axis=(0, 1, 2))])


def grad_terms(gradients, normed):
    return jnp.stack(
        [jnp.sum(gradients, axis=(0, 1, 2)), jnp.sum(gradients * normed, axis=(0, 1, 2))]
    )


def samples_of(values):
    return values.shape[0] * values.shape[1] * values.shape[2] * lax.axis_size("dp")


def norm_apply(values, totals, samples, norm_gain, offset):
    centre = totals[0] / samples
    spread = totals[1] / samples - centre * centre
    factor = lax.rsqrt(spread + EPSILON)
    normed = (values - centre) * factor
    return (normed, factor, normed * norm_gain + offset)


def norm_back(gradients, normed, factor, totals, samples, norm_gain):
    return norm_gain * factor * (gradients - totals[0] / samples - normed * (totals[1] / samples))


def forward_totals(partials):
    return lax.psum(jnp.stack(partials), "dp")


def backward_totals(partials):
    return lax.psum(jnp.stack(partials), "dp")


def gather_channels(pieces):
    return (
        lax.all_gather(pieces[0], "mp", axis=3, tiled=True),
        lax.all_gather(pieces[1], "mp", axis=3, tiled=True),
        lax.all_gather(pieces[2], "mp", axis=3, tiled=True),
    )


def gather_hidden(pieces):
    return (
        lax.all_gather(pieces[0], "mp", axis=3, tiled=True),
        lax.all_gather(pieces[1], "mp", axis=3, tiled=True),
        lax.all_gather(pieces[2], "mp", axis=3, tiled=True),
    )


def gather_spatial_grads(pieces):
    return (
        lax.all_gather(pieces[0], "mp", axis=3, tiled=True),
        lax.all_gather(pieces[1], "mp", axis=3, tiled=True),
        lax.all_gather(pieces[2], "mp", axis=3, tiled=True),
    )


def gather_entry_grads(pieces):
    return (
        lax.all_gather(pieces[0], "mp", axis=3, tiled=True),
        lax.all_gather(pieces[1], "mp", axis=3, tiled=True),
        lax.all_gather(pieces[2], "mp", axis=3, tiled=True),
    )


def front_forward(gathered, stride, params, width_masks):
    squeeze, squeeze_gain, squeeze_offset, spatial_conv, spatial_gain, spatial_offset = params
    entry = [reduce_pointwise(values, squeeze) for values in gathered]
    entry_totals = forward_totals([stat_terms(values) for values in entry])
    entry_norm = [
        norm_apply(
            entry[member],
            entry_totals[member],
            samples_of(entry[member]),
            squeeze_gain,
            squeeze_offset,
        )
        for member in range(3)
    ]
    hidden = [
        (width_masks[member] * sigmoid_linear(entry_norm[member][2])).astype(jnp.bfloat16)
        for member in range(3)
    ]
    hidden_full = gather_hidden(hidden)
    taps = [gather_taps(values, stride) for values in hidden_full]
    spatial_rows = spatial_conv.reshape(spatial_conv.shape[0], -1)
    middle = [reduce_pointwise(values, spatial_rows) for values in taps]
    middle_totals = forward_totals([stat_terms(values) for values in middle])
    middle_norm = [
        norm_apply(
            middle[member],
            middle_totals[member],
            samples_of(middle[member]),
            spatial_gain,
            spatial_offset,
        )
        for member in range(3)
    ]
    narrow = [
        (width_masks[member] * sigmoid_linear(middle_norm[member][2])).astype(jnp.bfloat16)
        for member in range(3)
    ]
    return (entry_norm, taps, middle_norm, narrow)


def front_backward(narrow_grads, saved, gathered, stride, params, width_masks, column_weights):
    squeeze, squeeze_gain, squeeze_offset, spatial_conv, spatial_gain, spatial_offset = params
    entry_norm, taps, middle_norm, narrow = saved
    middle_out = [
        narrow_grads[member] * width_masks[member] * sigmoid_slope(middle_norm[member][2])
        for member in range(3)
    ]
    middle_totals = backward_totals(
        [grad_terms(middle_out[member], middle_norm[member][0]) for member in range(3)]
    )
    middle_grads = [
        norm_back(
            middle_out[member],
            middle_norm[member][0],
            middle_norm[member][1],
            middle_totals[member],
            samples_of(middle_out[member]),
            spatial_gain,
        ).astype(jnp.bfloat16)
        for member in range(3)
    ]
    spatial_grad = sum(
        (reduce_term(middle_grads[member], taps[member]) for member in range(3))
    ).reshape(spatial_conv.shape)
    squeeze_cols, spatial_cols = column_weights
    channels = spatial_cols.shape[3]
    spatial_flat = spatial_cols.reshape(spatial_cols.shape[0], -1)
    middle_full = gather_spatial_grads(middle_grads)
    hidden_grads = [
        spread_taps(
            reduce_back(middle_full[member], spatial_flat),
            stride,
            gathered[member].shape[1],
            channels,
        )
        for member in range(3)
    ]
    entry_out = [
        hidden_grads[member] * width_masks[member] * sigmoid_slope(entry_norm[member][2])
        for member in range(3)
    ]
    entry_totals = backward_totals(
        [grad_terms(entry_out[member], entry_norm[member][0]) for member in range(3)]
    )
    entry_grads = [
        norm_back(
            entry_out[member],
            entry_norm[member][0],
            entry_norm[member][1],
            entry_totals[member],
            samples_of(entry_out[member]),
            squeeze_gain,
        ).astype(jnp.bfloat16)
        for member in range(3)
    ]
    squeeze_grad = sum((reduce_term(entry_grads[member], gathered[member]) for member in range(3)))
    entry_full = gather_entry_grads(entry_grads)
    squeeze_flat = squeeze_cols.reshape(squeeze_cols.shape[0], -1)
    input_part = [reduce_back(entry_full[member], squeeze_flat) for member in range(3)]
    gain_grads = (
        jnp.sum(entry_totals[:, 1], axis=0),
        jnp.sum(entry_totals[:, 0], axis=0),
        jnp.sum(middle_totals[:, 1], axis=0),
        jnp.sum(middle_totals[:, 0], axis=0),
    )
    return (input_part, squeeze_grad, spatial_grad, gain_grads)


def tail_forward(narrow, bypass_inputs, expand, shortcut):
    partials = []
    for member in range(3):
        pieces = [pointwise(narrow[member], expand)]
        if shortcut is not None:
            pieces.append(pointwise(bypass_inputs[member], shortcut))
        partials.append(jnp.stack(pieces))
    partials = (
        lax.psum_scatter(
            partials[0].astype(jnp.bfloat16), "mp", scatter_dimension=4, tiled=True
        ).astype(jnp.float32),
        lax.psum_scatter(
            partials[1].astype(jnp.bfloat16), "mp", scatter_dimension=4, tiled=True
        ).astype(jnp.float32),
        lax.psum_scatter(
            partials[2].astype(jnp.bfloat16), "mp", scatter_dimension=4, tiled=True
        ).astype(jnp.float32),
    )
    return (partials, narrow)


def tail_backward(gradients, sources, bypass_inputs, expand, shortcut):
    arriving = (
        lax.all_gather(gradients[0], "mp", axis=4, tiled=True),
        lax.all_gather(gradients[1], "mp", axis=4, tiled=True),
        lax.all_gather(gradients[2], "mp", axis=4, tiled=True),
    )
    expand_grad = sum((weight_term(sources[member], arriving[member][0]) for member in range(3)))
    narrow_terms = [back_pointwise(arriving[member][0], expand) for member in range(3)]
    if shortcut is None:
        return (narrow_terms, expand_grad, None, None)
    shortcut_grad = sum(
        (weight_term(bypass_inputs[member], arriving[member][1]) for member in range(3))
    )
    bypass_terms = [back_pointwise(arriving[member][1], shortcut) for member in range(3)]
    return (narrow_terms, expand_grad, shortcut_grad, bypass_terms)


def on_device(
    images_small,
    images_medium,
    images_large,
    width_choice,
    gates_small,
    gates_medium,
    gates_large,
    cotangent_small,
    cotangent_medium,
    cotangent_large,
    squeeze_one,
    squeeze_gain_one,
    squeeze_offset_one,
    spatial_one,
    spatial_gain_one,
    spatial_offset_one,
    expand_one,
    expand_gain_one,
    expand_offset_one,
    shortcut_one,
    shortcut_gain,
    shortcut_offset,
    squeeze_two,
    squeeze_gain_two,
    squeeze_offset_two,
    spatial_two,
    spatial_gain_two,
    spatial_offset_two,
    expand_two,
    expand_gain_two,
    expand_offset_two,
):
    images = [images_small, images_medium, images_large]
    depth_gates = [
        flags.astype(jnp.float32)[:, None, None, None]
        for flags in (gates_small, gates_medium, gates_large)
    ]
    cotangents = [
        values.astype(jnp.float32)
        for values in (cotangent_small, cotangent_medium, cotangent_large)
    ]
    mid_local = squeeze_one.shape[0]
    channel_index = lax.axis_index("mp") * mid_local + jnp.arange(mid_local, dtype=jnp.int32)
    limits = mid_local * lax.axis_size("mp") * (2 + width_choice) // 4
    width_masks = [(channel_index < limits[member]).astype(jnp.float32) for member in range(3)]
    out_local = expand_gain_one.shape[0]
    params_one = (
        squeeze_one,
        squeeze_gain_one,
        squeeze_offset_one,
        spatial_one,
        spatial_gain_one,
        spatial_offset_one,
    )
    params_two = (
        squeeze_two,
        squeeze_gain_two,
        squeeze_offset_two,
        spatial_two,
        spatial_gain_two,
        spatial_offset_two,
    )
    expand_first, bypass_weight, expand_second = (expand_one, shortcut_one, expand_two)
    squeeze_cols_one, spatial_cols_one, squeeze_cols_two, spatial_cols_two = (
        lax.all_to_all(
            squeeze_one.reshape(mid_local, 1, 1, -1), "mp", split_axis=3, concat_axis=0, tiled=True
        ),
        lax.all_to_all(spatial_one, "mp", split_axis=3, concat_axis=0, tiled=True),
        lax.all_to_all(
            squeeze_two.reshape(mid_local, 1, 1, -1), "mp", split_axis=3, concat_axis=0, tiled=True
        ),
        lax.all_to_all(spatial_two, "mp", split_axis=3, concat_axis=0, tiled=True),
    )
    columns_one = (squeeze_cols_one, spatial_cols_one)
    columns_two = (squeeze_cols_two, spatial_cols_two)
    first_full = gather_channels(images)
    first_saved = front_forward(first_full, 2, params_one, width_masks)
    bypass_inputs = [values[:, ::2, ::2, :] for values in images]
    first_tail, first_sources = tail_forward(
        first_saved[3], bypass_inputs, expand_first, bypass_weight
    )
    first_totals = forward_totals(
        [
            jnp.concatenate(
                [stat_terms(first_tail[member][0]), stat_terms(first_tail[member][1])], axis=1
            )
            for member in range(3)
        ]
    )
    widened_norm = [
        norm_apply(
            first_tail[member][0],
            first_totals[member][:, :out_local],
            samples_of(first_tail[member][0]),
            expand_gain_one,
            expand_offset_one,
        )
        for member in range(3)
    ]
    bypass_norm = [
        norm_apply(
            first_tail[member][1],
            first_totals[member][:, out_local:],
            samples_of(first_tail[member][1]),
            shortcut_gain,
            shortcut_offset,
        )
        for member in range(3)
    ]
    first_sum = [widened_norm[member][2] + bypass_norm[member][2] for member in range(3)]
    block_out = [sigmoid_linear(values) for values in first_sum]
    second_full = gather_channels([values.astype(jnp.bfloat16) for values in block_out])
    second_saved = front_forward(second_full, 1, params_two, width_masks)
    second_tail, second_sources = tail_forward(second_saved[3], None, expand_second, None)
    second_totals = forward_totals([stat_terms(second_tail[member][0]) for member in range(3)])
    final_norm = [
        norm_apply(
            second_tail[member][0],
            second_totals[member],
            samples_of(second_tail[member][0]),
            expand_gain_two,
            expand_offset_two,
        )
        for member in range(3)
    ]
    second_sum = [
        block_out[member] + depth_gates[member] * final_norm[member][2] for member in range(3)
    ]
    results = [sigmoid_linear(values) for values in second_sum]
    second_slope = [sigmoid_slope(second_sum[member]) * cotangents[member] for member in range(3)]
    final_out = [depth_gates[member] * second_slope[member] for member in range(3)]
    final_totals = backward_totals(
        [grad_terms(final_out[member], final_norm[member][0]) for member in range(3)]
    )
    final_grads = [
        norm_back(
            final_out[member],
            final_norm[member][0],
            final_norm[member][1],
            final_totals[member],
            samples_of(final_out[member]),
            expand_gain_two,
        ).astype(jnp.bfloat16)[None]
        for member in range(3)
    ]
    second_result = tail_backward(final_grads, second_sources, None, expand_second, None)
    second_input_part, squeeze_two_grad, spatial_two_grad, second_gain_grads = front_backward(
        second_result[0], second_saved, second_full, 1, params_two, width_masks, columns_two
    )
    expand_two_grad = second_result[1]
    block_grads = [second_slope[member] + second_input_part[member] for member in range(3)]
    first_slope = [sigmoid_slope(first_sum[member]) * block_grads[member] for member in range(3)]
    first_grad_totals = backward_totals(
        [
            jnp.concatenate(
                [
                    grad_terms(first_slope[member], widened_norm[member][0]),
                    grad_terms(first_slope[member], bypass_norm[member][0]),
                ],
                axis=1,
            )
            for member in range(3)
        ]
    )
    tail_grads = [
        jnp.stack(
            [
                norm_back(
                    first_slope[member],
                    widened_norm[member][0],
                    widened_norm[member][1],
                    first_grad_totals[member][:, :out_local],
                    samples_of(first_slope[member]),
                    expand_gain_one,
                ),
                norm_back(
                    first_slope[member],
                    bypass_norm[member][0],
                    bypass_norm[member][1],
                    first_grad_totals[member][:, out_local:],
                    samples_of(first_slope[member]),
                    shortcut_gain,
                ),
            ]
        ).astype(jnp.bfloat16)
        for member in range(3)
    ]
    first_result = tail_backward(
        tail_grads, first_sources, bypass_inputs, expand_first, bypass_weight
    )
    expand_one_grad = first_result[1]
    shortcut_grad = first_result[2]
    bypass_terms = first_result[3]
    first_input_part, squeeze_one_grad, spatial_one_grad, first_gain_grads = front_backward(
        first_result[0], first_saved, first_full, 2, params_one, width_masks, columns_one
    )
    input_grads = [
        first_input_part[member].at[:, ::2, ::2, :].add(bypass_terms[member]) for member in range(3)
    ]
    summed = (
        lax.psum(squeeze_one_grad.astype(jnp.bfloat16), "dp").astype(jnp.float32),
        lax.psum(spatial_one_grad.astype(jnp.bfloat16), "dp").astype(jnp.float32),
        lax.psum(expand_one_grad.astype(jnp.bfloat16), "dp").astype(jnp.float32),
        lax.psum(shortcut_grad.astype(jnp.bfloat16), "dp").astype(jnp.float32),
        lax.psum(squeeze_two_grad.astype(jnp.bfloat16), "dp").astype(jnp.float32),
        lax.psum(spatial_two_grad.astype(jnp.bfloat16), "dp").astype(jnp.float32),
        lax.psum(expand_two_grad.astype(jnp.bfloat16), "dp").astype(jnp.float32),
    )
    expand_gain_one_grad = jnp.sum(first_grad_totals[:, 1, :out_local], axis=0)
    expand_offset_one_grad = jnp.sum(first_grad_totals[:, 0, :out_local], axis=0)
    shortcut_gain_grad = jnp.sum(first_grad_totals[:, 1, out_local:], axis=0)
    shortcut_offset_grad = jnp.sum(first_grad_totals[:, 0, out_local:], axis=0)
    expand_gain_two_grad = jnp.sum(final_totals[:, 1], axis=0)
    expand_offset_two_grad = jnp.sum(final_totals[:, 0], axis=0)
    return (
        results[0],
        results[1],
        results[2],
        input_grads[0],
        input_grads[1],
        input_grads[2],
        summed[0],
        first_gain_grads[0],
        first_gain_grads[1],
        summed[1],
        first_gain_grads[2],
        first_gain_grads[3],
        summed[2],
        expand_gain_one_grad,
        expand_offset_one_grad,
        summed[3],
        shortcut_gain_grad,
        shortcut_offset_grad,
        summed[4],
        second_gain_grads[0],
        second_gain_grads[1],
        summed[5],
        second_gain_grads[2],
        second_gain_grads[3],
        summed[6],
        expand_gain_two_grad,
        expand_offset_two_grad,
    )


LANE = 128
GUARD = 32
MESH_ID = pl.DeviceIdType.MESH
DMA = pltpu.SemaphoreType.DMA
VMEM = pltpu.VMEM
F32 = jnp.float32
BF16 = jnp.bfloat16
WEIGHTS = 7
TENSOR_Q1, TENSOR_S1, TENSOR_E1, TENSOR_SC, TENSOR_Q2, TENSOR_S2, TENSOR_E2 = range(WEIGHTS)
NORM_Q1, NORM_S1, NORM_Q2, NORM_S2 = range(4)
NORM_E1, NORM_SC, NORM_E2 = range(3)


def nn(left, right):
    return lax.dot_general(left, right, (((1,), (0,)), ((), ())), preferred_element_type=F32)


def nt(left, right):
    return lax.dot_general(left, right, (((1,), (1,)), ((), ())), preferred_element_type=F32)


def tn(left, right):
    return lax.dot_general(left, right, (((0,), (0,)), ((), ())), preferred_element_type=F32)


def bag(tree):
    if isinstance(tree, dict):
        return types.SimpleNamespace(**{name: bag(value) for name, value in tree.items()})
    return tree


class Segment:
    def __init__(self, group, start, images, side, replicas):
        self.group = group
        self.side = side
        self.images = images
        self.inside = images <= 4
        self.right = images if self.inside else 1
        self.down = self.right * side
        self.start = start
        self.real = images * side * side
        self.size = -(-self.real // 16) * 16
        self.stop = start + self.size
        self.count = float(self.real * replicas)

    def pixel_first(self, values):
        return values.transpose(1, 2, 0, 3) if self.inside else values

    def image_first(self, values):
        return values.transpose(2, 0, 1, 3) if self.inside else values


class Chain:
    def __init__(self, groups, shapes, replicas):
        self.segments = []
        start = 0
        for group in groups:
            images, side = shapes[group]
            segment = Segment(group, start, images, side // 2, replicas)
            self.segments.append(segment)
            start = segment.stop
        self.rows = start
        self.padded = start + 2 * GUARD


class Weight:
    def __init__(self, block, width, taps):
        self.block = block
        self.width = width
        self.taps = taps


def weight_table(mid, wide, inner):
    return [
        Weight(mid, inner, 1),
        Weight(mid, mid, 9),
        Weight(mid, wide, 1),
        Weight(inner, wide, 1),
        Weight(mid, wide, 1),
        Weight(mid, mid, 9),
        Weight(mid, wide, 1),
    ]


class Unit:
    def __init__(self, tensor, weight, part, parts, direct=False):
        self.tensor = tensor
        self.block = weight.block
        self.taps = weight.taps // parts if weight.taps > 1 else 1
        self.width = weight.width if weight.taps > 1 else weight.width // parts
        self.first_tap = part * self.taps if weight.taps > 1 else 0
        self.first_column = 0 if weight.taps > 1 else part * self.width
        self.span = self.taps * self.width
        self.columns = slice(part * self.span, (part + 1) * self.span)
        self.direct = direct
        self.ways = 4 if direct else 2
        self.piece = weight.block // (2 * self.ways)


def unit_table(weights):
    units = []
    for tensor, parts in (
        (TENSOR_E2, 1),
        (TENSOR_S2, 3),
        (TENSOR_Q2, 1),
        (TENSOR_E1, 1),
        (TENSOR_SC, 2),
        (TENSOR_S1, 3),
        (TENSOR_Q1, 1),
    ):
        for part in range(parts):
            units.append(
                Unit(tensor, weights[tensor], part, parts, direct=tensor == TENSOR_Q1)
            )
    return units


def chain_scratch(chain, mid, wide, inner, dpn, mpn):
    rows = chain.rows
    padded = chain.padded
    near = mpn - 1

    def summed(lead, width):
        return dict(
            send=VMEM((mpn, lead, width), BF16),
            recv=VMEM((near, lead, width), BF16),
            sems=DMA((2,)),
        )

    def gathered(lead, width):
        return dict(full=VMEM((mpn, lead, width), BF16), sems=DMA((2,)))

    def reduced(terms, width):
        depth = -(-(len(chain.segments) * terms * width // LANE) // 8) * 8
        return dict(stat=VMEM((dpn, depth, LANE), F32), sems=DMA((2,)))

    return dict(
        z1=summed(4 * rows, mid),
        z2=summed(rows, mid),
        u1=summed(rows, mid),
        u2=summed(rows, mid),
        b2=summed(rows, mid),
        b1=summed(rows, mid),
        bx=summed(rows, inner),
        xs=gathered(rows, inner),
        h2=gathered(rows, mid),
        v2=gathered(rows, mid),
        g2=gathered(rows, mid),
        g1=gathered(rows, mid),
        k2=gathered(rows, mid),
        k1=gathered(4 * rows, mid),
        f1=reduced(2, mid),
        f2=reduced(2, mid),
        f3=reduced(2, wide),
        fp=reduced(2, wide),
        f4=reduced(2, mid),
        f5=reduced(2, mid),
        f6=reduced(2, wide),
        r6=reduced(2, wide),
        r5=reduced(2, mid),
        r4=reduced(2, mid),
        r3=reduced(3, wide),
        r2=reduced(2, mid),
        r1=reduced(2, mid),
        n1=VMEM((4, rows, mid), F32),
        sl1=VMEM((4, rows, mid), F32),
        h1=VMEM((4, padded, mid), F32),
        t1=VMEM((rows, 9 * mid), BF16),
        n2=VMEM((rows, mid), F32),
        sl2=VMEM((rows, mid), F32),
        n3=VMEM((rows, wide), F32),
        bypass=VMEM((rows, wide), F32),
        y=VMEM((rows, wide), F32),
        slq=VMEM((rows, wide), F32),
        r=VMEM((rows, wide), BF16),
        n4=VMEM((rows, mid), F32),
        sl4=VMEM((rows, mid), F32),
        v1=VMEM((padded, mid), F32),
        t2=VMEM((rows, 9 * mid), BF16),
        n5=VMEM((rows, mid), F32),
        sl5=VMEM((rows, mid), F32),
        n6=VMEM((rows, wide), F32),
        d2=VMEM((rows, wide), F32),
        du3=VMEM((rows, wide), BF16),
        dz3=VMEM((rows, wide), BF16),
        dzp=VMEM((rows, wide), BF16),
        dt=VMEM((padded, 9 * mid), F32),
        d=VMEM((4, rows, mid), F32),
        back=VMEM((rows, inner), F32),
        late=DMA((2,)),
        gate=VMEM((rows, LANE), F32),
        facm=VMEM((4, 8, mid), F32),
        facw=VMEM((3, 8, wide), F32),
        gm=VMEM((8, mid), F32),
        gw=VMEM((8, wide), F32),
    )


def weight_scratch(weight, mpn):
    return dict(
        full=VMEM((weight.taps, mpn * weight.block, weight.width), BF16),
        fetch=DMA((2,)),
        lift=DMA((2,)),
        hand=DMA((2,)),
        own=DMA((1,)),
    )


def unit_scratch(unit, mpn):
    spread = (mpn, unit.taps, unit.block // 2, unit.width)
    pieces = (unit.ways, mpn, unit.taps, unit.piece, unit.width)
    return dict(
        part=VMEM((mpn, unit.taps, unit.block, unit.width), BF16),
        twin=VMEM(spread, BF16),
        sums=VMEM(pieces, BF16),
        hop=VMEM(pieces, BF16),
        fin=VMEM(pieces, BF16),
        swap=VMEM(pieces, BF16),
        twins=DMA((2,)),
        swaps=DMA((2,)),
        outs=DMA((2,)),
        hop_sent=DMA((2,)),
        hop_came=DMA((2,)),
        mix=DMA((2,)),
        cast_sent=DMA((2,)),
        cast_came=DMA((2,)),
    )


class Body:
    def __init__(self, given, made, scratch, chains, weights, units, sizes):
        self.given = given
        self.made = made
        self.links = scratch.chains
        self.weights = weights
        self.held = scratch.weights
        self.units = units
        self.places = classes(units)[2]
        self.rows = Rows(chains, sizes[1], sizes[2])
        self.sums = scratch.units
        self.chains = chains
        self.mid, self.wide, self.inner, self.dpn, self.mpn = sizes
        self.dp = lax.axis_index("dp")
        self.mp = lax.axis_index("mp")
        self.z = lax.div(self.dp, 2)
        self.core = lax.rem(self.dp, 2)
        self.levels = self.dpn // 2
        across = lax.div(self.mp, 2)
        along = lax.rem(self.mp, 2)
        self.peers = (
            across * 2 + (1 - along),
            (1 - across) * 2 + along,
            (1 - across) * 2 + (1 - along),
        )
        self.twin = self.z * 2 + (1 - self.core)
        self.others = [lax.rem(self.dp + step, self.dpn) for step in range(1, self.dpn)]
        self.stack = [lax.rem(self.z + step, self.levels) for step in range(1, self.levels)]
        self.flying = {}
        self.fetched = set()
        self.lifting = {}
        self.passing = set()
        self.present = set()
        self.background = []

    def barrier(self):
        semaphore = pltpu.get_barrier_semaphore()
        for peer in self.peers:
            pl.semaphore_signal(
                semaphore, inc=1, device_id=(self.dp, peer), device_id_type=MESH_ID
            )
        for other in self.others:
            pl.semaphore_signal(
                semaphore, inc=1, device_id=(other, self.mp), device_id_type=MESH_ID
            )
        pl.semaphore_wait(semaphore, len(self.peers) + len(self.others))

    def remote(self, source, target, sent, came, device):
        return pltpu.make_async_remote_copy(
            src_ref=source,
            dst_ref=target,
            send_sem=sent,
            recv_sem=came,
            device_id=device,
            device_id_type=MESH_ID,
        )


    def settle(self, slab, sems, device):
        copy = self.remote(slab, slab, sems.at[0], sems.at[1], device)
        copy.wait_send()
        copy.wait_recv()

    def scatter(self, link, values):
        width = link.send.shape[2]
        for block in range(self.mpn):
            link.send[block] = values[:, block * width : (block + 1) * width].astype(BF16)
        for step, peer in enumerate(self.peers):
            self.remote(
                link.send.at[peer],
                link.recv.at[step],
                link.sems.at[0],
                link.sems.at[1],
                (self.dp, peer),
            ).start()
        yield
        self.settle(link.recv, link.sems, (self.dp, self.peers[0]))
        total = link.send[self.mp].astype(F32)
        for step in range(self.mpn - 1):
            total = total + link.recv[step].astype(F32)
        return total

    def gather(self, link):
        mine = link.full.at[self.mp]
        for peer in self.peers:
            self.remote(
                mine, mine, link.sems.at[0], link.sems.at[1], (self.dp, peer)
            ).start()
        yield
        slab = link.full.at[pl.ds(0, self.mpn - 1)]
        self.settle(slab, link.sems, (self.dp, self.peers[0]))

    def joined(self, link):
        return jnp.concatenate([link.full[block] for block in range(self.mpn)], axis=1)

    def reduce(self, link, terms):
        stat = link.stat
        depth = stat.shape[1]
        lanes = terms[0].shape[1] // LANE
        lines = [
            term[:, lane * LANE : (lane + 1) * LANE] for term in terms for lane in range(lanes)
        ]
        if depth > len(lines):
            lines.append(jnp.zeros((depth - len(lines), LANE), F32))
        stat[self.dp] = jnp.concatenate(lines, axis=0)
        mine = stat.at[self.dp]
        for other in self.others:
            self.remote(
                mine, mine, link.sems.at[0], link.sems.at[1], (other, self.mp)
            ).start()
        yield
        slab = stat.at[pl.ds(0, self.dpn - 1)]
        self.settle(slab, link.sems, (self.others[0], self.mp))
        total = stat[0]
        for source in range(1, self.dpn):
            total = total + stat[source]
        rows = []
        for index in range(len(terms)):
            first = index * lanes
            pieces = [total[first + lane : first + lane + 1] for lane in range(lanes)]
            rows.append(pieces[0] if lanes == 1 else jnp.concatenate(pieces, axis=1))
        return rows


    def half(self, block, first, core):
        return pl.ds(pl.multiple_of(first + core * (block // 2), 16), block // 2)

    def eighth(self, block, first, core, level):
        size = block // (2 * self.levels)
        return pl.ds(pl.multiple_of(first + core * (block // 2) + level * size, 16), size)

    def shared(self, tensor):
        return tensor != TENSOR_Q1

    def mine(self, tensor, first):
        block = self.weights[tensor].block
        if self.shared(tensor):
            return self.eighth(block, first, self.core, self.z)
        return self.half(block, first, self.core)

    def weight_start(self, tensor):
        weight = self.weights[tensor]
        held = self.held[tensor]
        source = self.given.weights[tensor]
        block, width = weight.block, weight.width

        def columns(device):
            return pl.ds(pl.multiple_of(device * width, LANE), width)

        for peer in self.peers:
            self.remote(
                source.at[:, self.mine(tensor, 0), columns(peer)],
                held.full.at[:, self.mine(tensor, self.mp * block), :],
                held.fetch.at[0],
                held.fetch.at[1],
                (self.dp, peer),
            ).start()
        own = pltpu.make_async_copy(
            source.at[:, :, columns(self.mp)],
            held.full.at[:, pl.ds(pl.multiple_of(self.mp * block, 16), block), :],
            held.own.at[0],
        )
        own.start()
        self.flying[tensor] = own

    def slab(self, tensor, rows):
        return self.held[tensor].full.at[:, pl.ds(0, rows), :]

    def weight_fetched(self, tensor):
        if tensor in self.fetched:
            return
        block = self.weights[tensor].block
        rows = block // (2 * self.levels) if self.shared(tensor) else block // 2
        held = self.held[tensor]
        slab = self.slab(tensor, len(self.peers) * rows)
        self.settle(slab, held.fetch, (self.dp, self.peers[0]))
        self.flying[tensor].wait()
        self.fetched.add(tensor)

    def weight_lift(self, tensor, steps=(0, 1, 2)):
        self.weight_fetched(tensor)
        block = self.weights[tensor].block
        held = self.held[tensor]
        for step in steps:
            came = held.full.at[:, self.mine(tensor, self.peers[step] * block), :]
            for level in self.stack:
                self.remote(
                    came,
                    came,
                    held.lift.at[0],
                    held.lift.at[1],
                    (level * 2 + self.core, self.mp),
                ).start()
        self.lifting[tensor] = self.lifting.get(tensor, ()) + tuple(steps)

    def weight_pass(self, tensor):
        if tensor in self.passing:
            return
        self.passing.add(tensor)
        self.weight_fetched(tensor)
        block = self.weights[tensor].block
        held = self.held[tensor]
        if self.shared(tensor):
            rest = [step for step in range(3) if step not in self.lifting.get(tensor, ())]
            if rest:
                self.weight_lift(tensor, rest)
            rows = block // (2 * self.levels) * len(self.peers) * len(self.stack)
            slab = self.slab(tensor, rows)
            self.settle(slab, held.lift, (self.stack[0] * 2 + self.core, self.mp))
        for peer in self.peers:
            came = held.full.at[:, self.half(block, peer * block, self.core), :]
            self.remote(
                came, came, held.hand.at[0], held.hand.at[1], (self.twin, self.mp)
            ).start()

    def weight(self, tensor):
        held = self.held[tensor]
        weight = self.weights[tensor]
        if tensor not in self.present:
            self.weight_pass(tensor)
            slab = self.slab(tensor, len(self.peers) * (weight.block // 2))
            self.settle(slab, held.hand, (self.twin, self.mp))
            self.present.add(tensor)
        if weight.taps == 1:
            return held.full[0]
        return jnp.concatenate([held.full[tap] for tap in range(weight.taps)], axis=1)


    def keep(self, segment, values):
        if segment.real == segment.size:
            return values
        rows = lax.broadcasted_iota(jnp.int32, values.shape, values.ndim - 2)
        return jnp.where(rows < segment.real, values, 0.0)

    def factors(self, sums, squares, count):
        centre = sums / count
        spread = squares / count - centre * centre
        return centre, lax.rsqrt(spread + EPSILON)

    def sum_rows(self, values):
        return jnp.sum(values.reshape(-1, values.shape[-1]), axis=0, keepdims=True)

    def moments(self, chain, values):
        terms = []
        for segment in chain.segments:
            part = values[..., segment.start : segment.stop, :]
            terms.append(self.sum_rows(part))
            terms.append(self.sum_rows(part * part))
        return terms

    def mid_row(self, norm, what):
        return self.given.mids[norm * 2 + what][...].reshape(1, self.mid)

    def wide_row(self, norm, what):
        return self.given.wides[norm * 2 + what][...].reshape(1, self.wide)

    def width_mask(self, group):
        limit = lax.div(self.mid * self.mpn * (2 + self.given.widths[group]), 4)
        index = lax.broadcasted_iota(jnp.int32, (1, self.mid), 1) + self.mp * self.mid
        return (index < limit).astype(F32)

    def narrow_norm(self, chain, link, norm, values, totals, normed_ref, slope_ref, store):
        gain = self.mid_row(norm, 0)
        offset = self.mid_row(norm, 1)
        for index, segment in enumerate(chain.segments):
            rows = slice(segment.start, segment.stop)
            count = segment.count * (4 if norm == NORM_Q1 else 1)
            centre, factor = self.factors(totals[2 * index], totals[2 * index + 1], count)
            link.facm[norm, index : index + 1, :] = factor
            mask = self.width_mask(segment.group)
            normed = (values[..., rows, :] - centre) * factor
            normed_ref[..., rows, :] = normed
            affine = normed * gain + offset
            logistic = jax.nn.sigmoid(affine)
            slope_ref[..., rows, :] = mask * (logistic * (1.0 + affine * (1.0 - logistic)))
            store(segment, self.keep(segment, mask * (affine * logistic)).astype(BF16))

    def narrow_terms(self, chain, gradients, normed_ref):
        terms = []
        for segment in chain.segments:
            rows = slice(segment.start, segment.stop)
            part = gradients[..., rows, :]
            terms.append(self.sum_rows(part))
            terms.append(self.sum_rows(part * normed_ref[..., rows, :]))
        return terms

    def narrow_back(self, chain, link, norm, gradients_ref, totals, normed_ref, store):
        gain = self.mid_row(norm, 0)
        gain_total = None
        offset_total = None
        for index, segment in enumerate(chain.segments):
            rows = slice(segment.start, segment.stop)
            count = segment.count * (4 if norm == NORM_Q1 else 1)
            factor = link.facm[norm, index : index + 1, :]
            first, second = totals[2 * index], totals[2 * index + 1]
            gain_total = second if gain_total is None else gain_total + second
            offset_total = first if offset_total is None else offset_total + first
            change = (gain * factor) * (
                gradients_ref[..., rows, :]
                - first / count
                - normed_ref[..., rows, :] * (second / count)
            )
            store(segment, self.keep(segment, change).astype(BF16))
        link.gm[2 * norm : 2 * norm + 1, :] = gain_total
        link.gm[2 * norm + 1 : 2 * norm + 2, :] = offset_total


    def edge(self, edges, start, size, down, right):
        mask = None
        for shift, first in ((down, 0), (right, 2)):
            if shift == 0:
                continue
            values = edges[first + (0 if shift < 0 else 1), start : start + size, :]
            mask = values if mask is None else mask * values
        return mask

    def tap_list(self, stride):
        taps = []
        for vertical in range(3):
            for lateral in range(3):
                if stride == 2:
                    plane = 2 * (vertical != 1) + (lateral != 1)
                    taps.append((plane, -(vertical == 0), -(lateral == 0)))
                else:
                    taps.append((0, vertical - 1, lateral - 1))
        return taps

    def collect(self, chain, stride, padded, edges, taps_ref):
        mid = self.mid
        for position, (plane, down, right) in enumerate(self.tap_list(stride)):
            for index, segment in enumerate(chain.segments):
                shift = down * segment.down + right * segment.right
                base = GUARD + segment.start
                rows = slice(base + shift, base + shift + segment.size)
                values = padded[plane, rows, :] if stride == 2 else padded[rows, :]
                mask = self.edge(edges.at[index], base, segment.size, down, right)
                if mask is not None:
                    values = values * mask
                taps_ref[
                    segment.start : segment.stop, position * mid : (position + 1) * mid
                ] = values.astype(BF16)

    def spread(self, chain, stride, columns, edges):
        mid = self.mid
        taps = self.tap_list(stride)
        results = []
        for index, segment in enumerate(chain.segments):
            base = GUARD + segment.start
            for plane in range(4 if stride == 2 else 1):
                total = None
                for position, (where, down, right) in enumerate(taps):
                    if where != plane:
                        continue
                    start = base - (down * segment.down + right * segment.right)
                    values = columns[
                        start : start + segment.size, position * mid : (position + 1) * mid
                    ]
                    mask = self.edge(edges.at[index], start, segment.size, down, right)
                    if mask is not None:
                        values = values * mask
                    total = values if total is None else total + values
                results.append((segment, plane, self.keep(segment, total)))
        return results


    def clear(self, chain, link):
        rows = chain.rows
        for array in (link.h1, link.v1, link.dt):
            blank = jnp.zeros(array.shape[:-2] + (GUARD, array.shape[-1]), array.dtype)
            array[..., 0:GUARD, :] = blank
            array[..., GUARD + rows : 2 * GUARD + rows, :] = blank
        link.gm[...] = jnp.zeros_like(link.gm)
        link.gw[...] = jnp.zeros_like(link.gw)
        for segment in chain.segments:
            flags = [
                self.given.gates[segment.group][image].astype(F32)
                for image in range(segment.images)
            ]
            area = segment.side * segment.side
            link.gate[segment.start : segment.stop, :] = jnp.zeros((segment.size, LANE), F32)
            if segment.inside:
                rows = lax.broadcasted_iota(jnp.int32, (segment.size, LANE), 0)
                place = lax.rem(rows, segment.images)
                total = jnp.zeros((segment.size, LANE), F32)
                for image, flag in enumerate(flags):
                    total = jnp.where(place == image, flag, total)
                link.gate[segment.start : segment.stop, :] = total
            else:
                for image, flag in enumerate(flags):
                    start = segment.start + image * area
                    link.gate[start : start + area, :] = jnp.full((area, LANE), flag, F32)

    def lay_cotangent(self, chain, link):
        for segment in chain.segments:
            source = self.given.cotangents[segment.group]
            side = segment.side
            whole = segment.start + segment.real // 8 * 8
            if whole < segment.stop:
                link.d2[whole : segment.stop, :] = jnp.zeros(
                    (segment.stop - whole, self.wide), F32
                )
            if segment.inside:
                for i in range(side):
                    for j in range(side):
                        first = segment.start + i * segment.down + j * segment.right
                        link.d2[first : first + segment.images, :] = source[i, j].astype(F32)
            else:
                for image in range(segment.images):
                    for i in range(side):
                        first = segment.start + (image * side + i) * side
                        link.d2[first : first + side, :] = source[image, i].astype(F32)

    def gates(self, link, rows):
        return jnp.concatenate([link.gate[rows, :]] * (self.wide // LANE), axis=1)

    def bypass(self, chain, link, pixels):
        link.xs.full[self.mp] = pixels[0]
        yield from self.gather(link.xs)
        product = nn(self.joined(link.xs), self.weight(TENSOR_SC))
        link.bypass[...] = product
        totals = yield from self.reduce(link.fp, self.moments(chain, product))
        for index, segment in enumerate(chain.segments):
            rows = slice(segment.start, segment.stop)
            centre, factor = self.factors(
                totals[2 * index], totals[2 * index + 1], segment.count
            )
            link.facw[NORM_SC, index : index + 1, :] = factor
            link.bypass[rows, :] = (link.bypass[rows, :] - centre) * factor

    def chain(self, chain, link, given, place):
        rows = chain.rows
        start = self.rows.start[place]
        mid = self.mid

        def into(full):
            def store(segment, values):
                full[self.mp, segment.start : segment.stop, :] = values

            return store

        pixels = given.pixels[...].reshape(4 * rows, self.inner)
        total = yield from self.scatter(link.z1, nt(pixels, self.weight(TENSOR_Q1)))
        total = total.reshape(4, rows, mid)
        link.n1[...] = total
        totals = yield from self.reduce(link.f1, self.moments(chain, total))

        def store_one(segment, values):
            start = GUARD + segment.start
            link.h1[:, start : start + segment.size, :] = values.astype(F32)

        self.narrow_norm(chain, link, NORM_Q1, link.n1, totals, link.n1, link.sl1, store_one)
        self.collect(chain, 2, link.h1, given.edges, link.t1)
        total = yield from self.scatter(link.z2, nt(link.t1[...], self.weight(TENSOR_S1)))
        link.n2[...] = total
        totals = yield from self.reduce(link.f2, self.moments(chain, total))
        self.narrow_norm(
            chain, link, NORM_S1, link.n2, totals, link.n2, link.sl2, into(link.h2.full)
        )
        yield from self.gather(link.h2)
        product = nn(self.joined(link.h2), self.weight(TENSOR_E1))
        link.n3[...] = product
        totals = yield from self.reduce(link.f3, self.moments(chain, product))
        for index, segment in enumerate(chain.segments):
            span = slice(segment.start, segment.stop)
            centre, factor = self.factors(
                totals[2 * index], totals[2 * index + 1], segment.count
            )
            link.facw[NORM_E1, index : index + 1, :] = factor
            normed = (link.n3[span, :] - centre) * factor
            link.n3[span, :] = normed
            joint = (normed * self.wide_row(NORM_E1, 0) + self.wide_row(NORM_E1, 1)) + (
                link.bypass[span, :] * self.wide_row(NORM_SC, 0) + self.wide_row(NORM_SC, 1)
            )
            logistic = jax.nn.sigmoid(joint)
            link.slq[span, :] = logistic * (1.0 + joint * (1.0 - logistic))
            widened = joint * logistic
            link.y[span, :] = widened
            link.r[span, :] = self.keep(segment, widened).astype(BF16)

        total = yield from self.scatter(link.u1, nt(link.r[...], self.weight(TENSOR_Q2)))
        link.n4[...] = total
        totals = yield from self.reduce(link.f4, self.moments(chain, total))

        def store_four(segment, values):
            start = GUARD + segment.start
            link.v1[start : start + segment.size, :] = values.astype(F32)

        self.narrow_norm(chain, link, NORM_Q2, link.n4, totals, link.n4, link.sl4, store_four)
        self.collect(chain, 1, link.v1, given.edges, link.t2)
        total = yield from self.scatter(link.u2, nt(link.t2[...], self.weight(TENSOR_S2)))
        link.n5[...] = total
        totals = yield from self.reduce(link.f5, self.moments(chain, total))
        self.narrow_norm(
            chain, link, NORM_S2, link.n5, totals, link.n5, link.sl5, into(link.v2.full)
        )
        yield from self.gather(link.v2)
        product = nn(self.joined(link.v2), self.weight(TENSOR_E2))
        link.n6[...] = product
        totals = yield from self.reduce(link.f6, self.moments(chain, product))

        terms = []
        for index, segment in enumerate(chain.segments):
            span = slice(segment.start, segment.stop)
            centre, factor = self.factors(
                totals[2 * index], totals[2 * index + 1], segment.count
            )
            link.facw[NORM_E2, index : index + 1, :] = factor
            normed = (link.n6[span, :] - centre) * factor
            link.n6[span, :] = normed
            gate = self.gates(link, span)
            final = link.y[span, :] + gate * (
                normed * self.wide_row(NORM_E2, 0) + self.wide_row(NORM_E2, 1)
            )
            logistic = jax.nn.sigmoid(final)
            self.made.rows[start + segment.start : start + segment.stop, :] = final * logistic
            slope = logistic * (1.0 + final * (1.0 - logistic))
            change = slope * link.d2[span, :]
            link.d2[span, :] = change
            gated = gate * change
            terms.append(self.sum_rows(gated))
            terms.append(self.sum_rows(gated * normed))
        totals = yield from self.reduce(link.r6, terms)
        gain_total = None
        offset_total = None
        for index, segment in enumerate(chain.segments):
            span = slice(segment.start, segment.stop)
            factor = link.facw[NORM_E2, index : index + 1, :]
            first, second = totals[2 * index], totals[2 * index + 1]
            gain_total = second if gain_total is None else gain_total + second
            offset_total = first if offset_total is None else offset_total + first
            change = (self.wide_row(NORM_E2, 0) * factor) * (
                self.gates(link, span) * link.d2[span, :]
                - first / segment.count
                - link.n6[span, :] * (second / segment.count)
            )
            link.du3[span, :] = self.keep(segment, change).astype(BF16)
        link.gw[4:5, :] = gain_total
        link.gw[5:6, :] = offset_total
        total = yield from self.scatter(link.b2, nt(link.du3[...], self.weight(TENSOR_E2)))
        gradients = total * link.sl5[...]
        link.d[0] = gradients
        totals = yield from self.reduce(link.r5, self.narrow_terms(chain, gradients, link.n5))
        self.narrow_back(
            chain, link, NORM_S2, link.d.at[0], totals, link.n5, into(link.g2.full)
        )
        yield from self.gather(link.g2)
        link.dt[GUARD : GUARD + rows, :] = nn(self.joined(link.g2), self.weight(TENSOR_S2))
        for segment, _, values in self.spread(chain, 1, link.dt, given.edges):
            span = slice(segment.start, segment.stop)
            link.d[0, span, :] = values * link.sl4[span, :]
        totals = yield from self.reduce(
            link.r4, self.narrow_terms(chain, link.d.at[0], link.n4)
        )
        self.narrow_back(
            chain, link, NORM_Q2, link.d.at[0], totals, link.n4, into(link.g1.full)
        )
        yield from self.gather(link.g1)

        link.d2[...] = (
            link.d2[...] + nn(self.joined(link.g1), self.weight(TENSOR_Q2))
        ) * link.slq[...]
        terms = []
        for segment in chain.segments:
            span = slice(segment.start, segment.stop)
            part = link.d2[span, :]
            terms.append(self.sum_rows(part))
            terms.append(self.sum_rows(part * link.n3[span, :]))
            terms.append(self.sum_rows(part * link.bypass[span, :]))
        totals = yield from self.reduce(link.r3, terms)
        sums = [None] * 3
        for index, segment in enumerate(chain.segments):
            span = slice(segment.start, segment.stop)
            part = link.d2[span, :]
            first = totals[3 * index]
            for which in range(3):
                value = totals[3 * index + which]
                sums[which] = value if sums[which] is None else sums[which] + value
            for norm, normed, target in (
                (NORM_E1, link.n3, link.dz3),
                (NORM_SC, link.bypass, link.dzp),
            ):
                factor = link.facw[norm, index : index + 1, :]
                second = totals[3 * index + 1 + norm]
                change = (self.wide_row(norm, 0) * factor) * (
                    part - first / segment.count - normed[span, :] * (second / segment.count)
                )
                target[span, :] = self.keep(segment, change).astype(BF16)
        link.gw[0:1, :] = sums[1]
        link.gw[1:2, :] = sums[0]
        link.gw[2:3, :] = sums[2]
        link.gw[3:4, :] = sums[0]
        total = yield from self.scatter(link.b1, nt(link.dz3[...], self.weight(TENSOR_E1)))
        gradients = total * link.sl2[...]
        link.d[0] = gradients
        totals = yield from self.reduce(link.r2, self.narrow_terms(chain, gradients, link.n2))
        self.narrow_back(
            chain, link, NORM_S1, link.d.at[0], totals, link.n2, into(link.k2.full)
        )
        yield from self.gather(link.k2)
        link.dt[GUARD : GUARD + rows, :] = nn(self.joined(link.k2), self.weight(TENSOR_S1))
        for segment, plane, values in self.spread(chain, 2, link.dt, given.edges):
            span = slice(segment.start, segment.stop)
            link.d[plane, span, :] = values * link.sl1[plane, span, :]
        totals = yield from self.reduce(link.r1, self.narrow_terms(chain, link.d, link.n1))

        def store_back_one(segment, values):
            for plane in range(4):
                start = plane * rows + segment.start
                link.k1.full[self.mp, start : start + segment.size, :] = values[plane]

        self.narrow_back(chain, link, NORM_Q1, link.d, totals, link.n1, store_back_one)
        span = 2 * rows
        for part in range(3):
            if part < 2:
                mine = link.k1.full.at[self.mp, part * span : (part + 1) * span]
                sems = link.k1.sems if part == 0 else link.late
                for peer in self.peers:
                    self.remote(mine, mine, sems.at[0], sems.at[1], (self.dp, peer)).start()
            if part > 0:
                before = slice((part - 1) * span, part * span)
                full = link.k1.full
                pixels = jnp.concatenate([full[k, before] for k in range(self.mpn)], axis=1)
                product = nn(pixels, self.weight(TENSOR_Q1))
                for half in range(2):
                    plane = 2 * (part - 1) + half
                    first, columns = self.rows.plane(place, plane)
                    values = product[half * rows : (half + 1) * rows, :]
                    if plane == 0:
                        values = values + link.back[...]
                    self.made.rows[first : first + rows, columns] = values
            if part < 2:
                yield
                slab = link.k1.full.at[0 : self.mpn - 1, part * span : (part + 1) * span]
                self.settle(slab, sems, (self.dp, self.peers[0]))

    def bypass_back(self, link):
        product = nt(link.dzp[...], self.weight(TENSOR_SC))
        total = yield from self.scatter(link.bx, product)
        link.back[...] = total


    def unit_product(self, unit):
        total = None
        for link, given in zip(self.links, self.given.chains, strict=True):
            if unit.tensor == TENSOR_Q1:
                pixels = given.pixels[...]
                part = tn(self.joined(link.k1), pixels.reshape(-1, self.inner))
            else:
                left, right = {
                    TENSOR_S1: (link.k2, link.t1),
                    TENSOR_E1: (link.h2, link.dz3),
                    TENSOR_SC: (link.xs, link.dzp),
                    TENSOR_Q2: (link.g1, link.r),
                    TENSOR_S2: (link.g2, link.t2),
                    TENSOR_E2: (link.v2, link.du3),
                }[unit.tensor]
                part = tn(self.joined(left), right[:, unit.columns])
            total = part if total is None else total + part
        return total

    def unit_gradient(self, index):
        unit = self.units[index]
        held = self.sums[index]
        block, width, piece = unit.block, unit.width, unit.piece
        product = self.unit_product(unit).astype(BF16)
        for tap in range(unit.taps):
            columns = product[:, tap * width : (tap + 1) * width]
            held.part[:, tap] = columns.reshape(self.mpn, block, width)
        theirs = self.half(block, 0, 1 - self.core)
        copy = self.remote(
            held.part.at[:, :, theirs, :],
            held.twin,
            held.twins.at[0],
            held.twins.at[1],
            (self.twin, self.mp),
        )
        copy.start()
        yield 1
        copy.wait()
        mine = held.part[:, :, self.half(block, 0, self.core), :]
        both = mine.astype(F32) + held.twin[...].astype(F32)
        for way in range(unit.ways):
            held.sums[way] = both[:, :, way * piece : (way + 1) * piece, :].astype(BF16)
        yield from (self.direct(held) if unit.direct else self.climb(held))
        copy = self.remote(
            held.fin, held.swap, held.swaps.at[0], held.swaps.at[1], (self.twin, self.mp)
        )
        copy.start()
        yield 1
        copy.wait()
        which, place = self.places[index]
        out = self.made.units[which].at[place]
        copies = (
            pltpu.make_async_copy(held.fin, out.at[self.core], held.outs.at[0]),
            pltpu.make_async_copy(held.swap, out.at[1 - self.core], held.outs.at[1]),
        )
        for copy in copies:
            copy.start()
        yield 1
        for copy in copies:
            copy.wait()

    def mix(self, held, way):
        for peer in self.peers:
            self.remote(
                held.sums.at[way, peer],
                held.fin.at[way, self.mp],
                held.mix.at[0],
                held.mix.at[1],
                (self.dp, peer),
            ).start()
        held.fin[way, self.mp] = held.sums[way, self.mp]

    def mixed(self, held, way):
        slab = held.fin.at[way, pl.ds(0, len(self.peers))]
        self.settle(slab, held.mix, (self.dp, self.peers[0]))

    def direct(self, held):
        def above(level):
            return (level * 2 + self.core, self.mp)

        first = above(self.stack[0])
        others = pl.ds(0, len(self.stack))
        for level in self.stack:
            self.remote(
                held.sums.at[level],
                held.hop.at[self.z],
                held.hop_sent.at[0],
                held.hop_came.at[0],
                above(level),
            ).start()
        yield 2
        slab = held.hop.at[others]
        copy = self.remote(slab, slab, held.hop_sent.at[0], held.hop_came.at[0], first)
        copy.wait_send()
        copy.wait_recv()
        total = held.sums[self.z].astype(F32)
        for level in self.stack:
            total = total + held.hop[level].astype(F32)
        held.sums[self.z] = total.astype(BF16)
        self.mix(held, self.z)
        yield 2
        self.mixed(held, self.z)
        mine = held.fin.at[self.z]
        for level in self.stack:
            self.remote(
                mine, mine, held.cast_sent.at[0], held.cast_came.at[0], above(level)
            ).start()
        yield 2
        slab = held.fin.at[others]
        copy = self.remote(slab, slab, held.cast_sent.at[0], held.cast_came.at[0], first)
        copy.wait_send()
        copy.wait_recv()

    def climb(self, held):
        last = self.levels - 1

        def place(way, step):
            return step if way else last - step

        def onward(way):
            target = self.z + 1 if way else self.z - 1
            return (target * 2 + self.core, self.mp)

        def backward(way):
            target = self.z - 1 if way else self.z + 1
            return (target * 2 + self.core, self.mp)

        def hop(way, device):
            return self.remote(
                held.sums.at[way],
                held.hop.at[way],
                held.hop_sent.at[way],
                held.hop_came.at[way],
                device,
            )

        def cast(way, device):
            slot = held.fin.at[way]
            return self.remote(
                slot, slot, held.cast_sent.at[way], held.cast_came.at[way], device
            )

        for step in range(last + 1):
            for way in (0, 1):

                @pl.when(self.z == place(way, step))
                def _(way=way, step=step):
                    if step > 0:
                        hop(way, backward(way)).wait_recv()
                        total = held.sums[way].astype(F32) + held.hop[way].astype(F32)
                        held.sums[way] = total.astype(BF16)
                    if step < last:
                        hop(way, onward(way)).start()
                    else:
                        self.mix(held, way)

            yield 2
        for step in range(last, -1, -1):
            for way in (0, 1):

                @pl.when(self.z == place(way, step))
                def _(way=way, step=step):
                    if step == last:
                        self.mixed(held, way)
                    else:
                        hop(way, onward(way)).wait_send()
                        cast(way, onward(way)).wait_recv()
                    if step > 0:
                        cast(way, backward(way)).start()

            if step > 0:
                yield 2
        for way in (0, 1):

            @pl.when(self.z != place(way, 0))
            def _(way=way):
                cast(way, backward(way)).wait_send()


    def launch(self, task, delay=0):
        self.background.append([task, delay])

    def advance(self):
        for entry in list(self.background):
            entry[1] -= 1
            if entry[1] > 0:
                continue
            pause = next(entry[0], self)
            if pause is self:
                self.background.remove(entry)
            else:
                entry[1] = pause or 1

    def run(self):
        self.barrier()
        for tensor in (TENSOR_Q1, TENSOR_S1, TENSOR_E1, TENSOR_SC, TENSOR_Q2):
            self.weight_start(tensor)
        for chain, link in zip(self.chains, self.links, strict=True):
            self.clear(chain, link)
        parts = [
            (chain, link, given, place)
            for place, (chain, link, given) in enumerate(
                zip(self.chains, self.links, self.given.chains, strict=True)
            )
        ]
        tasks = [self.chain(*part) for part in parts]

        def start(tensor):
            return lambda: self.weight_start(tensor)

        def lift(tensor, steps=(0, 1, 2)):
            return lambda: self.weight_lift(tensor, steps)

        def hand(tensor):
            return lambda: self.weight_pass(tensor)

        def grad(tensor, part=0):
            places = [place for place, unit in enumerate(self.units) if unit.tensor == tensor]
            return lambda: self.launch(self.unit_gradient(places[part]), part)

        def bypass(index):
            chain, link, given, _ = parts[index]
            return lambda: self.launch(self.bypass(chain, link, given.pixels))

        def cotangent(index):
            chain, link, _, _ = parts[index]
            return lambda: self.lay_cotangent(chain, link)

        def bypass_back(index):
            return lambda: self.launch(self.bypass_back(self.links[index]))

        events = {
            1: (
                lift(TENSOR_S1),
                lift(TENSOR_E1),
                lift(TENSOR_SC),
                lift(TENSOR_Q2),
                cotangent(0),
                cotangent(1),
            ),
            2: (bypass(0), start(TENSOR_S2), start(TENSOR_E2), hand(TENSOR_S1)),
            3: (lift(TENSOR_S2, (0, 1)),),
            4: (bypass(1), hand(TENSOR_E1), hand(TENSOR_SC)),
            5: (lift(TENSOR_S2, (2,)),),
            6: (hand(TENSOR_Q2),),
            7: (lift(TENSOR_E2),),
            8: (hand(TENSOR_S2),),
            10: (hand(TENSOR_E2),),
            14: (grad(TENSOR_E2),),
            17: (grad(TENSOR_S2, 0),),
            18: (grad(TENSOR_S2, 1),),
            19: (grad(TENSOR_S2, 2), grad(TENSOR_Q2)),
            20: (grad(TENSOR_E1), grad(TENSOR_SC, 0)),
            21: (bypass_back(0), grad(TENSOR_SC, 1)),
            23: (
                bypass_back(1),
                grad(TENSOR_S1, 0),
                grad(TENSOR_S1, 1),
                grad(TENSOR_S1, 2),
            ),
        }
        slot = 0
        while tasks:
            slot += 1
            rounds = (0, 2) if slot in (24, 25) else (1, 1)
            for place, task in enumerate(list(tasks)):
                if next(task, self) is self:
                    tasks.remove(task)
                if place == 1:
                    for event in events.get(slot, ()):
                        event()
                for _ in range(rounds[place]):
                    self.advance()
        self.launch(self.unit_gradient(len(self.units) - 1))
        self.advance()
        first, second = self.links
        mids, wides = self.rows.mids, self.rows.wides
        self.made.rows[mids : mids + 8, : self.mid] = first.gm[...] + second.gm[...]
        self.made.rows[wides : wides + 8, :] = first.gw[...] + second.gw[...]
        while self.background:
            self.advance()


class Rows:
    def __init__(self, chains, wide, inner):
        self.total = sum(chain.rows for chain in chains)
        self.start = [0]
        for chain in chains:
            self.start.append(self.start[-1] + chain.rows)
        self.mids = 3 * self.total
        self.wides = self.mids + 8
        self.shape = (self.wides + 8, wide)
        self.inner = inner

    def plane(self, place, plane):
        first = (1 + plane // 2) * self.total + self.start[place]
        column = plane % 2 * self.inner
        return first, slice(column, column + self.inner)


def classes(units):
    shapes = []
    counts = []
    places = []
    for unit in units:
        key = (unit.ways, unit.taps, unit.piece, unit.width)
        if key not in shapes:
            shapes.append(key)
            counts.append(0)
        index = shapes.index(key)
        places.append((index, counts[index]))
        counts[index] += 1
    return shapes, counts, places


def kernel_text(trees, chains, weights, units, sizes, *refs):
    given_tree, made_tree, scratch_tree = trees
    given_size = given_tree.num_leaves
    made_size = made_tree.num_leaves
    given = jax.tree.unflatten(given_tree, refs[:given_size])
    made = jax.tree.unflatten(made_tree, refs[given_size : given_size + made_size])
    scratch = jax.tree.unflatten(scratch_tree, refs[given_size + made_size :])
    given = {**given, **dict(chains=[bag(value) for value in given["chains"]])}
    scratch = dict(
        chains=[bag(value) for value in scratch["chains"]],
        weights=[bag(value) for value in scratch["weights"]],
        units=[bag(value) for value in scratch["units"]],
    )
    Body(bag(given), bag(made), bag(scratch), chains, weights, units, sizes).run()


def finish_text(chains, weights, units, sizes, *refs):
    mid, wide, inner, mpn = sizes
    count = len(weights)
    take = iter(refs)
    shapes, _, places = classes(units)
    layout = Rows(chains, wide, inner)
    pieces = [next(take) for _ in shapes]
    rows_in = next(take)
    outs = [next(take) for _ in range(count)]
    groups = [(next(take), next(take)) for _ in range(3)]
    mid_outs = [next(take) for _ in range(8)]
    wide_outs = [next(take) for _ in range(6)]
    near = [next(take) for _ in shapes]
    rows = next(take)
    wided = [next(take) for _ in range(count)]
    woven, came, gone, weave = next(take), next(take), next(take), next(take)
    arrivals = []
    for index, (which, place) in enumerate(places):
        copy = pltpu.make_async_copy(
            pieces[which].at[place], near[which].at[place], came.at[index]
        )
        copy.start()
        arrivals.append(copy)
    last = pltpu.make_async_copy(rows_in, rows, came.at[len(units)])
    last.start()
    leaving = []
    for index, unit in enumerate(units):
        arrivals[index].wait()
        which, place = places[index]
        width, piece = unit.width, unit.piece
        stride = weights[unit.tensor].width
        for core in range(2):
            for way in range(unit.ways):
                first = core * (unit.block // 2) + way * piece
                for source in range(mpn):
                    column = source * stride + unit.first_column
                    for tap in range(unit.taps):
                        wided[unit.tensor][
                            unit.first_tap + tap,
                            first : first + piece,
                            column : column + width,
                        ] = near[which][place, core, way, source, tap].astype(F32)
        if index + 1 == len(units) or units[index + 1].tensor != unit.tensor:
            whole = unit.tensor
            copy = pltpu.make_async_copy(wided[whole], outs[whole], gone.at[whole])
            copy.start()
            leaving.append(copy)
    last.wait()
    for row, out in enumerate(mid_outs):
        out[...] = rows[layout.mids + row, :mid]
    for row, out in enumerate(wide_outs):
        out[...] = rows[layout.wides + row, :]
    for place, chain in enumerate(chains):
        for segment in chain.segments:
            out, back = groups[segment.group]
            side = segment.side
            if segment.inside:
                for i in range(side):
                    for j in range(side):
                        offset = segment.start + i * segment.down + j * segment.right
                        first = layout.start[place] + offset
                        out[i, j] = rows[first : first + segment.images, :]
                        for plane in range(4):
                            first, columns = layout.plane(place, plane)
                            first += offset
                            back[2 * i + plane // 2, 2 * j + plane % 2] = rows[
                                first : first + segment.images, columns
                            ]
                continue
            for image in range(segment.images):
                for i in range(side):
                    offset = segment.start + image * side * side + i * side
                    first = layout.start[place] + offset
                    out[image, i] = rows[first : first + side, :]
                    for plane in range(4):
                        first, columns = layout.plane(place, plane)
                        first += offset
                        for lane in range(inner // LANE):
                            column = columns.start + lane * LANE
                            woven[
                                lane,
                                image,
                                2 * i + plane // 2,
                                pl.ds(plane % 2, side, stride=2),
                                :,
                            ] = rows[first : first + side, column : column + LANE]
            for lane in range(inner // LANE):
                copy = pltpu.make_async_copy(
                    woven.at[lane],
                    back.at[:, :, :, pl.ds(lane * LANE, LANE)],
                    weave.at[lane],
                )
                copy.start()
                leaving.append(copy)
    for copy in leaving:
        copy.wait()


def padded_rows(values, size):
    extra = size - values.shape[-2]
    if extra == 0:
        return values
    widths = [(0, 0)] * (values.ndim - 2) + [(0, extra), (0, 0)]
    return jnp.pad(values, widths)


def planes_of(segment, images):
    side = segment.side
    channels = images.shape[3]
    values = segment.pixel_first(images)
    if segment.inside:
        split = values.reshape(side, 2, side, 2, segment.images, channels)
        split = split.transpose(1, 3, 0, 2, 4, 5)
    else:
        split = values.reshape(segment.images, side, 2, side, 2, channels)
        split = split.transpose(2, 4, 0, 1, 3, 5)
    return padded_rows(split.reshape(4, segment.real, channels), segment.size)


def edge_masks(chain):
    masks = np.zeros((len(chain.segments), 4, chain.padded, LANE), np.float32)
    for place, segment in enumerate(chain.segments):
        index = np.arange(segment.real)
        down = index // segment.down % segment.side
        right = index // segment.right % segment.side
        start = GUARD + segment.start
        last = segment.side - 1
        for which, inside in enumerate((down > 0, down < last, right > 0, right < last)):
            masks[place, which, start : start + segment.real] = inside[:, None]
    return jnp.asarray(masks)


def fused_device(dpn, mpn, *args):
    images, widths, gates, cotangents = args[0:3], args[3], args[4:7], args[7:10]
    q1, s1, e1, sc, q2, s2, e2 = (args[index] for index in (10, 13, 16, 19, 22, 25, 28))
    mids = [args[index] for index in (11, 12, 14, 15, 23, 24, 26, 27)]
    wides = [args[index] for index in (17, 18, 20, 21, 29, 30)]
    mid = q1.shape[0]
    wide = wides[0].shape[0]
    inner = images[0].shape[3]
    shapes = [(values.shape[0], values.shape[1]) for values in images]
    chains = [Chain((2, 0), shapes, dpn), Chain((1,), shapes, dpn)]
    weights = weight_table(mid, wide, inner)
    units = unit_table(weights)
    sizes = (mid, wide, inner, dpn, mpn)
    vmem = pl.BlockSpec(memory_space=VMEM)
    smem = pl.BlockSpec(memory_space=pltpu.SMEM)
    anywhere = pl.BlockSpec(memory_space=pl.ANY)
    hbm = pl.BlockSpec(memory_space=pltpu.HBM)

    def by_tap(spatial):
        return spatial.transpose(1, 2, 0, 3).reshape(9, mid, mpn * mid)

    def rows_of(chain, build):
        return jnp.concatenate([build(s) for s in chain.segments], axis=-2)

    given = dict(
        chains=[
            dict(
                pixels=rows_of(chain, lambda s: planes_of(s, images[s.group])),
                edges=edge_masks(chain),
            )
            for chain in chains
        ],
        mids=mids,
        wides=wides,
        widths=widths,
        gates=list(gates),
        cotangents=[
            s.pixel_first(cotangents[s.group])
            for s in sorted(
                (s for chain in chains for s in chain.segments), key=lambda s: s.group
            )
        ],
        weights=[q1[None], by_tap(s1), e1[None], sc[None], q2[None], by_tap(s2), e2[None]],
    )
    given_specs = dict(
        chains=[dict(pixels=vmem, edges=vmem) for _ in chains],
        mids=[vmem] * len(mids),
        wides=[vmem] * len(wides),
        widths=smem,
        gates=[smem] * 3,
        cotangents=[vmem] * 3,
        weights=[anywhere] * WEIGHTS,
    )
    shape = jax.ShapeDtypeStruct
    layout = Rows(chains, wide, inner)
    unit_shapes, unit_counts, _ = classes(units)
    made = dict(
        rows=shape(layout.shape, F32),
        units=[
            shape((count, 2, ways, mpn, *rest), BF16)
            for count, (ways, *rest) in zip(unit_counts, unit_shapes, strict=True)
        ],
    )
    made_specs = dict(rows=vmem, units=[anywhere] * len(unit_shapes))
    scratch = dict(
        chains=[chain_scratch(chain, mid, wide, inner, dpn, mpn) for chain in chains],
        weights=[weight_scratch(weight, mpn) for weight in weights],
        units=[unit_scratch(unit, mpn) for unit in units],
    )
    trees = tuple(jax.tree.structure(tree) for tree in (given_specs, made_specs, scratch))
    results = pl.pallas_call(
        functools.partial(kernel_text, trees, chains, weights, units, sizes),
        out_shape=jax.tree.leaves(made),
        in_specs=jax.tree.leaves(given_specs),
        out_specs=jax.tree.leaves(made_specs),
        scratch_shapes=jax.tree.leaves(scratch),
        compiler_params=pltpu.CompilerParams(
            collective_id=0, has_side_effects=True, vmem_limit_bytes=62 * 2**20
        ),
        name="bottlenecks",
    )(*jax.tree.leaves(given))
    got = bag(jax.tree.unflatten(trees[1], results))

    final_shapes = [shape((w.taps, w.block, mpn * w.width), F32) for w in weights]
    segments = sorted((s for chain in chains for s in chain.segments), key=lambda s: s.group)

    def laid(s, side, channels):
        if s.inside:
            return shape((side, side, s.images, channels), F32)
        return shape((s.images, side, side, channels), F32)

    group_shapes = []
    for s in segments:
        group_shapes += [laid(s, s.side, wide), laid(s, 2 * s.side, inner)]
    woven = [laid(s, 2 * s.side, inner) for s in segments if not s.inside]
    vector_shapes = [shape((mid,), F32)] * 8 + [shape((wide,), F32)] * 6
    final = pl.pallas_call(
        functools.partial(finish_text, chains, weights, units, (mid, wide, inner, mpn)),
        out_shape=final_shapes + group_shapes + vector_shapes,
        in_specs=[hbm] * (len(unit_shapes) + 1),
        out_specs=[hbm] * WEIGHTS
        + [spec for s in segments for spec in (vmem, vmem if s.inside else hbm)]
        + [vmem] * len(vector_shapes),
        scratch_shapes=[VMEM(value.shape, BF16) for value in made["units"]]
        + [VMEM(layout.shape, F32)]
        + [VMEM(value.shape, F32) for value in final_shapes]
        + [VMEM((inner // LANE, *woven[0].shape[:3], LANE), F32)]
        + [DMA((len(units) + 1,)), DMA((WEIGHTS,)), DMA((inner // LANE,))],
        compiler_params=pltpu.CompilerParams(vmem_limit_bytes=62 * 2**20),
        name="finish",
    )(*got.units, got.rows)
    tensors = final[:WEIGHTS]
    grads = [value[0] for value in tensors]
    for place in (TENSOR_S1, TENSOR_S2):
        split = tensors[place].reshape(3, 3, mid, mpn * mid)
        grads[place] = split.transpose(2, 0, 1, 3)
    laid_out = final[WEIGHTS : WEIGHTS + 6]
    outputs = [s.image_first(laid_out[2 * s.group]) for s in segments]
    input_grads = [s.image_first(laid_out[2 * s.group + 1]) for s in segments]
    gm = final[WEIGHTS + 6 : WEIGHTS + 14]
    gw = final[WEIGHTS + 14 :]
    return (
        *outputs,
        *input_grads,
        grads[TENSOR_Q1],
        gm[0],
        gm[1],
        grads[TENSOR_S1],
        gm[2],
        gm[3],
        grads[TENSOR_E1],
        gw[0],
        gw[1],
        grads[TENSOR_SC],
        gw[2],
        gw[3],
        grads[TENSOR_Q2],
        gm[4],
        gm[5],
        grads[TENSOR_S2],
        gm[6],
        gm[7],
        grads[TENSOR_E2],
        gw[4],
        gw[5],
    )


def fits_kernel(mesh, args):
    mid = args[10].shape[0]
    inner = args[0].shape[3]
    wide = args[17].shape[0]
    return (
        mesh.shape["mp"] == 4
        and mesh.shape["dp"] == 8
        and mid == LANE
        and inner % LANE == 0
        and wide == 2 * inner
    )


def per_device(mesh, *args):
    if fits_kernel(mesh, args):
        return fused_device(mesh.shape["dp"], mesh.shape["mp"], *args)
    return on_device(*args)


def solution(mesh):
    in_specs = (
        P("dp", None, None, "mp"),
        P("dp", None, None, "mp"),
        P("dp", None, None, "mp"),
        P(),
        P("dp"),
        P("dp"),
        P("dp"),
        P("dp", None, None, "mp"),
        P("dp", None, None, "mp"),
        P("dp", None, None, "mp"),
        P("mp", None),
        P("mp"),
        P("mp"),
        P("mp", None, None, None),
        P("mp"),
        P("mp"),
        P("mp", None),
        P("mp"),
        P("mp"),
        P("mp", None),
        P("mp"),
        P("mp"),
        P("mp", None),
        P("mp"),
        P("mp"),
        P("mp", None, None, None),
        P("mp"),
        P("mp"),
        P("mp", None),
        P("mp"),
        P("mp"),
    )
    out_specs = (
        P("dp", None, None, "mp"),
        P("dp", None, None, "mp"),
        P("dp", None, None, "mp"),
        P("dp", None, None, "mp"),
        P("dp", None, None, "mp"),
        P("dp", None, None, "mp"),
        P("mp", None),
        P("mp"),
        P("mp"),
        P("mp", None, None, None),
        P("mp"),
        P("mp"),
        P("mp", None),
        P("mp"),
        P("mp"),
        P("mp", None),
        P("mp"),
        P("mp"),
        P("mp", None),
        P("mp"),
        P("mp"),
        P("mp", None, None, None),
        P("mp"),
        P("mp"),
        P("mp", None),
        P("mp"),
        P("mp"),
    )
    return jax.shard_map(
        functools.partial(per_device, mesh),
        mesh=mesh,
        in_specs=in_specs,
        out_specs=out_specs,
        check_vma=False,
    )
```

```python
import functools
import types

import jax
import jax.numpy as jnp
import numpy as np
from jax import lax
from jax.experimental import pallas as pl
from jax.experimental.pallas import tpu as pltpu
from jax.sharding import PartitionSpec as P

EPSILON = 1e-05


def sigmoid_linear(values):
    return values * jax.nn.sigmoid(values)


def sigmoid_slope(values):
    logistic = jax.nn.sigmoid(values)
    return logistic * (1.0 + values * (1.0 - logistic))


def pointwise(hidden, weight):
    return jnp.einsum("nhwc,cd->nhwd", hidden, weight, preferred_element_type=jnp.float32)


def back_pointwise(gradients, weight):
    return jnp.einsum("nhwd,cd->nhwc", gradients, weight, preferred_element_type=jnp.float32)


def weight_term(activations, gradients):
    return jnp.einsum("nhwc,nhwd->cd", activations, gradients, preferred_element_type=jnp.float32)


def reduce_pointwise(hidden, weight):
    return jnp.einsum("nhwc,dc->nhwd", hidden, weight, preferred_element_type=jnp.float32)


def reduce_back(gradients, weight):
    return jnp.einsum("nhwd,dc->nhwc", gradients, weight, preferred_element_type=jnp.float32)


def reduce_term(gradients, activations):
    return jnp.einsum("nhwd,nhwc->dc", gradients, activations, preferred_element_type=jnp.float32)


def gather_taps(hidden, stride):
    extent = hidden.shape[1] // stride
    span_end = stride * (extent - 1) + 1
    padded = jnp.pad(hidden, ((0, 0), (1, 1), (1, 1), (0, 0)))
    pieces = [
        padded[:, vertical : vertical + span_end : stride, lateral : lateral + span_end : stride, :]
        for vertical in range(3)
        for lateral in range(3)
    ]
    return jnp.concatenate(pieces, axis=3)


def spread_taps(columns, stride, edge_size, channels):
    extent = columns.shape[1]
    span_end = stride * (extent - 1) + 1
    padded = jnp.zeros((columns.shape[0], edge_size + 2, edge_size + 2, channels), jnp.float32)
    for position in range(9):
        vertical = position // 3
        lateral = position % 3
        padded = padded.at[
            :, vertical : vertical + span_end : stride, lateral : lateral + span_end : stride, :
        ].add(columns[..., position * channels : (position + 1) * channels])
    return padded[:, 1:-1, 1:-1, :]


def stat_terms(values):
    return jnp.stack([jnp.sum(values, axis=(0, 1, 2)), jnp.sum(values * values, axis=(0, 1, 2))])


def grad_terms(gradients, normed):
    return jnp.stack(
        [jnp.sum(gradients, axis=(0, 1, 2)), jnp.sum(gradients * normed, axis=(0, 1, 2))]
    )


def samples_of(values):
    return values.shape[0] * values.shape[1] * values.shape[2] * lax.axis_size("dp")


def norm_apply(values, totals, samples, norm_gain, offset):
    centre = totals[0] / samples
    spread = totals[1] / samples - centre * centre
    factor = lax.rsqrt(spread + EPSILON)
    normed = (values - centre) * factor
    return (normed, factor, normed * norm_gain + offset)


def norm_back(gradients, normed, factor, totals, samples, norm_gain):
    return norm_gain * factor * (gradients - totals[0] / samples - normed * (totals[1] / samples))


def forward_totals(partials):
    return lax.psum(jnp.stack(partials), "dp")


def backward_totals(partials):
    return lax.psum(jnp.stack(partials), "dp")


def gather_channels(pieces):
    return (
        lax.all_gather(pieces[0], "mp", axis=3, tiled=True),
        lax.all_gather(pieces[1], "mp", axis=3, tiled=True),
        lax.all_gather(pieces[2], "mp", axis=3, tiled=True),
    )


def gather_hidden(pieces):
    return (
        lax.all_gather(pieces[0], "mp", axis=3, tiled=True),
        lax.all_gather(pieces[1], "mp", axis=3, tiled=True),
        lax.all_gather(pieces[2], "mp", axis=3, tiled=True),
    )


def gather_spatial_grads(pieces):
    return (
        lax.all_gather(pieces[0], "mp", axis=3, tiled=True),
        lax.all_gather(pieces[1], "mp", axis=3, tiled=True),
        lax.all_gather(pieces[2], "mp", axis=3, tiled=True),
    )


def gather_entry_grads(pieces):
    return (
        lax.all_gather(pieces[0], "mp", axis=3, tiled=True),
        lax.all_gather(pieces[1], "mp", axis=3, tiled=True),
        lax.all_gather(pieces[2], "mp", axis=3, tiled=True),
    )


def front_forward(gathered, stride, params, width_masks):
    squeeze, squeeze_gain, squeeze_offset, spatial_conv, spatial_gain, spatial_offset = params
    entry = [reduce_pointwise(values, squeeze) for values in gathered]
    entry_totals = forward_totals([stat_terms(values) for values in entry])
    entry_norm = [
        norm_apply(
            entry[member],
            entry_totals[member],
            samples_of(entry[member]),
            squeeze_gain,
            squeeze_offset,
        )
        for member in range(3)
    ]
    hidden = [
        (width_masks[member] * sigmoid_linear(entry_norm[member][2])).astype(jnp.bfloat16)
        for member in range(3)
    ]
    hidden_full = gather_hidden(hidden)
    taps = [gather_taps(values, stride) for values in hidden_full]
    spatial_rows = spatial_conv.reshape(spatial_conv.shape[0], -1)
    middle = [reduce_pointwise(values, spatial_rows) for values in taps]
    middle_totals = forward_totals([stat_terms(values) for values in middle])
    middle_norm = [
        norm_apply(
            middle[member],
            middle_totals[member],
            samples_of(middle[member]),
            spatial_gain,
            spatial_offset,
        )
        for member in range(3)
    ]
    narrow = [
        (width_masks[member] * sigmoid_linear(middle_norm[member][2])).astype(jnp.bfloat16)
        for member in range(3)
    ]
    return (entry_norm, taps, middle_norm, narrow)


def front_backward(narrow_grads, saved, gathered, stride, params, width_masks, column_weights):
    squeeze, squeeze_gain, squeeze_offset, spatial_conv, spatial_gain, spatial_offset = params
    entry_norm, taps, middle_norm, narrow = saved
    middle_out = [
        narrow_grads[member] * width_masks[member] * sigmoid_slope(middle_norm[member][2])
        for member in range(3)
    ]
    middle_totals = backward_totals(
        [grad_terms(middle_out[member], middle_norm[member][0]) for member in range(3)]
    )
    middle_grads = [
        norm_back(
            middle_out[member],
            middle_norm[member][0],
            middle_norm[member][1],
            middle_totals[member],
            samples_of(middle_out[member]),
            spatial_gain,
        ).astype(jnp.bfloat16)
        for member in range(3)
    ]
    spatial_grad = sum(
        (reduce_term(middle_grads[member], taps[member]) for member in range(3))
    ).reshape(spatial_conv.shape)
    squeeze_cols, spatial_cols = column_weights
    channels = spatial_cols.shape[3]
    spatial_flat = spatial_cols.reshape(spatial_cols.shape[0], -1)
    middle_full = gather_spatial_grads(middle_grads)
    hidden_grads = [
        spread_taps(
            reduce_back(middle_full[member], spatial_flat),
            stride,
            gathered[member].shape[1],
            channels,
        )
        for member in range(3)
    ]
    entry_out = [
        hidden_grads[member] * width_masks[member] * sigmoid_slope(entry_norm[member][2])
        for member in range(3)
    ]
    entry_totals = backward_totals(
        [grad_terms(entry_out[member], entry_norm[member][0]) for member in range(3)]
    )
    entry_grads = [
        norm_back(
            entry_out[member],
            entry_norm[member][0],
            entry_norm[member][1],
            entry_totals[member],
            samples_of(entry_out[member]),
            squeeze_gain,
        ).astype(jnp.bfloat16)
        for member in range(3)
    ]
    squeeze_grad = sum((reduce_term(entry_grads[member], gathered[member]) for member in range(3)))
    entry_full = gather_entry_grads(entry_grads)
    squeeze_flat = squeeze_cols.reshape(squeeze_cols.shape[0], -1)
    input_part = [reduce_back(entry_full[member], squeeze_flat) for member in range(3)]
    gain_grads = (
        jnp.sum(entry_totals[:, 1], axis=0),
        jnp.sum(entry_totals[:, 0], axis=0),
        jnp.sum(middle_totals[:, 1], axis=0),
        jnp.sum(middle_totals[:, 0], axis=0),
    )
    return (input_part, squeeze_grad, spatial_grad, gain_grads)


def tail_forward(narrow, bypass_inputs, expand, shortcut):
    partials = []
    for member in range(3):
        pieces = [pointwise(narrow[member], expand)]
        if shortcut is not None:
            pieces.append(pointwise(bypass_inputs[member], shortcut))
        partials.append(jnp.stack(pieces))
    partials = (
        lax.psum_scatter(
            partials[0].astype(jnp.bfloat16), "mp", scatter_dimension=4, tiled=True
        ).astype(jnp.float32),
        lax.psum_scatter(
            partials[1].astype(jnp.bfloat16), "mp", scatter_dimension=4, tiled=True
        ).astype(jnp.float32),
        lax.psum_scatter(
            partials[2].astype(jnp.bfloat16), "mp", scatter_dimension=4, tiled=True
        ).astype(jnp.float32),
    )
    return (partials, narrow)


def tail_backward(gradients, sources, bypass_inputs, expand, shortcut):
    arriving = (
        lax.all_gather(gradients[0], "mp", axis=4, tiled=True),
        lax.all_gather(gradients[1], "mp", axis=4, tiled=True),
        lax.all_gather(gradients[2], "mp", axis=4, tiled=True),
    )
    expand_grad = sum((weight_term(sources[member], arriving[member][0]) for member in range(3)))
    narrow_terms = [back_pointwise(arriving[member][0], expand) for member in range(3)]
    if shortcut is None:
        return (narrow_terms, expand_grad, None, None)
    shortcut_grad = sum(
        (weight_term(bypass_inputs[member], arriving[member][1]) for member in range(3))
    )
    bypass_terms = [back_pointwise(arriving[member][1], shortcut) for member in range(3)]
    return (narrow_terms, expand_grad, shortcut_grad, bypass_terms)


def on_device(
    images_small,
    images_medium,
    images_large,
    width_choice,
    gates_small,
    gates_medium,
    gates_large,
    cotangent_small,
    cotangent_medium,
    cotangent_large,
    squeeze_one,
    squeeze_gain_one,
    squeeze_offset_one,
    spatial_one,
    spatial_gain_one,
    spatial_offset_one,
    expand_one,
    expand_gain_one,
    expand_offset_one,
    shortcut_one,
    shortcut_gain,
    shortcut_offset,
    squeeze_two,
    squeeze_gain_two,
    squeeze_offset_two,
    spatial_two,
    spatial_gain_two,
    spatial_offset_two,
    expand_two,
    expand_gain_two,
    expand_offset_two,
):
    images = [images_small, images_medium, images_large]
    depth_gates = [
        flags.astype(jnp.float32)[:, None, None, None]
        for flags in (gates_small, gates_medium, gates_large)
    ]
    cotangents = [
        values.astype(jnp.float32)
        for values in (cotangent_small, cotangent_medium, cotangent_large)
    ]
    mid_local = squeeze_one.shape[0]
    channel_index = lax.axis_index("mp") * mid_local + jnp.arange(mid_local, dtype=jnp.int32)
    limits = mid_local * lax.axis_size("mp") * (2 + width_choice) // 4
    width_masks = [(channel_index < limits[member]).astype(jnp.float32) for member in range(3)]
    out_local = expand_gain_one.shape[0]
    params_one = (
        squeeze_one,
        squeeze_gain_one,
        squeeze_offset_one,
        spatial_one,
        spatial_gain_one,
        spatial_offset_one,
    )
    params_two = (
        squeeze_two,
        squeeze_gain_two,
        squeeze_offset_two,
        spatial_two,
        spatial_gain_two,
        spatial_offset_two,
    )
    expand_first, bypass_weight, expand_second = (expand_one, shortcut_one, expand_two)
    squeeze_cols_one, spatial_cols_one, squeeze_cols_two, spatial_cols_two = (
        lax.all_to_all(
            squeeze_one.reshape(mid_local, 1, 1, -1), "mp", split_axis=3, concat_axis=0, tiled=True
        ),
        lax.all_to_all(spatial_one, "mp", split_axis=3, concat_axis=0, tiled=True),
        lax.all_to_all(
            squeeze_two.reshape(mid_local, 1, 1, -1), "mp", split_axis=3, concat_axis=0, tiled=True
        ),
        lax.all_to_all(spatial_two, "mp", split_axis=3, concat_axis=0, tiled=True),
    )
    columns_one = (squeeze_cols_one, spatial_cols_one)
    columns_two = (squeeze_cols_two, spatial_cols_two)
    first_full = gather_channels(images)
    first_saved = front_forward(first_full, 2, params_one, width_masks)
    bypass_inputs = [values[:, ::2, ::2, :] for values in images]
    first_tail, first_sources = tail_forward(
        first_saved[3], bypass_inputs, expand_first, bypass_weight
    )
    first_totals = forward_totals(
        [
            jnp.concatenate(
                [stat_terms(first_tail[member][0]), stat_terms(first_tail[member][1])], axis=1
            )
            for member in range(3)
        ]
    )
    widened_norm = [
        norm_apply(
            first_tail[member][0],
            first_totals[member][:, :out_local],
            samples_of(first_tail[member][0]),
            expand_gain_one,
            expand_offset_one,
        )
        for member in range(3)
    ]
    bypass_norm = [
        norm_apply(
            first_tail[member][1],
            first_totals[member][:, out_local:],
            samples_of(first_tail[member][1]),
            shortcut_gain,
            shortcut_offset,
        )
        for member in range(3)
    ]
    first_sum = [widened_norm[member][2] + bypass_norm[member][2] for member in range(3)]
    block_out = [sigmoid_linear(values) for values in first_sum]
    second_full = gather_channels([values.astype(jnp.bfloat16) for values in block_out])
    second_saved = front_forward(second_full, 1, params_two, width_masks)
    second_tail, second_sources = tail_forward(second_saved[3], None, expand_second, None)
    second_totals = forward_totals([stat_terms(second_tail[member][0]) for member in range(3)])
    final_norm = [
        norm_apply(
            second_tail[member][0],
            second_totals[member],
            samples_of(second_tail[member][0]),
            expand_gain_two,
            expand_offset_two,
        )
        for member in range(3)
    ]
    second_sum = [
        block_out[member] + depth_gates[member] * final_norm[member][2] for member in range(3)
    ]
    results = [sigmoid_linear(values) for values in second_sum]
    second_slope = [sigmoid_slope(second_sum[member]) * cotangents[member] for member in range(3)]
    final_out = [depth_gates[member] * second_slope[member] for member in range(3)]
    final_totals = backward_totals(
        [grad_terms(final_out[member], final_norm[member][0]) for member in range(3)]
    )
    final_grads = [
        norm_back(
            final_out[member],
            final_norm[member][0],
            final_norm[member][1],
            final_totals[member],
            samples_of(final_out[member]),
            expand_gain_two,
        ).astype(jnp.bfloat16)[None]
        for member in range(3)
    ]
    second_result = tail_backward(final_grads, second_sources, None, expand_second, None)
    second_input_part, squeeze_two_grad, spatial_two_grad, second_gain_grads = front_backward(
        second_result[0], second_saved, second_full, 1, params_two, width_masks, columns_two
    )
    expand_two_grad = second_result[1]
    block_grads = [second_slope[member] + second_input_part[member] for member in range(3)]
    first_slope = [sigmoid_slope(first_sum[member]) * block_grads[member] for member in range(3)]
    first_grad_totals = backward_totals(
        [
            jnp.concatenate(
                [
                    grad_terms(first_slope[member], widened_norm[member][0]),
                    grad_terms(first_slope[member], bypass_norm[member][0]),
                ],
                axis=1,
            )
            for member in range(3)
        ]
    )
    tail_grads = [
        jnp.stack(
            [
                norm_back(
                    first_slope[member],
                    widened_norm[member][0],
                    widened_norm[member][1],
                    first_grad_totals[member][:, :out_local],
                    samples_of(first_slope[member]),
                    expand_gain_one,
                ),
                norm_back(
                    first_slope[member],
                    bypass_norm[member][0],
                    bypass_norm[member][1],
                    first_grad_totals[member][:, out_local:],
                    samples_of(first_slope[member]),
                    shortcut_gain,
                ),
            ]
        ).astype(jnp.bfloat16)
        for member in range(3)
    ]
    first_result = tail_backward(
        tail_grads, first_sources, bypass_inputs, expand_first, bypass_weight
    )
    expand_one_grad = first_result[1]
    shortcut_grad = first_result[2]
    bypass_terms = first_result[3]
    first_input_part, squeeze_one_grad, spatial_one_grad, first_gain_grads = front_backward(
        first_result[0], first_saved, first_full, 2, params_one, width_masks, columns_one
    )
    input_grads = [
        first_input_part[member].at[:, ::2, ::2, :].add(bypass_terms[member]) for member in range(3)
    ]
    summed = (
        lax.psum(squeeze_one_grad.astype(jnp.bfloat16), "dp").astype(jnp.float32),
        lax.psum(spatial_one_grad.astype(jnp.bfloat16), "dp").astype(jnp.float32),
        lax.psum(expand_one_grad.astype(jnp.bfloat16), "dp").astype(jnp.float32),
        lax.psum(shortcut_grad.astype(jnp.bfloat16), "dp").astype(jnp.float32),
        lax.psum(squeeze_two_grad.astype(jnp.bfloat16), "dp").astype(jnp.float32),
        lax.psum(spatial_two_grad.astype(jnp.bfloat16), "dp").astype(jnp.float32),
        lax.psum(expand_two_grad.astype(jnp.bfloat16), "dp").astype(jnp.float32),
    )
    expand_gain_one_grad = jnp.sum(first_grad_totals[:, 1, :out_local], axis=0)
    expand_offset_one_grad = jnp.sum(first_grad_totals[:, 0, :out_local], axis=0)
    shortcut_gain_grad = jnp.sum(first_grad_totals[:, 1, out_local:], axis=0)
    shortcut_offset_grad = jnp.sum(first_grad_totals[:, 0, out_local:], axis=0)
    expand_gain_two_grad = jnp.sum(final_totals[:, 1], axis=0)
    expand_offset_two_grad = jnp.sum(final_totals[:, 0], axis=0)
    return (
        results[0],
        results[1],
        results[2],
        input_grads[0],
        input_grads[1],
        input_grads[2],
        summed[0],
        first_gain_grads[0],
        first_gain_grads[1],
        summed[1],
        first_gain_grads[2],
        first_gain_grads[3],
        summed[2],
        expand_gain_one_grad,
        expand_offset_one_grad,
        summed[3],
        shortcut_gain_grad,
        shortcut_offset_grad,
        summed[4],
        second_gain_grads[0],
        second_gain_grads[1],
        summed[5],
        second_gain_grads[2],
        second_gain_grads[3],
        summed[6],
        expand_gain_two_grad,
        expand_offset_two_grad,
    )


LANE = 128
GUARD = 32
MESH_ID = pl.DeviceIdType.MESH
DMA = pltpu.SemaphoreType.DMA
VMEM = pltpu.VMEM
F32 = jnp.float32
BF16 = jnp.bfloat16
WEIGHTS = 7
TENSOR_Q1, TENSOR_S1, TENSOR_E1, TENSOR_SC, TENSOR_Q2, TENSOR_S2, TENSOR_E2 = range(WEIGHTS)
NORM_Q1, NORM_S1, NORM_Q2, NORM_S2 = range(4)
NORM_E1, NORM_SC, NORM_E2 = range(3)


def nn(left, right):
    return lax.dot_general(left, right, (((1,), (0,)), ((), ())), preferred_element_type=F32)


def nt(left, right):
    return lax.dot_general(left, right, (((1,), (1,)), ((), ())), preferred_element_type=F32)


def tn(left, right):
    return lax.dot_general(left, right, (((0,), (0,)), ((), ())), preferred_element_type=F32)


def bag(tree):
    if isinstance(tree, dict):
        return types.SimpleNamespace(**{name: bag(value) for name, value in tree.items()})
    return tree


class Segment:
    def __init__(self, group, start, images, side, replicas):
        self.group = group
        self.side = side
        self.images = images
        self.inside = images <= 4
        self.right = images if self.inside else 1
        self.down = self.right * side
        self.start = start
        self.real = images * side * side
        self.size = -(-self.real // 16) * 16
        self.stop = start + self.size
        self.count = float(self.real * replicas)

    def pixel_first(self, values):
        return values.transpose(1, 2, 0, 3) if self.inside else values

    def image_first(self, values):
        return values.transpose(2, 0, 1, 3) if self.inside else values


class Chain:
    def __init__(self, groups, shapes, replicas):
        self.segments = []
        start = 0
        for group in groups:
            images, side = shapes[group]
            segment = Segment(group, start, images, side // 2, replicas)
            self.segments.append(segment)
            start = segment.stop
        self.rows = start
        self.padded = start + 2 * GUARD


class Weight:
    def __init__(self, block, width, taps):
        self.block = block
        self.width = width
        self.taps = taps


def weight_table(mid, wide, inner):
    return [
        Weight(mid, inner, 1),
        Weight(mid, mid, 9),
        Weight(mid, wide, 1),
        Weight(inner, wide, 1),
        Weight(mid, wide, 1),
        Weight(mid, mid, 9),
        Weight(mid, wide, 1),
    ]


class Unit:
    def __init__(self, tensor, weight, part, parts, direct=False):
        self.tensor = tensor
        self.block = weight.block
        self.taps = weight.taps // parts if weight.taps > 1 else 1
        self.width = weight.width if weight.taps > 1 else weight.width // parts
        self.first_tap = part * self.taps if weight.taps > 1 else 0
        self.first_column = 0 if weight.taps > 1 else part * self.width
        self.span = self.taps * self.width
        self.columns = slice(part * self.span, (part + 1) * self.span)
        self.direct = direct
        self.ways = 4 if direct else 2
        self.piece = weight.block // (2 * self.ways)


def unit_table(weights):
    units = []
    for tensor, parts in (
        (TENSOR_E2, 1),
        (TENSOR_S2, 3),
        (TENSOR_Q2, 1),
        (TENSOR_E1, 1),
        (TENSOR_SC, 2),
        (TENSOR_S1, 3),
        (TENSOR_Q1, 1),
    ):
        for part in range(parts):
            units.append(
                Unit(tensor, weights[tensor], part, parts, direct=tensor == TENSOR_Q1)
            )
    return units


def chain_scratch(chain, mid, wide, inner, dpn, mpn):
    rows = chain.rows
    padded = chain.padded
    near = mpn - 1

    def summed(lead, width):
        return dict(
            send=VMEM((mpn, lead, width), BF16),
            recv=VMEM((near, lead, width), BF16),
            sems=DMA((2,)),
        )

    def gathered(lead, width):
        return dict(full=VMEM((mpn, lead, width), BF16), sems=DMA((2,)))

    def reduced(terms, width):
        depth = -(-(len(chain.segments) * terms * width // LANE) // 8) * 8
        return dict(stat=VMEM((dpn, depth, LANE), F32), sems=DMA((2,)))

    return dict(
        z1=summed(4 * rows, mid),
        z2=summed(rows, mid),
        u1=summed(rows, mid),
        u2=summed(rows, mid),
        b2=summed(rows, mid),
        b1=summed(rows, mid),
        bx=summed(rows, inner),
        xs=gathered(rows, inner),
        h2=gathered(rows, mid),
        v2=gathered(rows, mid),
        g2=gathered(rows, mid),
        g1=gathered(rows, mid),
        k2=gathered(rows, mid),
        k1=gathered(4 * rows, mid),
        f1=reduced(2, mid),
        f2=reduced(2, mid),
        f3=reduced(2, wide),
        fp=reduced(2, wide),
        f4=reduced(2, mid),
        f5=reduced(2, mid),
        f6=reduced(2, wide),
        r6=reduced(2, wide),
        r5=reduced(2, mid),
        r4=reduced(2, mid),
        r3=reduced(3, wide),
        r2=reduced(2, mid),
        r1=reduced(2, mid),
        n1=VMEM((4, rows, mid), F32),
        sl1=VMEM((4, rows, mid), F32),
        h1=VMEM((4, padded, mid), F32),
        t1=VMEM((rows, 9 * mid), BF16),
        n2=VMEM((rows, mid), F32),
        sl2=VMEM((rows, mid), F32),
        n3=VMEM((rows, wide), F32),
        bypass=VMEM((rows, wide), F32),
        y=VMEM((rows, wide), F32),
        slq=VMEM((rows, wide), F32),
        r=VMEM((rows, wide), BF16),
        n4=VMEM((rows, mid), F32),
        sl4=VMEM((rows, mid), F32),
        v1=VMEM((padded, mid), F32),
        t2=VMEM((rows, 9 * mid), BF16),
        n5=VMEM((rows, mid), F32),
        sl5=VMEM((rows, mid), F32),
        n6=VMEM((rows, wide), F32),
        d2=VMEM((rows, wide), F32),
        du3=VMEM((rows, wide), BF16),
        dz3=VMEM((rows, wide), BF16),
        dzp=VMEM((rows, wide), BF16),
        dt=VMEM((padded, 9 * mid), F32),
        d=VMEM((4, rows, mid), F32),
        back=VMEM((rows, inner), F32),
        pixels=VMEM((4, rows, inner), BF16),
        edges=VMEM((len(chain.segments), 4, padded, LANE), F32),
        loads=DMA((2,)),
        late=DMA((2,)),
        gate=VMEM((rows, LANE), F32),
        facm=VMEM((4, 8, mid), F32),
        facw=VMEM((3, 8, wide), F32),
        gm=VMEM((8, mid), F32),
        gw=VMEM((8, wide), F32),
    )


def weight_scratch(weight, mpn):
    return dict(
        full=VMEM((weight.taps, mpn * weight.block, weight.width), BF16),
        fetch=DMA((2,)),
        lift=DMA((2,)),
        hand=DMA((2,)),
        own=DMA((1,)),
    )


def unit_scratch(unit, mpn):
    spread = (mpn, unit.taps, unit.block // 2, unit.width)
    pieces = (unit.ways, mpn, unit.taps, unit.piece, unit.width)
    return dict(
        part=VMEM((mpn, unit.taps, unit.block, unit.width), BF16),
        twin=VMEM(spread, BF16),
        sums=VMEM(pieces, BF16),
        hop=VMEM(pieces, BF16),
        fin=VMEM(pieces, BF16),
        swap=VMEM(pieces, BF16),
        twins=DMA((2,)),
        swaps=DMA((2,)),
        outs=DMA((2,)),
        hop_sent=DMA((2,)),
        hop_came=DMA((2,)),
        mix=DMA((2,)),
        cast_sent=DMA((2,)),
        cast_came=DMA((2,)),
    )


class Body:
    def __init__(self, given, made, scratch, chains, weights, units, sizes):
        self.given = given
        self.made = made
        self.links = scratch.chains
        self.weights = weights
        self.held = scratch.weights
        self.units = units
        self.places = classes(units)[2]
        self.rows = Rows(chains, sizes[1], sizes[2])
        self.sums = scratch.units
        self.result = scratch.rows
        self.result_sem = scratch.rows_out
        self.chains = chains
        self.mid, self.wide, self.inner, self.dpn, self.mpn = sizes
        self.dp = lax.axis_index("dp")
        self.mp = lax.axis_index("mp")
        self.z = lax.div(self.dp, 2)
        self.core = lax.rem(self.dp, 2)
        self.levels = self.dpn // 2
        across = lax.div(self.mp, 2)
        along = lax.rem(self.mp, 2)
        self.peers = (
            across * 2 + (1 - along),
            (1 - across) * 2 + along,
            (1 - across) * 2 + (1 - along),
        )
        self.twin = self.z * 2 + (1 - self.core)
        self.others = [lax.rem(self.dp + step, self.dpn) for step in range(1, self.dpn)]
        self.stack = [lax.rem(self.z + step, self.levels) for step in range(1, self.levels)]
        self.flying = {}
        self.fetched = set()
        self.lifting = {}
        self.passing = set()
        self.present = set()
        self.background = []

    def barrier(self):
        semaphore = pltpu.get_barrier_semaphore()
        for peer in self.peers:
            pl.semaphore_signal(
                semaphore, inc=1, device_id=(self.dp, peer), device_id_type=MESH_ID
            )
        for other in self.others:
            pl.semaphore_signal(
                semaphore, inc=1, device_id=(other, self.mp), device_id_type=MESH_ID
            )
        pl.semaphore_wait(semaphore, len(self.peers) + len(self.others))

    def remote(self, source, target, sent, came, device):
        return pltpu.make_async_remote_copy(
            src_ref=source,
            dst_ref=target,
            send_sem=sent,
            recv_sem=came,
            device_id=device,
            device_id_type=MESH_ID,
        )


    def settle(self, slab, sems, device):
        copy = self.remote(slab, slab, sems.at[0], sems.at[1], device)
        copy.wait_send()
        copy.wait_recv()

    def scatter(self, link, values):
        width = link.send.shape[2]
        for block in range(self.mpn):
            link.send[block] = values[:, block * width : (block + 1) * width].astype(BF16)
        for step, peer in enumerate(self.peers):
            self.remote(
                link.send.at[peer],
                link.recv.at[step],
                link.sems.at[0],
                link.sems.at[1],
                (self.dp, peer),
            ).start()
        yield
        self.settle(link.recv, link.sems, (self.dp, self.peers[0]))
        total = link.send[self.mp].astype(F32)
        for step in range(self.mpn - 1):
            total = total + link.recv[step].astype(F32)
        return total

    def gather(self, link):
        mine = link.full.at[self.mp]
        for peer in self.peers:
            self.remote(
                mine, mine, link.sems.at[0], link.sems.at[1], (self.dp, peer)
            ).start()
        yield
        slab = link.full.at[pl.ds(0, self.mpn - 1)]
        self.settle(slab, link.sems, (self.dp, self.peers[0]))

    def joined(self, link):
        return jnp.concatenate([link.full[block] for block in range(self.mpn)], axis=1)

    def reduce(self, link, terms):
        stat = link.stat
        depth = stat.shape[1]
        lanes = terms[0].shape[1] // LANE
        lines = [
            term[:, lane * LANE : (lane + 1) * LANE] for term in terms for lane in range(lanes)
        ]
        if depth > len(lines):
            lines.append(jnp.zeros((depth - len(lines), LANE), F32))
        stat[self.dp] = jnp.concatenate(lines, axis=0)
        mine = stat.at[self.dp]
        for other in self.others:
            self.remote(
                mine, mine, link.sems.at[0], link.sems.at[1], (other, self.mp)
            ).start()
        yield
        slab = stat.at[pl.ds(0, self.dpn - 1)]
        self.settle(slab, link.sems, (self.others[0], self.mp))
        total = stat[0]
        for source in range(1, self.dpn):
            total = total + stat[source]
        rows = []
        for index in range(len(terms)):
            first = index * lanes
            pieces = [total[first + lane : first + lane + 1] for lane in range(lanes)]
            rows.append(pieces[0] if lanes == 1 else jnp.concatenate(pieces, axis=1))
        return rows


    def half(self, block, first, core):
        return pl.ds(pl.multiple_of(first + core * (block // 2), 16), block // 2)

    def eighth(self, block, first, core, level):
        size = block // (2 * self.levels)
        return pl.ds(pl.multiple_of(first + core * (block // 2) + level * size, 16), size)

    def shared(self, tensor):
        return tensor != TENSOR_Q1

    def mine(self, tensor, first):
        block = self.weights[tensor].block
        if self.shared(tensor):
            return self.eighth(block, first, self.core, self.z)
        return self.half(block, first, self.core)

    def weight_start(self, tensor):
        weight = self.weights[tensor]
        held = self.held[tensor]
        source = self.given.weights[tensor]
        block, width = weight.block, weight.width

        def columns(device):
            return pl.ds(pl.multiple_of(device * width, LANE), width)

        for peer in self.peers:
            self.remote(
                source.at[:, self.mine(tensor, 0), columns(peer)],
                held.full.at[:, self.mine(tensor, self.mp * block), :],
                held.fetch.at[0],
                held.fetch.at[1],
                (self.dp, peer),
            ).start()
        own = pltpu.make_async_copy(
            source.at[:, :, columns(self.mp)],
            held.full.at[:, pl.ds(pl.multiple_of(self.mp * block, 16), block), :],
            held.own.at[0],
        )
        own.start()
        self.flying[tensor] = own

    def slab(self, tensor, rows):
        return self.held[tensor].full.at[:, pl.ds(0, rows), :]

    def weight_fetched(self, tensor):
        if tensor in self.fetched:
            return
        block = self.weights[tensor].block
        rows = block // (2 * self.levels) if self.shared(tensor) else block // 2
        held = self.held[tensor]
        slab = self.slab(tensor, len(self.peers) * rows)
        self.settle(slab, held.fetch, (self.dp, self.peers[0]))
        self.flying[tensor].wait()
        self.fetched.add(tensor)

    def weight_lift(self, tensor, steps=(0, 1, 2)):
        self.weight_fetched(tensor)
        block = self.weights[tensor].block
        held = self.held[tensor]
        for step in steps:
            came = held.full.at[:, self.mine(tensor, self.peers[step] * block), :]
            for level in self.stack:
                self.remote(
                    came,
                    came,
                    held.lift.at[0],
                    held.lift.at[1],
                    (level * 2 + self.core, self.mp),
                ).start()
        self.lifting[tensor] = self.lifting.get(tensor, ()) + tuple(steps)

    def weight_pass(self, tensor):
        if tensor in self.passing:
            return
        self.passing.add(tensor)
        self.weight_fetched(tensor)
        block = self.weights[tensor].block
        held = self.held[tensor]
        if self.shared(tensor):
            rest = [step for step in range(3) if step not in self.lifting.get(tensor, ())]
            if rest:
                self.weight_lift(tensor, rest)
            rows = block // (2 * self.levels) * len(self.peers) * len(self.stack)
            slab = self.slab(tensor, rows)
            self.settle(slab, held.lift, (self.stack[0] * 2 + self.core, self.mp))
        for peer in self.peers:
            came = held.full.at[:, self.half(block, peer * block, self.core), :]
            self.remote(
                came, came, held.hand.at[0], held.hand.at[1], (self.twin, self.mp)
            ).start()

    def weight(self, tensor):
        held = self.held[tensor]
        weight = self.weights[tensor]
        if tensor not in self.present:
            self.weight_pass(tensor)
            slab = self.slab(tensor, len(self.peers) * (weight.block // 2))
            self.settle(slab, held.hand, (self.twin, self.mp))
            self.present.add(tensor)
        if weight.taps == 1:
            return held.full[0]
        return jnp.concatenate([held.full[tap] for tap in range(weight.taps)], axis=1)


    def keep(self, segment, values):
        if segment.real == segment.size:
            return values
        rows = lax.broadcasted_iota(jnp.int32, values.shape, values.ndim - 2)
        return jnp.where(rows < segment.real, values, 0.0)

    def factors(self, sums, squares, count):
        centre = sums / count
        spread = squares / count - centre * centre
        return centre, lax.rsqrt(spread + EPSILON)

    def sum_rows(self, values):
        return jnp.sum(values.reshape(-1, values.shape[-1]), axis=0, keepdims=True)

    def moments(self, chain, values):
        terms = []
        for segment in chain.segments:
            part = values[..., segment.start : segment.stop, :]
            terms.append(self.sum_rows(part))
            terms.append(self.sum_rows(part * part))
        return terms

    def mid_row(self, norm, what):
        return self.given.mids[norm * 2 + what][...].reshape(1, self.mid)

    def wide_row(self, norm, what):
        return self.given.wides[norm * 2 + what][...].reshape(1, self.wide)

    def width_mask(self, group):
        limit = lax.div(self.mid * self.mpn * (2 + self.given.widths[group]), 4)
        index = lax.broadcasted_iota(jnp.int32, (1, self.mid), 1) + self.mp * self.mid
        return (index < limit).astype(F32)

    def narrow_norm(self, chain, link, norm, values, totals, normed_ref, slope_ref, store):
        gain = self.mid_row(norm, 0)
        offset = self.mid_row(norm, 1)
        for index, segment in enumerate(chain.segments):
            rows = slice(segment.start, segment.stop)
            count = segment.count * (4 if norm == NORM_Q1 else 1)
            centre, factor = self.factors(totals[2 * index], totals[2 * index + 1], count)
            link.facm[norm, index : index + 1, :] = factor
            mask = self.width_mask(segment.group)
            normed = (values[..., rows, :] - centre) * factor
            normed_ref[..., rows, :] = normed
            affine = normed * gain + offset
            logistic = jax.nn.sigmoid(affine)
            slope_ref[..., rows, :] = mask * (logistic * (1.0 + affine * (1.0 - logistic)))
            store(segment, self.keep(segment, mask * (affine * logistic)).astype(BF16))

    def narrow_terms(self, chain, gradients, normed_ref):
        terms = []
        for segment in chain.segments:
            rows = slice(segment.start, segment.stop)
            part = gradients[..., rows, :]
            terms.append(self.sum_rows(part))
            terms.append(self.sum_rows(part * normed_ref[..., rows, :]))
        return terms

    def narrow_back(self, chain, link, norm, gradients_ref, totals, normed_ref, store):
        gain = self.mid_row(norm, 0)
        gain_total = None
        offset_total = None
        for index, segment in enumerate(chain.segments):
            rows = slice(segment.start, segment.stop)
            count = segment.count * (4 if norm == NORM_Q1 else 1)
            factor = link.facm[norm, index : index + 1, :]
            first, second = totals[2 * index], totals[2 * index + 1]
            gain_total = second if gain_total is None else gain_total + second
            offset_total = first if offset_total is None else offset_total + first
            change = (gain * factor) * (
                gradients_ref[..., rows, :]
                - first / count
                - normed_ref[..., rows, :] * (second / count)
            )
            store(segment, self.keep(segment, change).astype(BF16))
        link.gm[2 * norm : 2 * norm + 1, :] = gain_total
        link.gm[2 * norm + 1 : 2 * norm + 2, :] = offset_total


    def edge(self, edges, start, size, down, right):
        mask = None
        for shift, first in ((down, 0), (right, 2)):
            if shift == 0:
                continue
            values = edges[first + (0 if shift < 0 else 1), start : start + size, :]
            mask = values if mask is None else mask * values
        return mask

    def tap_list(self, stride):
        taps = []
        for vertical in range(3):
            for lateral in range(3):
                if stride == 2:
                    plane = 2 * (vertical != 1) + (lateral != 1)
                    taps.append((plane, -(vertical == 0), -(lateral == 0)))
                else:
                    taps.append((0, vertical - 1, lateral - 1))
        return taps

    def collect(self, chain, stride, padded, edges, taps_ref):
        mid = self.mid
        for position, (plane, down, right) in enumerate(self.tap_list(stride)):
            for index, segment in enumerate(chain.segments):
                shift = down * segment.down + right * segment.right
                base = GUARD + segment.start
                rows = slice(base + shift, base + shift + segment.size)
                values = padded[plane, rows, :] if stride == 2 else padded[rows, :]
                mask = self.edge(edges.at[index], base, segment.size, down, right)
                if mask is not None:
                    values = values * mask
                taps_ref[
                    segment.start : segment.stop, position * mid : (position + 1) * mid
                ] = values.astype(BF16)

    def spread(self, chain, stride, columns, edges):
        mid = self.mid
        taps = self.tap_list(stride)
        results = []
        for index, segment in enumerate(chain.segments):
            base = GUARD + segment.start
            for plane in range(4 if stride == 2 else 1):
                total = None
                for position, (where, down, right) in enumerate(taps):
                    if where != plane:
                        continue
                    start = base - (down * segment.down + right * segment.right)
                    values = columns[
                        start : start + segment.size, position * mid : (position + 1) * mid
                    ]
                    mask = self.edge(edges.at[index], start, segment.size, down, right)
                    if mask is not None:
                        values = values * mask
                    total = values if total is None else total + values
                results.append((segment, plane, self.keep(segment, total)))
        return results


    def clear(self, chain, link):
        rows = chain.rows
        for array in (link.h1, link.v1, link.dt):
            blank = jnp.zeros(array.shape[:-2] + (GUARD, array.shape[-1]), array.dtype)
            array[..., 0:GUARD, :] = blank
            array[..., GUARD + rows : 2 * GUARD + rows, :] = blank
        link.gm[...] = jnp.zeros_like(link.gm)
        link.gw[...] = jnp.zeros_like(link.gw)
        for segment in chain.segments:
            flags = [
                self.given.gates[segment.group][image].astype(F32)
                for image in range(segment.images)
            ]
            area = segment.side * segment.side
            link.gate[segment.start : segment.stop, :] = jnp.zeros((segment.size, LANE), F32)
            if segment.inside:
                rows = lax.broadcasted_iota(jnp.int32, (segment.size, LANE), 0)
                place = lax.rem(rows, segment.images)
                total = jnp.zeros((segment.size, LANE), F32)
                for image, flag in enumerate(flags):
                    total = jnp.where(place == image, flag, total)
                link.gate[segment.start : segment.stop, :] = total
            else:
                for image, flag in enumerate(flags):
                    start = segment.start + image * area
                    link.gate[start : start + area, :] = jnp.full((area, LANE), flag, F32)

    def lay_cotangent(self, chain, link):
        for segment in chain.segments:
            source = self.given.cotangents[segment.group]
            side = segment.side
            whole = segment.start + segment.real // 8 * 8
            if whole < segment.stop:
                link.d2[whole : segment.stop, :] = jnp.zeros(
                    (segment.stop - whole, self.wide), F32
                )
            if segment.inside:
                for i in range(side):
                    for j in range(side):
                        first = segment.start + i * segment.down + j * segment.right
                        link.d2[first : first + segment.images, :] = source[i, j].astype(F32)
            else:
                for image in range(segment.images):
                    for i in range(side):
                        first = segment.start + (image * side + i) * side
                        link.d2[first : first + side, :] = source[image, i].astype(F32)

    def gates(self, link, rows):
        return jnp.concatenate([link.gate[rows, :]] * (self.wide // LANE), axis=1)

    def bypass(self, chain, link, pixels):
        link.xs.full[self.mp] = pixels[0]
        yield from self.gather(link.xs)
        product = nn(self.joined(link.xs), self.weight(TENSOR_SC))
        link.bypass[...] = product
        totals = yield from self.reduce(link.fp, self.moments(chain, product))
        for index, segment in enumerate(chain.segments):
            rows = slice(segment.start, segment.stop)
            centre, factor = self.factors(
                totals[2 * index], totals[2 * index + 1], segment.count
            )
            link.facw[NORM_SC, index : index + 1, :] = factor
            link.bypass[rows, :] = (link.bypass[rows, :] - centre) * factor

    def chain(self, chain, link, given, place):
        rows = chain.rows
        start = self.rows.start[place]
        mid = self.mid

        def into(full):
            def store(segment, values):
                full[self.mp, segment.start : segment.stop, :] = values

            return store

        pixels = given.pixels[...].reshape(4 * rows, self.inner)
        total = yield from self.scatter(link.z1, nt(pixels, self.weight(TENSOR_Q1)))
        total = total.reshape(4, rows, mid)
        link.n1[...] = total
        totals = yield from self.reduce(link.f1, self.moments(chain, total))

        def store_one(segment, values):
            start = GUARD + segment.start
            link.h1[:, start : start + segment.size, :] = values.astype(F32)

        self.narrow_norm(chain, link, NORM_Q1, link.n1, totals, link.n1, link.sl1, store_one)
        self.collect(chain, 2, link.h1, given.edges, link.t1)
        total = yield from self.scatter(link.z2, nt(link.t1[...], self.weight(TENSOR_S1)))
        link.n2[...] = total
        totals = yield from self.reduce(link.f2, self.moments(chain, total))
        self.narrow_norm(
            chain, link, NORM_S1, link.n2, totals, link.n2, link.sl2, into(link.h2.full)
        )
        yield from self.gather(link.h2)
        product = nn(self.joined(link.h2), self.weight(TENSOR_E1))
        link.n3[...] = product
        totals = yield from self.reduce(link.f3, self.moments(chain, product))
        for index, segment in enumerate(chain.segments):
            span = slice(segment.start, segment.stop)
            centre, factor = self.factors(
                totals[2 * index], totals[2 * index + 1], segment.count
            )
            link.facw[NORM_E1, index : index + 1, :] = factor
            normed = (link.n3[span, :] - centre) * factor
            link.n3[span, :] = normed
            joint = (normed * self.wide_row(NORM_E1, 0) + self.wide_row(NORM_E1, 1)) + (
                link.bypass[span, :] * self.wide_row(NORM_SC, 0) + self.wide_row(NORM_SC, 1)
            )
            logistic = jax.nn.sigmoid(joint)
            link.slq[span, :] = logistic * (1.0 + joint * (1.0 - logistic))
            widened = joint * logistic
            link.y[span, :] = widened
            link.r[span, :] = self.keep(segment, widened).astype(BF16)

        total = yield from self.scatter(link.u1, nt(link.r[...], self.weight(TENSOR_Q2)))
        link.n4[...] = total
        totals = yield from self.reduce(link.f4, self.moments(chain, total))

        def store_four(segment, values):
            start = GUARD + segment.start
            link.v1[start : start + segment.size, :] = values.astype(F32)

        self.narrow_norm(chain, link, NORM_Q2, link.n4, totals, link.n4, link.sl4, store_four)
        self.collect(chain, 1, link.v1, given.edges, link.t2)
        total = yield from self.scatter(link.u2, nt(link.t2[...], self.weight(TENSOR_S2)))
        link.n5[...] = total
        totals = yield from self.reduce(link.f5, self.moments(chain, total))
        self.narrow_norm(
            chain, link, NORM_S2, link.n5, totals, link.n5, link.sl5, into(link.v2.full)
        )
        yield from self.gather(link.v2)
        product = nn(self.joined(link.v2), self.weight(TENSOR_E2))
        link.n6[...] = product
        totals = yield from self.reduce(link.f6, self.moments(chain, product))

        terms = []
        for index, segment in enumerate(chain.segments):
            span = slice(segment.start, segment.stop)
            centre, factor = self.factors(
                totals[2 * index], totals[2 * index + 1], segment.count
            )
            link.facw[NORM_E2, index : index + 1, :] = factor
            normed = (link.n6[span, :] - centre) * factor
            link.n6[span, :] = normed
            gate = self.gates(link, span)
            final = link.y[span, :] + gate * (
                normed * self.wide_row(NORM_E2, 0) + self.wide_row(NORM_E2, 1)
            )
            logistic = jax.nn.sigmoid(final)
            self.result[start + segment.start : start + segment.stop, :] = final * logistic
            slope = logistic * (1.0 + final * (1.0 - logistic))
            change = slope * link.d2[span, :]
            link.d2[span, :] = change
            gated = gate * change
            terms.append(self.sum_rows(gated))
            terms.append(self.sum_rows(gated * normed))
        totals = yield from self.reduce(link.r6, terms)
        gain_total = None
        offset_total = None
        for index, segment in enumerate(chain.segments):
            span = slice(segment.start, segment.stop)
            factor = link.facw[NORM_E2, index : index + 1, :]
            first, second = totals[2 * index], totals[2 * index + 1]
            gain_total = second if gain_total is None else gain_total + second
            offset_total = first if offset_total is None else offset_total + first
            change = (self.wide_row(NORM_E2, 0) * factor) * (
                self.gates(link, span) * link.d2[span, :]
                - first / segment.count
                - link.n6[span, :] * (second / segment.count)
            )
            link.du3[span, :] = self.keep(segment, change).astype(BF16)
        link.gw[4:5, :] = gain_total
        link.gw[5:6, :] = offset_total
        total = yield from self.scatter(link.b2, nt(link.du3[...], self.weight(TENSOR_E2)))
        gradients = total * link.sl5[...]
        link.d[0] = gradients
        totals = yield from self.reduce(link.r5, self.narrow_terms(chain, gradients, link.n5))
        self.narrow_back(
            chain, link, NORM_S2, link.d.at[0], totals, link.n5, into(link.g2.full)
        )
        yield from self.gather(link.g2)
        link.dt[GUARD : GUARD + rows, :] = nn(self.joined(link.g2), self.weight(TENSOR_S2))
        for segment, _, values in self.spread(chain, 1, link.dt, given.edges):
            span = slice(segment.start, segment.stop)
            link.d[0, span, :] = values * link.sl4[span, :]
        totals = yield from self.reduce(
            link.r4, self.narrow_terms(chain, link.d.at[0], link.n4)
        )
        self.narrow_back(
            chain, link, NORM_Q2, link.d.at[0], totals, link.n4, into(link.g1.full)
        )
        yield from self.gather(link.g1)

        link.d2[...] = (
            link.d2[...] + nn(self.joined(link.g1), self.weight(TENSOR_Q2))
        ) * link.slq[...]
        terms = []
        for segment in chain.segments:
            span = slice(segment.start, segment.stop)
            part = link.d2[span, :]
            terms.append(self.sum_rows(part))
            terms.append(self.sum_rows(part * link.n3[span, :]))
            terms.append(self.sum_rows(part * link.bypass[span, :]))
        totals = yield from self.reduce(link.r3, terms)
        sums = [None] * 3
        for index, segment in enumerate(chain.segments):
            span = slice(segment.start, segment.stop)
            part = link.d2[span, :]
            first = totals[3 * index]
            for which in range(3):
                value = totals[3 * index + which]
                sums[which] = value if sums[which] is None else sums[which] + value
            for norm, normed, target in (
                (NORM_E1, link.n3, link.dz3),
                (NORM_SC, link.bypass, link.dzp),
            ):
                factor = link.facw[norm, index : index + 1, :]
                second = totals[3 * index + 1 + norm]
                change = (self.wide_row(norm, 0) * factor) * (
                    part - first / segment.count - normed[span, :] * (second / segment.count)
                )
                target[span, :] = self.keep(segment, change).astype(BF16)
        link.gw[0:1, :] = sums[1]
        link.gw[1:2, :] = sums[0]
        link.gw[2:3, :] = sums[2]
        link.gw[3:4, :] = sums[0]
        total = yield from self.scatter(link.b1, nt(link.dz3[...], self.weight(TENSOR_E1)))
        gradients = total * link.sl2[...]
        link.d[0] = gradients
        totals = yield from self.reduce(link.r2, self.narrow_terms(chain, gradients, link.n2))
        self.narrow_back(
            chain, link, NORM_S1, link.d.at[0], totals, link.n2, into(link.k2.full)
        )
        yield from self.gather(link.k2)
        link.dt[GUARD : GUARD + rows, :] = nn(self.joined(link.k2), self.weight(TENSOR_S1))
        for segment, plane, values in self.spread(chain, 2, link.dt, given.edges):
            span = slice(segment.start, segment.stop)
            link.d[plane, span, :] = values * link.sl1[plane, span, :]
        totals = yield from self.reduce(link.r1, self.narrow_terms(chain, link.d, link.n1))

        def store_back_one(segment, values):
            for plane in range(4):
                start = plane * rows + segment.start
                link.k1.full[self.mp, start : start + segment.size, :] = values[plane]

        self.narrow_back(chain, link, NORM_Q1, link.d, totals, link.n1, store_back_one)
        span = 2 * rows
        for part in range(3):
            if part < 2:
                mine = link.k1.full.at[self.mp, part * span : (part + 1) * span]
                sems = link.k1.sems if part == 0 else link.late
                for peer in self.peers:
                    self.remote(mine, mine, sems.at[0], sems.at[1], (self.dp, peer)).start()
            if part > 0:
                before = slice((part - 1) * span, part * span)
                full = link.k1.full
                pixels = jnp.concatenate([full[k, before] for k in range(self.mpn)], axis=1)
                product = nn(pixels, self.weight(TENSOR_Q1))
                for half in range(2):
                    plane = 2 * (part - 1) + half
                    first, columns = self.rows.plane(place, plane)
                    values = product[half * rows : (half + 1) * rows, :]
                    if plane == 0:
                        values = values + link.back[...]
                    self.result[first : first + rows, columns] = values
            if part < 2:
                yield
                slab = link.k1.full.at[0 : self.mpn - 1, part * span : (part + 1) * span]
                self.settle(slab, sems, (self.dp, self.peers[0]))

    def bypass_back(self, link):
        product = nt(link.dzp[...], self.weight(TENSOR_SC))
        total = yield from self.scatter(link.bx, product)
        link.back[...] = total


    def unit_product(self, unit):
        total = None
        for link in self.links:
            if unit.tensor == TENSOR_Q1:
                pixels = link.pixels[...]
                part = tn(self.joined(link.k1), pixels.reshape(-1, self.inner))
            else:
                left, right = {
                    TENSOR_S1: (link.k2, link.t1),
                    TENSOR_E1: (link.h2, link.dz3),
                    TENSOR_SC: (link.xs, link.dzp),
                    TENSOR_Q2: (link.g1, link.r),
                    TENSOR_S2: (link.g2, link.t2),
                    TENSOR_E2: (link.v2, link.du3),
                }[unit.tensor]
                part = tn(self.joined(left), right[:, unit.columns])
            total = part if total is None else total + part
        return total

    def unit_gradient(self, index):
        unit = self.units[index]
        held = self.sums[index]
        block, width, piece = unit.block, unit.width, unit.piece
        product = self.unit_product(unit).astype(BF16)
        for tap in range(unit.taps):
            columns = product[:, tap * width : (tap + 1) * width]
            held.part[:, tap] = columns.reshape(self.mpn, block, width)
        theirs = self.half(block, 0, 1 - self.core)
        copy = self.remote(
            held.part.at[:, :, theirs, :],
            held.twin,
            held.twins.at[0],
            held.twins.at[1],
            (self.twin, self.mp),
        )
        copy.start()
        yield 1
        copy.wait()
        mine = held.part[:, :, self.half(block, 0, self.core), :]
        both = mine.astype(F32) + held.twin[...].astype(F32)
        for way in range(unit.ways):
            held.sums[way] = both[:, :, way * piece : (way + 1) * piece, :].astype(BF16)
        yield from (self.direct(held) if unit.direct else self.climb(held))
        copy = self.remote(
            held.fin, held.swap, held.swaps.at[0], held.swaps.at[1], (self.twin, self.mp)
        )
        copy.start()
        yield 1
        copy.wait()
        which, place = self.places[index]
        out = self.made.units[which].at[place]
        copies = (
            pltpu.make_async_copy(held.fin, out.at[self.core], held.outs.at[0]),
            pltpu.make_async_copy(held.swap, out.at[1 - self.core], held.outs.at[1]),
        )
        for copy in copies:
            copy.start()
        yield 1
        for copy in copies:
            copy.wait()

    def mix(self, held, way):
        for peer in self.peers:
            self.remote(
                held.sums.at[way, peer],
                held.fin.at[way, self.mp],
                held.mix.at[0],
                held.mix.at[1],
                (self.dp, peer),
            ).start()
        held.fin[way, self.mp] = held.sums[way, self.mp]

    def mixed(self, held, way):
        slab = held.fin.at[way, pl.ds(0, len(self.peers))]
        self.settle(slab, held.mix, (self.dp, self.peers[0]))

    def direct(self, held):
        def above(level):
            return (level * 2 + self.core, self.mp)

        first = above(self.stack[0])
        others = pl.ds(0, len(self.stack))
        for level in self.stack:
            self.remote(
                held.sums.at[level],
                held.hop.at[self.z],
                held.hop_sent.at[0],
                held.hop_came.at[0],
                above(level),
            ).start()
        yield 2
        slab = held.hop.at[others]
        copy = self.remote(slab, slab, held.hop_sent.at[0], held.hop_came.at[0], first)
        copy.wait_send()
        copy.wait_recv()
        total = held.sums[self.z].astype(F32)
        for level in self.stack:
            total = total + held.hop[level].astype(F32)
        held.sums[self.z] = total.astype(BF16)
        self.mix(held, self.z)
        yield 2
        self.mixed(held, self.z)
        mine = held.fin.at[self.z]
        for level in self.stack:
            self.remote(
                mine, mine, held.cast_sent.at[0], held.cast_came.at[0], above(level)
            ).start()
        yield 2
        slab = held.fin.at[others]
        copy = self.remote(slab, slab, held.cast_sent.at[0], held.cast_came.at[0], first)
        copy.wait_send()
        copy.wait_recv()

    def climb(self, held):
        last = self.levels - 1

        def place(way, step):
            return step if way else last - step

        def onward(way):
            target = self.z + 1 if way else self.z - 1
            return (target * 2 + self.core, self.mp)

        def backward(way):
            target = self.z - 1 if way else self.z + 1
            return (target * 2 + self.core, self.mp)

        def hop(way, device):
            return self.remote(
                held.sums.at[way],
                held.hop.at[way],
                held.hop_sent.at[way],
                held.hop_came.at[way],
                device,
            )

        def cast(way, device):
            slot = held.fin.at[way]
            return self.remote(
                slot, slot, held.cast_sent.at[way], held.cast_came.at[way], device
            )

        for step in range(last + 1):
            for way in (0, 1):

                @pl.when(self.z == place(way, step))
                def _(way=way, step=step):
                    if step > 0:
                        hop(way, backward(way)).wait_recv()
                        total = held.sums[way].astype(F32) + held.hop[way].astype(F32)
                        held.sums[way] = total.astype(BF16)
                    if step < last:
                        hop(way, onward(way)).start()
                    else:
                        self.mix(held, way)

            yield 2
        for step in range(last, -1, -1):
            for way in (0, 1):

                @pl.when(self.z == place(way, step))
                def _(way=way, step=step):
                    if step == last:
                        self.mixed(held, way)
                    else:
                        hop(way, onward(way)).wait_send()
                        cast(way, onward(way)).wait_recv()
                    if step > 0:
                        cast(way, backward(way)).start()

            if step > 0:
                yield 2
        for way in (0, 1):

            @pl.when(self.z != place(way, 0))
            def _(way=way):
                cast(way, backward(way)).wait_send()


    def launch(self, task, delay=0):
        self.background.append([task, delay])

    def advance(self):
        for entry in list(self.background):
            entry[1] -= 1
            if entry[1] > 0:
                continue
            pause = next(entry[0], self)
            if pause is self:
                self.background.remove(entry)
            else:
                entry[1] = pause or 1

    def run(self):
        loads = []
        for link, given in zip(self.links, self.given.chains, strict=True):
            loads.append(
                pltpu.make_async_copy(given.pixels, link.pixels, link.loads.at[0])
            )
            loads.append(pltpu.make_async_copy(given.edges, link.edges, link.loads.at[1]))
        for load in loads:
            load.start()
        self.barrier()
        for tensor in (TENSOR_Q1, TENSOR_S1, TENSOR_E1, TENSOR_SC, TENSOR_Q2):
            self.weight_start(tensor)
        for chain, link in zip(self.chains, self.links, strict=True):
            self.clear(chain, link)
        for load in loads:
            load.wait()
        parts = [
            (chain, link, link, place)
            for place, (chain, link) in enumerate(zip(self.chains, self.links, strict=True))
        ]
        tasks = [self.chain(*part) for part in parts]

        def start(tensor):
            return lambda: self.weight_start(tensor)

        def lift(tensor, steps=(0, 1, 2)):
            return lambda: self.weight_lift(tensor, steps)

        def hand(tensor):
            return lambda: self.weight_pass(tensor)

        def grad(tensor, part=0):
            places = [place for place, unit in enumerate(self.units) if unit.tensor == tensor]
            return lambda: self.launch(self.unit_gradient(places[part]), part)

        def bypass(index):
            chain, link, given, _ = parts[index]
            return lambda: self.launch(self.bypass(chain, link, given.pixels))

        def cotangent(index):
            chain, link, _, _ = parts[index]
            return lambda: self.lay_cotangent(chain, link)

        def bypass_back(index):
            return lambda: self.launch(self.bypass_back(self.links[index]))

        events = {
            1: (
                lift(TENSOR_S1),
                lift(TENSOR_E1),
                lift(TENSOR_SC),
                lift(TENSOR_Q2),
                cotangent(0),
                cotangent(1),
            ),
            2: (bypass(0), start(TENSOR_S2), start(TENSOR_E2), hand(TENSOR_S1)),
            3: (lift(TENSOR_S2, (0, 1)),),
            4: (bypass(1), hand(TENSOR_E1), hand(TENSOR_SC)),
            5: (lift(TENSOR_S2, (2,)),),
            6: (hand(TENSOR_Q2),),
            7: (lift(TENSOR_E2),),
            8: (hand(TENSOR_S2),),
            10: (hand(TENSOR_E2),),
            14: (grad(TENSOR_E2),),
            17: (grad(TENSOR_S2, 0),),
            18: (grad(TENSOR_S2, 1),),
            19: (grad(TENSOR_S2, 2), grad(TENSOR_Q2)),
            20: (grad(TENSOR_E1), grad(TENSOR_SC, 0)),
            21: (bypass_back(0), grad(TENSOR_SC, 1)),
            23: (
                bypass_back(1),
                grad(TENSOR_S1, 0),
                grad(TENSOR_S1, 1),
                grad(TENSOR_S1, 2),
            ),
        }
        slot = 0
        while tasks:
            slot += 1
            rounds = (0, 2) if slot in (24, 25) else (1, 1)
            for place, task in enumerate(list(tasks)):
                if next(task, self) is self:
                    tasks.remove(task)
                if place == 1:
                    for event in events.get(slot, ()):
                        event()
                for _ in range(rounds[place]):
                    self.advance()
        self.launch(self.unit_gradient(len(self.units) - 1))
        self.advance()
        first, second = self.links
        mids, wides = self.rows.mids, self.rows.wides
        self.result[mids : mids + 8, : self.mid] = first.gm[...] + second.gm[...]
        self.result[wides : wides + 8, :] = first.gw[...] + second.gw[...]
        leaving = pltpu.make_async_copy(self.result, self.made.rows, self.result_sem.at[0])
        leaving.start()
        while self.background:
            self.advance()
        leaving.wait()


class Rows:
    def __init__(self, chains, wide, inner):
        self.total = sum(chain.rows for chain in chains)
        self.start = [0]
        for chain in chains:
            self.start.append(self.start[-1] + chain.rows)
        self.mids = 3 * self.total
        self.wides = self.mids + 8
        self.shape = (self.wides + 8, wide)
        self.inner = inner

    def plane(self, place, plane):
        first = (1 + plane // 2) * self.total + self.start[place]
        column = plane % 2 * self.inner
        return first, slice(column, column + self.inner)


def classes(units):
    shapes = []
    counts = []
    places = []
    for unit in units:
        key = (unit.ways, unit.taps, unit.piece, unit.width)
        if key not in shapes:
            shapes.append(key)
            counts.append(0)
        index = shapes.index(key)
        places.append((index, counts[index]))
        counts[index] += 1
    return shapes, counts, places


def kernel_text(trees, chains, weights, units, sizes, *refs):
    given_tree, made_tree, scratch_tree = trees
    given_size = given_tree.num_leaves
    made_size = made_tree.num_leaves
    given = jax.tree.unflatten(given_tree, refs[:given_size])
    made = jax.tree.unflatten(made_tree, refs[given_size : given_size + made_size])
    scratch = jax.tree.unflatten(scratch_tree, refs[given_size + made_size :])
    given = {**given, **dict(chains=[bag(value) for value in given["chains"]])}
    scratch = dict(
        chains=[bag(value) for value in scratch["chains"]],
        weights=[bag(value) for value in scratch["weights"]],
        units=[bag(value) for value in scratch["units"]],
        rows=scratch["rows"],
        rows_out=scratch["rows_out"],
    )
    Body(bag(given), bag(made), bag(scratch), chains, weights, units, sizes).run()


def finish_text(chains, weights, units, sizes, *refs):
    mid, wide, inner, mpn = sizes
    count = len(weights)
    take = iter(refs)
    shapes, _, places = classes(units)
    layout = Rows(chains, wide, inner)
    pieces = [next(take) for _ in shapes]
    rows_in = next(take)
    outs = [next(take) for _ in range(count)]
    groups = [(next(take), next(take)) for _ in range(3)]
    mid_outs = [next(take) for _ in range(8)]
    wide_outs = [next(take) for _ in range(6)]
    near = [next(take) for _ in shapes]
    rows = next(take)
    wided = [next(take) for _ in range(count)]
    woven, came, gone, weave = next(take), next(take), next(take), next(take)
    arrivals = []
    for index, (which, place) in enumerate(places):
        copy = pltpu.make_async_copy(
            pieces[which].at[place], near[which].at[place], came.at[index]
        )
        copy.start()
        arrivals.append(copy)
    last = pltpu.make_async_copy(rows_in, rows, came.at[len(units)])
    last.start()
    leaving = []
    for index, unit in enumerate(units):
        arrivals[index].wait()
        which, place = places[index]
        width, piece = unit.width, unit.piece
        stride = weights[unit.tensor].width
        for core in range(2):
            for way in range(unit.ways):
                first = core * (unit.block // 2) + way * piece
                for source in range(mpn):
                    column = source * stride + unit.first_column
                    for tap in range(unit.taps):
                        wided[unit.tensor][
                            unit.first_tap + tap,
                            first : first + piece,
                            column : column + width,
                        ] = near[which][place, core, way, source, tap].astype(F32)
        if index + 1 == len(units) or units[index + 1].tensor != unit.tensor:
            whole = unit.tensor
            copy = pltpu.make_async_copy(wided[whole], outs[whole], gone.at[whole])
            copy.start()
            leaving.append(copy)
    last.wait()
    for row, out in enumerate(mid_outs):
        out[...] = rows[layout.mids + row, :mid]
    for row, out in enumerate(wide_outs):
        out[...] = rows[layout.wides + row, :]
    for place, chain in enumerate(chains):
        for segment in chain.segments:
            out, back = groups[segment.group]
            side = segment.side
            if segment.inside:
                for i in range(side):
                    for j in range(side):
                        offset = segment.start + i * segment.down + j * segment.right
                        first = layout.start[place] + offset
                        out[i, j] = rows[first : first + segment.images, :]
                        for plane in range(4):
                            first, columns = layout.plane(place, plane)
                            first += offset
                            back[2 * i + plane // 2, 2 * j + plane % 2] = rows[
                                first : first + segment.images, columns
                            ]
                continue
            for image in range(segment.images):
                for i in range(side):
                    offset = segment.start + image * side * side + i * side
                    first = layout.start[place] + offset
                    out[image, i] = rows[first : first + side, :]
                    for plane in range(4):
                        first, columns = layout.plane(place, plane)
                        first += offset
                        for lane in range(inner // LANE):
                            column = columns.start + lane * LANE
                            woven[
                                lane,
                                image,
                                2 * i + plane // 2,
                                pl.ds(plane % 2, side, stride=2),
                                :,
                            ] = rows[first : first + side, column : column + LANE]
            for lane in range(inner // LANE):
                copy = pltpu.make_async_copy(
                    woven.at[lane],
                    back.at[:, :, :, pl.ds(lane * LANE, LANE)],
                    weave.at[lane],
                )
                copy.start()
                leaving.append(copy)
    for copy in leaving:
        copy.wait()


def padded_rows(values, size):
    extra = size - values.shape[-2]
    if extra == 0:
        return values
    widths = [(0, 0)] * (values.ndim - 2) + [(0, extra), (0, 0)]
    return jnp.pad(values, widths)


def planes_of(segment, images):
    side = segment.side
    channels = images.shape[3]
    values = segment.pixel_first(images)
    if segment.inside:
        split = values.reshape(side, 2, side, 2, segment.images, channels)
        split = split.transpose(1, 3, 0, 2, 4, 5)
    else:
        split = values.reshape(segment.images, side, 2, side, 2, channels)
        split = split.transpose(2, 4, 0, 1, 3, 5)
    return padded_rows(split.reshape(4, segment.real, channels), segment.size)


def edge_masks(chain):
    masks = np.zeros((len(chain.segments), 4, chain.padded, LANE), np.float32)
    for place, segment in enumerate(chain.segments):
        index = np.arange(segment.real)
        down = index // segment.down % segment.side
        right = index // segment.right % segment.side
        start = GUARD + segment.start
        last = segment.side - 1
        for which, inside in enumerate((down > 0, down < last, right > 0, right < last)):
            masks[place, which, start : start + segment.real] = inside[:, None]
    return jnp.asarray(masks)


def fused_device(dpn, mpn, *args):
    images, widths, gates, cotangents = args[0:3], args[3], args[4:7], args[7:10]
    q1, s1, e1, sc, q2, s2, e2 = (args[index] for index in (10, 13, 16, 19, 22, 25, 28))
    mids = [args[index] for index in (11, 12, 14, 15, 23, 24, 26, 27)]
    wides = [args[index] for index in (17, 18, 20, 21, 29, 30)]
    mid = q1.shape[0]
    wide = wides[0].shape[0]
    inner = images[0].shape[3]
    shapes = [(values.shape[0], values.shape[1]) for values in images]
    chains = [Chain((2, 0), shapes, dpn), Chain((1,), shapes, dpn)]
    weights = weight_table(mid, wide, inner)
    units = unit_table(weights)
    sizes = (mid, wide, inner, dpn, mpn)
    vmem = pl.BlockSpec(memory_space=VMEM)
    smem = pl.BlockSpec(memory_space=pltpu.SMEM)
    anywhere = pl.BlockSpec(memory_space=pl.ANY)
    hbm = pl.BlockSpec(memory_space=pltpu.HBM)

    def by_tap(spatial):
        return spatial.transpose(1, 2, 0, 3).reshape(9, mid, mpn * mid)

    def rows_of(chain, build):
        return jnp.concatenate([build(s) for s in chain.segments], axis=-2)

    given = dict(
        chains=[
            dict(
                pixels=rows_of(chain, lambda s: planes_of(s, images[s.group])),
                edges=edge_masks(chain),
            )
            for chain in chains
        ],
        mids=mids,
        wides=wides,
        widths=widths,
        gates=list(gates),
        cotangents=[
            s.pixel_first(cotangents[s.group])
            for s in sorted(
                (s for chain in chains for s in chain.segments), key=lambda s: s.group
            )
        ],
        weights=[q1[None], by_tap(s1), e1[None], sc[None], q2[None], by_tap(s2), e2[None]],
    )
    given_specs = dict(
        chains=[dict(pixels=anywhere, edges=anywhere) for _ in chains],
        mids=[vmem] * len(mids),
        wides=[vmem] * len(wides),
        widths=smem,
        gates=[smem] * 3,
        cotangents=[vmem] * 3,
        weights=[anywhere] * WEIGHTS,
    )
    shape = jax.ShapeDtypeStruct
    layout = Rows(chains, wide, inner)
    unit_shapes, unit_counts, _ = classes(units)
    made = dict(
        rows=shape(layout.shape, F32),
        units=[
            shape((count, 2, ways, mpn, *rest), BF16)
            for count, (ways, *rest) in zip(unit_counts, unit_shapes, strict=True)
        ],
    )
    made_specs = dict(rows=anywhere, units=[anywhere] * len(unit_shapes))
    scratch = dict(
        chains=[chain_scratch(chain, mid, wide, inner, dpn, mpn) for chain in chains],
        weights=[weight_scratch(weight, mpn) for weight in weights],
        units=[unit_scratch(unit, mpn) for unit in units],
        rows=VMEM(layout.shape, F32),
        rows_out=DMA((1,)),
    )
    trees = tuple(jax.tree.structure(tree) for tree in (given_specs, made_specs, scratch))
    results = pl.pallas_call(
        functools.partial(kernel_text, trees, chains, weights, units, sizes),
        out_shape=jax.tree.leaves(made),
        in_specs=jax.tree.leaves(given_specs),
        out_specs=jax.tree.leaves(made_specs),
        scratch_shapes=jax.tree.leaves(scratch),
        compiler_params=pltpu.CompilerParams(
            collective_id=0, has_side_effects=True, vmem_limit_bytes=62 * 2**20
        ),
        name="bottlenecks",
    )(*jax.tree.leaves(given))
    got = bag(jax.tree.unflatten(trees[1], results))

    final_shapes = [shape((w.taps, w.block, mpn * w.width), F32) for w in weights]
    segments = sorted((s for chain in chains for s in chain.segments), key=lambda s: s.group)

    def laid(s, side, channels):
        if s.inside:
            return shape((side, side, s.images, channels), F32)
        return shape((s.images, side, side, channels), F32)

    group_shapes = []
    for s in segments:
        group_shapes += [laid(s, s.side, wide), laid(s, 2 * s.side, inner)]
    woven = [laid(s, 2 * s.side, inner) for s in segments if not s.inside]
    vector_shapes = [shape((mid,), F32)] * 8 + [shape((wide,), F32)] * 6
    final = pl.pallas_call(
        functools.partial(finish_text, chains, weights, units, (mid, wide, inner, mpn)),
        out_shape=final_shapes + group_shapes + vector_shapes,
        in_specs=[hbm] * (len(unit_shapes) + 1),
        out_specs=[hbm] * WEIGHTS
        + [spec for s in segments for spec in (vmem, vmem if s.inside else hbm)]
        + [vmem] * len(vector_shapes),
        scratch_shapes=[VMEM(value.shape, BF16) for value in made["units"]]
        + [VMEM(layout.shape, F32)]
        + [VMEM(value.shape, F32) for value in final_shapes]
        + [VMEM((inner // LANE, *woven[0].shape[:3], LANE), F32)]
        + [DMA((len(units) + 1,)), DMA((WEIGHTS,)), DMA((inner // LANE,))],
        compiler_params=pltpu.CompilerParams(vmem_limit_bytes=62 * 2**20),
        name="finish",
    )(*got.units, got.rows)
    tensors = final[:WEIGHTS]
    grads = [value[0] for value in tensors]
    for place in (TENSOR_S1, TENSOR_S2):
        split = tensors[place].reshape(3, 3, mid, mpn * mid)
        grads[place] = split.transpose(2, 0, 1, 3)
    laid_out = final[WEIGHTS : WEIGHTS + 6]
    outputs = [s.image_first(laid_out[2 * s.group]) for s in segments]
    input_grads = [s.image_first(laid_out[2 * s.group + 1]) for s in segments]
    gm = final[WEIGHTS + 6 : WEIGHTS + 14]
    gw = final[WEIGHTS + 14 :]
    return (
        *outputs,
        *input_grads,
        grads[TENSOR_Q1],
        gm[0],
        gm[1],
        grads[TENSOR_S1],
        gm[2],
        gm[3],
        grads[TENSOR_E1],
        gw[0],
        gw[1],
        grads[TENSOR_SC],
        gw[2],
        gw[3],
        grads[TENSOR_Q2],
        gm[4],
        gm[5],
        grads[TENSOR_S2],
        gm[6],
        gm[7],
        grads[TENSOR_E2],
        gw[4],
        gw[5],
    )


def fits_kernel(mesh, args):
    mid = args[10].shape[0]
    inner = args[0].shape[3]
    wide = args[17].shape[0]
    return (
        mesh.shape["mp"] == 4
        and mesh.shape["dp"] == 8
        and mid == LANE
        and inner % LANE == 0
        and wide == 2 * inner
    )


def per_device(mesh, *args):
    if fits_kernel(mesh, args):
        return fused_device(mesh.shape["dp"], mesh.shape["mp"], *args)
    return on_device(*args)


def solution(mesh):
    in_specs = (
        P("dp", None, None, "mp"),
        P("dp", None, None, "mp"),
        P("dp", None, None, "mp"),
        P(),
        P("dp"),
        P("dp"),
        P("dp"),
        P("dp", None, None, "mp"),
        P("dp", None, None, "mp"),
        P("dp", None, None, "mp"),
        P("mp", None),
        P("mp"),
        P("mp"),
        P("mp", None, None, None),
        P("mp"),
        P("mp"),
        P("mp", None),
        P("mp"),
        P("mp"),
        P("mp", None),
        P("mp"),
        P("mp"),
        P("mp", None),
        P("mp"),
        P("mp"),
        P("mp", None, None, None),
        P("mp"),
        P("mp"),
        P("mp", None),
        P("mp"),
        P("mp"),
    )
    out_specs = (
        P("dp", None, None, "mp"),
        P("dp", None, None, "mp"),
        P("dp", None, None, "mp"),
        P("dp", None, None, "mp"),
        P("dp", None, None, "mp"),
        P("dp", None, None, "mp"),
        P("mp", None),
        P("mp"),
        P("mp"),
        P("mp", None, None, None),
        P("mp"),
        P("mp"),
        P("mp", None),
        P("mp"),
        P("mp"),
        P("mp", None),
        P("mp"),
        P("mp"),
        P("mp", None),
        P("mp"),
        P("mp"),
        P("mp", None, None, None),
        P("mp"),
        P("mp"),
        P("mp", None),
        P("mp"),
        P("mp"),
    )
    return jax.shard_map(
        functools.partial(per_device, mesh),
        mesh=mesh,
        in_specs=in_specs,
        out_specs=out_specs,
        check_vma=False,
    )
```
